256 devices in a mesh: tm: 8 (over y, z_hi), blk: 32 (over z_lo, x, core).
Axes of the slice: x: 4, y: 4, z: 8 (z_hi: 2, z_lo: 4; z = z_hi * 4 + z_lo), core: 2. Of those that a mesh axis runs over, the one named last changes fastest.
Arguments:
- frames_x: bfloat16 [512, 64, 2048], P('tm', 'blk'), may hold values from -6 to 6
- bc_weight: bfloat16 [2048, 256], replicated, may hold values from -0.125 to 0.125
- decay_codes: int32 [512, 64, 32], P('tm', 'blk'), may hold values from 32 to 32768
- decay_rates: float32 [32], replicated, may hold values from 0.025 to 2
- skip_gain: float32 [32], replicated, may hold values from 0.5 to 1.5
- queries: bfloat16 [512, 64, 2048], P('tm', 'blk')
- keys: bfloat16 [512, 64, 2048], P('tm', 'blk')
- values: bfloat16 [512, 64, 2048], P('tm', 'blk'), may hold values from -6 to 6
- cotangent: bfloat16 [512, 64, 2048], P('tm', 'blk'), may hold values from -6 to 6
Outputs:
- grad_x: bfloat16 [512, 64, 2048], P('tm', 'blk')
- grad_q: bfloat16 [512, 64, 2048], P('tm', 'blk')
- grad_k: bfloat16 [512, 64, 2048], P('tm', 'blk')
- grad_v: bfloat16 [512, 64, 2048], P('tm', 'blk')
- grad_bc: float32 [2048, 256], P(('tm', 'blk'))
The draws below stay inside these ranges and needn't reach their ends.
All inputs are finite; a program needn't handle non-finite values.
Results may differ from the reference program's by a relative error of at most 0.025.
Values may be sent and summed in bfloat16 or wider, within the bound.
No kernel may reach another device: no remote copies, remote signals or barrier semaphores. Data moves between devices by JAX's collectives and lax.ppermute only.
A program may use at most 192 MiB of HBM per device.

```python
import jax
import jax.numpy as jnp
from jax import lax

HEADS = 32
HEAD = 64
STATE = 128
WIN = 64
FR_DEV = 64
BL_DEV = 2
D = 2048
ROLLOUT_FRAMES = 512
SPATIAL_BLOCKS = 64
TOKENS = 32768


def draw_decay_codes(key, part):
    baseline_sample = jax.random.randint(jax.random.fold_in(key, 11), (ROLLOUT_FRAMES, SPATIAL_BLOCKS, HEADS), 32, 64)
    frame_idx = jnp.arange(ROLLOUT_FRAMES)[:, None]
    block_idx = jnp.arange(SPATIAL_BLOCKS)[None, :]
    multiplier = 1 + (frame_idx // FR_DEV + block_idx // BL_DEV) % 2
    spike_frames = jax.random.randint(jax.random.fold_in(key, 12), (3, SPATIAL_BLOCKS), 0, ROLLOUT_FRAMES)
    spike_consumed = jax.random.randint(jax.random.fold_in(key, 13), (3, SPATIAL_BLOCKS), 0, 2)
    spike_consumed = jnp.concatenate([jnp.ones((1, SPATIAL_BLOCKS), jnp.int32), spike_consumed[1:]], axis=0)
    spike_reached = jnp.any((jnp.arange(ROLLOUT_FRAMES)[None, :, None] == spike_frames[:, None, :]) & (spike_consumed[:, None, :] > 0), axis=0)
    category_labels = jnp.where(spike_reached[:, :, None], 32768, baseline_sample * multiplier[:, :, None])
    return category_labels.astype(jnp.int32)


def draw_decay_rates(key, part):
    level = jax.random.uniform(jax.random.fold_in(key, 31), (HEADS,), jnp.float32)
    picker = jax.random.uniform(jax.random.fold_in(key, 32), (HEADS,), jnp.float32)
    share = 0.5
    slow_rate = 0.025 * jnp.exp(level * jnp.log(2.0))
    fast_rate = jnp.exp(level * jnp.log(2.0))
    return jnp.where(picker < share, fast_rate, slow_rate).astype(jnp.float32)


def draw_queries(key, part):
    result = jnp.clip(jax.random.normal(jax.random.fold_in(key, 43), (ROLLOUT_FRAMES, SPATIAL_BLOCKS, D), jnp.float32), -6.0, 6.0)
    return result.astype(jnp.bfloat16)


def draw_keys(key, part):
    result = jnp.clip(jax.random.normal(jax.random.fold_in(key, 44), (ROLLOUT_FRAMES, SPATIAL_BLOCKS, D), jnp.float32), -6.0, 6.0)
    return result.astype(jnp.bfloat16)


def level_of(key, shape, shards, smallest, top_value):
    gain, own = 1.0, jax.random.fold_in(key, 6)
    for dim, shards_of in shards:
        steps = jnp.exp(jax.random.uniform(jax.random.fold_in(own, dim), (shards_of,), jnp.float32, smallest / len(shards), top_value / len(shards)))
        gain = gain * jnp.repeat(steps, shape[dim] // shards_of).reshape([-1 if axis == dim else 1 for axis in range(len(shape))])
    return gain


def scatter_about(key, shape, scale, limit, shards=(), dtype=jnp.bfloat16):
    values = jax.random.normal(key, shape, jnp.float32) * scale
    if len(shards) > 0:
        values = level_of(key, shape, shards, -0.22, 0.18) * values
    return jnp.clip(values, min=-limit, max=limit).astype(dtype)


def setup_inputs(seed: int = 0) -> dict:
    key_of = jax.random.split(jax.random.key(seed), 10)
    return {
        "frames_x": scatter_about(key_of[0], (ROLLOUT_FRAMES, SPATIAL_BLOCKS, D), 1.0, 6.0, ((0, 8), (1, 32))),
        "bc_weight": scatter_about(key_of[1], (D, 2 * STATE), D ** -0.5, 0.125),
        "decay_codes": draw_decay_codes(jax.random.fold_in(key_of[9], 71), 0),
        "decay_rates": draw_decay_rates(jax.random.fold_in(key_of[9], 71), 0),
        "skip_gain": jnp.clip(1.0 + 0.1 * jax.random.normal(key_of[4], (HEADS,), jnp.float32), 0.5, 1.5),
        "queries": draw_queries(jax.random.fold_in(key_of[9], 71), 0),
        "keys": draw_keys(jax.random.fold_in(key_of[9], 71), 0),
        "values": scatter_about(key_of[7], (ROLLOUT_FRAMES, SPATIAL_BLOCKS, D), 1.0, 6.0, ((0, 8), (1, 32))),
        "cotangent": scatter_about(key_of[8], (ROLLOUT_FRAMES, SPATIAL_BLOCKS, D), 1.0, 6.0, ((0, 8), (1, 32))),
    }


INJECT = 0.015625
CODE_UNIT = 4096.0
SCALE = 0.125
EXACT = lax.Precision.HIGHEST


def scan_sequence(x_seq, g_seq, bc_seq, log_decay):
    frame_count = x_seq.shape[0]
    group_count = frame_count // WIN
    x_parts = x_seq.astype(jnp.float32).reshape(group_count, WIN, HEADS, HEAD)
    g_parts = g_seq.astype(jnp.float32).reshape(group_count, WIN, HEADS, HEAD)
    bc_parts = bc_seq.astype(jnp.float32).reshape(group_count, WIN, 2 * STATE)
    b_rows = bc_parts[:, :, :STATE]
    c_rows = bc_parts[:, :, STATE:]
    cumulative = jnp.cumsum(log_decay.reshape(group_count, WIN, HEADS), axis=1)
    log_total = cumulative[:, -1]
    log_gap = cumulative[:, None, :, :] - cumulative[:, :, None, :]
    positions = jnp.arange(WIN)
    forward_mask = (positions[:, None] <= positions[None, :])[None, :, :, None]
    decay_mat = jnp.where(forward_mask, jnp.exp(jnp.where(forward_mask, log_gap, 0.0)), 0.0)
    inner_xg = jnp.einsum('kthp,kshp->ktsh', x_parts, g_parts, precision=EXACT)
    mixing = INJECT * jnp.sum(decay_mat * inner_xg, axis=3)
    grad_b_local = jnp.einsum('kts,ksn->ktn', mixing, c_rows, precision=EXACT)
    grad_c_local = jnp.einsum('kts,ktn->ksn', mixing, b_rows, precision=EXACT)
    kernel = jnp.einsum('ktn,ksn->kts', b_rows, c_rows, precision=EXACT)
    grad_x_local = INJECT * jnp.einsum('ktsh,kshp->kthp', decay_mat * kernel[:, :, :, None], g_parts, precision=EXACT)
    to_end = jnp.exp(log_total[:, None, :] - cumulative)
    growth = jnp.exp(cumulative)
    summary = INJECT * jnp.einsum('kth,kthp,ktn->khpn', to_end, x_parts, b_rows, precision=EXACT)
    adjoint = jnp.einsum('kth,kthp,ktn->khpn', growth, g_parts, c_rows, precision=EXACT)
    total_decay = jnp.exp(log_total)
    empty_state = jnp.zeros((HEADS, HEAD, STATE), jnp.float32)

    def advance(running, element):
        return element[0][:, None, None] * running + element[1], running

    ignored, carried = lax.scan(advance, empty_state, (total_decay, summary))
    ignored_back, incoming = lax.scan(advance, empty_state, (total_decay, adjoint), reverse=True)
    grad_c = grad_c_local + jnp.einsum('kth,kthp,khpn->ktn', growth, g_parts, carried, precision=EXACT)
    grad_x = grad_x_local + INJECT * jnp.einsum('kth,khpn,ktn->kthp', to_end, incoming, b_rows, precision=EXACT)
    grad_b = grad_b_local + INJECT * jnp.einsum('kth,kthp,khpn->ktn', to_end, x_parts, incoming, precision=EXACT)
    return grad_x.reshape(frame_count, HEADS * HEAD), jnp.concatenate([grad_b, grad_c], axis=2).reshape(frame_count, 2 * STATE)


def window_attention(q_seq, k_seq, v_seq, g_seq):
    frame_count = q_seq.shape[0]
    group_count = frame_count // WIN

    def split_heads(array):
        return array.astype(jnp.float32).reshape(group_count, WIN, HEADS, HEAD)

    def paired(array):
        previous = jnp.concatenate([jnp.zeros_like(array[:1]), array[:-1]], axis=0)
        return jnp.concatenate([previous, array], axis=1)

    q_parts = split_heads(q_seq)
    g_parts = split_heads(g_seq)
    key_pairs = paired(split_heads(k_seq))
    value_pairs = paired(split_heads(v_seq))
    query_pos = jnp.arange(WIN)[:, None]
    key_pos = jnp.arange(2 * WIN)[None, :]
    in_window = (key_pos >= query_pos) & (key_pos <= query_pos + WIN)
    key_exists = (jnp.arange(group_count) > 0)[:, None, None] | (key_pos >= WIN)[None]
    allowed = (in_window[None] & key_exists)[:, None]
    scores = jnp.einsum('kthp,kjhp->khtj', q_parts, key_pairs, precision=EXACT) * SCALE
    masked = jnp.where(allowed, scores, -jnp.inf)
    row_max = jnp.max(masked, axis=-1)
    log_norm = row_max + jnp.log(jnp.sum(jnp.exp(masked - row_max[..., None]), axis=-1))
    probability = jnp.where(allowed, jnp.exp(scores - log_norm[..., None]), 0.0)
    weights = lax.optimization_barrier(probability.astype(jnp.bfloat16)).astype(jnp.float32)
    attended = jnp.einsum('khtj,kjhp->kthp', weights, value_pairs, precision=EXACT)
    delta_row = jnp.sum(g_parts * attended, axis=-1)
    grad_v_pairs = jnp.einsum('khtj,kthp->kjhp', weights, g_parts, precision=EXACT)
    value_inner = jnp.einsum('kthp,kjhp->khtj', g_parts, value_pairs, precision=EXACT)
    score_cot = probability * (value_inner - jnp.transpose(delta_row, (0, 2, 1))[..., None]) * SCALE
    score_cot = lax.optimization_barrier(score_cot.astype(jnp.bfloat16)).astype(jnp.float32)
    grad_q = jnp.einsum('khtj,kjhp->kthp', score_cot, key_pairs, precision=EXACT)
    grad_k_pairs = jnp.einsum('khtj,kthp->kjhp', score_cot, q_parts, precision=EXACT)

    def folded(array):
        later = jnp.concatenate([array[1:, :WIN], jnp.zeros_like(array[:1, :WIN])], axis=0)
        return (array[:, WIN:] + later).reshape(frame_count, HEADS * HEAD).astype(jnp.bfloat16)

    return grad_q.reshape(frame_count, HEADS * HEAD).astype(jnp.bfloat16), folded(grad_k_pairs), folded(grad_v_pairs)


def by_block(array):
    return jnp.swapaxes(array, 0, 1)


def scan_entry(arrays):
    return scan_sequence(arrays[0], arrays[1], arrays[2], arrays[3])


def attention_entry(arrays):
    return window_attention(arrays[0], arrays[1], arrays[2], arrays[3])


def reference(frames_x, bc_weight, decay_codes, decay_rates, skip_gain, queries, keys, values, cotangent):
    model_width = HEADS * HEAD
    flat_x = frames_x.reshape(ROLLOUT_FRAMES * SPATIAL_BLOCKS, model_width)
    bc_rows = jnp.dot(flat_x, bc_weight, preferred_element_type=jnp.float32).astype(jnp.bfloat16)
    bc_rows = bc_rows.reshape(ROLLOUT_FRAMES, SPATIAL_BLOCKS, 2 * STATE)
    log_decay = -decay_rates * decay_codes.astype(jnp.float32) / CODE_UNIT
    scan_grad_x, scan_grad_bc = lax.map(scan_entry, (by_block(frames_x), by_block(cotangent), by_block(bc_rows), by_block(log_decay)))
    bc_cot = by_block(scan_grad_bc).astype(jnp.bfloat16)
    flat_cot = bc_cot.reshape(ROLLOUT_FRAMES * SPATIAL_BLOCKS, 2 * STATE)
    back_proj = lax.dot_general(flat_cot, bc_weight, (((1,), (1,)), ((), ())), preferred_element_type=jnp.float32)
    skip_term = (cotangent.astype(jnp.float32).reshape(ROLLOUT_FRAMES, SPATIAL_BLOCKS, HEADS, HEAD) * skip_gain[:, None]).reshape(ROLLOUT_FRAMES * SPATIAL_BLOCKS, model_width)
    scan_part = by_block(scan_grad_x).reshape(ROLLOUT_FRAMES * SPATIAL_BLOCKS, model_width)
    grad_x = (scan_part + skip_term + back_proj).astype(jnp.bfloat16).reshape(ROLLOUT_FRAMES, SPATIAL_BLOCKS, model_width)
    grad_bc = lax.dot_general(flat_x, flat_cot, (((0,), (0,)), ((), ())), preferred_element_type=jnp.float32) / TOKENS
    grad_q, grad_k, grad_v = lax.map(attention_entry, (by_block(queries), by_block(keys), by_block(values), by_block(cotangent)))
    return grad_x, by_block(grad_q), by_block(grad_k), by_block(grad_v), grad_bc
```

```python
import functools

import jax
import jax.numpy as jnp
from jax import lax
from jax.experimental import pallas as pl
from jax.experimental.pallas import tpu as pltpu
from jax.sharding import Mesh, PartitionSpec as P

HEAD = 64
LANES = 128
INJECT = 0.015625
CODE_UNIT = 4096.0
SCALE = 0.125
LOW = -1e30
BF = jnp.bfloat16
F32 = jnp.float32
TM = ("y", "zh")
VM = pl.BlockSpec(memory_space=pltpu.VMEM)
SM = pl.BlockSpec(memory_space=pltpu.SMEM)


def call(body, outs, scalars, arrays, scratch=()):
    return pl.pallas_call(
        body,
        out_shape=[jax.ShapeDtypeStruct(s, d) for s, d in outs],
        in_specs=[SM] * len(scalars) + [VM] * len(arrays),
        out_specs=[VM] * len(outs),
        scratch_shapes=list(scratch),
        compiler_params=pltpu.CompilerParams(vmem_limit_bytes=48 * 1024 * 1024),
    )(*scalars, *arrays)


def nn(a, b):
    return lax.dot_general(a, b, (((1,), (0,)), ((), ())), preferred_element_type=F32)


def nt(a, b):
    return lax.dot_general(a, b, (((1,), (1,)), ((), ())), preferred_element_type=F32)


def tn(a, b):
    return lax.dot_general(a, b, (((0,), (0,)), ((), ())), preferred_element_type=F32)


def iota(shape, dim):
    return lax.broadcasted_iota(jnp.int32, shape, dim)


def one(cond):
    return jnp.where(cond, 1.0, 0.0).astype(BF)


def halves(value, scale=1.0):
    low = jnp.where(iota((1, LANES), 1) < HEAD, scale, 0.0).astype(BF)
    high = jnp.where(iota((1, LANES), 1) < HEAD, 0.0, scale).astype(BF)
    return jnp.concatenate([value * low, value * high], axis=0)


def side(value):
    n = value.shape[0] // 2
    return jnp.concatenate([value[:n], value[n:]], axis=1)


def pack_body(at, x, g, codes, own, out):
    z = at[0]
    rows, width = x.shape
    n = rows // 2
    row, col = iota((n, rows), 0), iota((n, rows), 1)
    keep, give = one(col == 2 * row + z), one(col == 2 * row + 1 - z)
    for pick, ref in ((keep, own), (give, out)):
        ref[:, :width] = nn(pick, x[...]).astype(BF)
        ref[:, width : 2 * width] = nn(pick, g[...]).astype(BF)
        ref[:, 2 * width :] = nn(pick, codes[...]).astype(BF)


def summary_body(
    at, own, got, w, rate, xs, gs, bc, sums, sums_t, scaled_x, scaled_g, leave, m1, m2, m3
):
    z, y = at[0], at[1]
    n = own.shape[0]
    rows = 2 * n
    width = xs.shape[1]
    mine = pl.multiple_of(z * n, n)
    other = pl.multiple_of((1 - z) * n, n)
    for src, start in ((own, mine), (got, other)):
        xs[pl.ds(start, n), :] = src[:, :width]
        gs[pl.ds(start, n), :] = src[:, width : 2 * width]
    first = jnp.where(z == 0, own[:, 2 * width :].astype(F32), got[:, 2 * width :].astype(F32))
    second = jnp.where(z == 0, got[:, 2 * width :].astype(F32), own[:, 2 * width :].astype(F32))
    codes = jnp.concatenate([first, second], axis=0).astype(BF)
    hi, lo = codes[:, :LANES], codes[:, LANES:]
    row, col = iota((rows, rows), 0), iota((rows, rows), 1)
    lower, upper = one(col <= row), one(row <= col)
    total = nn(lower, hi) * 256.0 + nn(lower, lo)
    sums[...] = total
    sums_t[...] = tn(hi, upper) * 256.0 + tn(lo, upper)
    whole = total.astype(jnp.int32)
    spread = one(iota((LANES, width), 1) // HEAD == iota((LANES, width), 0))
    wide = jnp.zeros((rows, width), F32)
    lasts = []
    for shift in (16, 8, 0):
        piece = ((whole >> shift) & 255).astype(F32).astype(BF)
        part = nn(piece, spread)
        lasts.append(part[rows - 1 :, :])
        wide = wide * 256.0 + part
    last = wide[rows - 1 :, :]
    slope = rate[...] * (-1.0 / CODE_UNIT)
    to_end = jnp.exp((last - wide) * slope)
    growth = jnp.exp(wide * slope)
    bc_rows = nn(xs[...], w[...]).astype(BF)
    bc[...] = bc_rows
    gone = xs[...].astype(F32) * to_end
    sx = gone.astype(BF)
    sg = (gs[...].astype(F32) * growth).astype(BF)
    scaled_x[...] = sx
    scaled_g[...] = sg
    leave[...] = to_end
    state = (tn(bc_rows[:, :LANES], sx) * INJECT).astype(BF)
    back = tn(bc_rows[:, LANES:], sg).astype(BF)
    tail = jnp.concatenate(lasts + [jnp.zeros((13, width), F32)], axis=0).astype(BF)
    for shift, ref in ((1, m1), (2, m2), (3, m3)):
        later = y + shift < 4

        @pl.when(later)
        def _():
            ref[:LANES, :] = state

        @pl.when(jnp.logical_not(later))
        def _():
            ref[:LANES, :] = back

        ref[LANES:, :] = tail


def inner_body(rate, xs, gs, bc, sums, sums_t, gx, gb, gc, x_t):
    rows, width = xs.shape
    row, col = iota((rows, rows), 0), iota((rows, rows), 1)
    ahead = row <= col
    b_rows, c_rows = bc[:, :LANES], bc[:, LANES:]
    kernel = nt(b_rows, c_rows) * INJECT
    mixing = jnp.zeros((rows, rows), F32)
    for p in range(width // LANES):
        at = slice(p * LANES, (p + 1) * LANES)
        x_pair, g_pair = xs[:, at], gs[:, at]
        both = nt(halves(x_pair), g_pair)
        parts = []
        for k in (0, 1):
            h = 2 * p + k
            gap = sums_t[h : h + 1, :] - sums[:, h : h + 1]
            decay = jnp.exp(jnp.where(ahead, gap * (rate[h] * (-1.0 / CODE_UNIT)), LOW))
            mixing = mixing + decay * both[k * rows : (k + 1) * rows]
            parts.append((decay * kernel).astype(BF))
        gx[:, at] = nn(jnp.concatenate(parts, axis=1), halves(g_pair))
        x_t[at, :] = x_pair.astype(F32).T.astype(BF)
    mixed = (mixing * INJECT).astype(BF)
    gb[...] = nn(mixed, c_rows)
    gc[...] = tn(mixed, b_rows)


def carry_body(
    at, order, m1, m2, m3, rate, gain, w, gs, bc, scaled_x, scaled_g, leave, gx, gb, gc, x_t,
    keep, give, partial,
):
    z, y = at[0], at[1]
    n = keep.shape[0]
    slope = rate[...] * (-1.0 / CODE_UNIT)

    def fade(ref):
        v = ref[LANES : LANES + 16, :].astype(F32)
        return ((v[0:1] * 256.0 + v[1:2]) * 256.0 + v[2:3]) * slope

    l1, l2, l3 = fade(m1), fade(m2), fade(m3)
    s1, s2, s3 = (m[:LANES, :].astype(F32) for m in (m1, m2, m3))

    def use(cond, log):
        return jnp.where(cond, jnp.exp(log), 0.0)

    zero = jnp.zeros_like(l1)
    state = use(y >= 1, zero) * s1 + use(y >= 2, l1) * s2 + use(y >= 3, l1 + l2) * s3
    back = use(y < 3, zero) * s3 + use(y < 2, l3) * s2 + use(y < 1, l3 + l2) * s1
    state, back = state.astype(BF), back.astype(BF)
    b_cot = gb[...] + nt(scaled_x[...], back) * INJECT
    c_cot = gc[...] + nt(scaled_g[...], state)
    cot = jnp.concatenate([b_cot, c_cot], axis=1).astype(BF)
    out = gx[...] + leave[...] * (nn(bc[:, :LANES], back) * INJECT)
    out = out + gs[...].astype(F32) * gain[...] + nt(cot, w[...])

    @pl.when(z == 0)
    def _():
        keep[...] = out[:n].astype(BF)
        give[...] = out[n:].astype(BF)

    @pl.when(z == 1)
    def _():
        keep[...] = out[n:].astype(BF)
        give[...] = out[:n].astype(BF)

    grad = nn(x_t[...], cot) * order
    for index in range(partial.shape[0]):
        partial[index] = grad[8 * index : 8 * index + 8]


def softened(k_pair, v_pair, q_pair, g_pair, seen):
    rows = q_pair.shape[0]
    score = nt(halves(k_pair, SCALE), q_pair)
    inner = nt(halves(v_pair), g_pair)
    result = []
    for k in (0, 1):
        s = jnp.where(seen, score[k * rows : (k + 1) * rows], LOW)
        result.append((s, inner[k * rows : (k + 1) * rows]))
    return result


def row_sums(s, d):
    top = jnp.max(s, axis=0, keepdims=True)
    e = jnp.exp(s - top)
    norm = jnp.sum(e, axis=0, keepdims=True)
    return e, top, norm, jnp.sum(e * d, axis=0, keepdims=True) / norm


def merged(log_a, delta_a, log_b, delta_b):
    top = jnp.maximum(log_a, log_b)
    a, b = jnp.exp(log_a - top), jnp.exp(log_b - top)
    norm = a + b
    return top + jnp.log(norm), (a * delta_a + b * delta_b) / norm


def seen_mask(rows, cross):
    key, query = iota((rows, rows), 0), iota((rows, rows), 1)
    order = key >= query if cross else key <= query
    return jnp.logical_and(order, (key & 1) == (query & 1))


def stats_body(q, k, v, g, stats):
    rows, width = q.shape
    heads = width // HEAD
    seen = seen_mask(rows, False)
    for p in range(width // LANES):
        at = slice(p * LANES, (p + 1) * LANES)
        for j, (s, d) in enumerate(softened(k[:, at], v[:, at], q[:, at], g[:, at], seen)):
            e, top, norm, delta = row_sums(s, d)
            stats[2 * p + j : 2 * p + j + 1, :] = top + jnp.log(norm)
            stats[heads + 2 * p + j : heads + 2 * p + j + 1, :] = delta


def products(ps, ds, q_pair, k_pair, g_pair):
    p_side = jnp.concatenate(ps, axis=1)
    d_side = jnp.concatenate(ds, axis=1)
    grad_v = nn(p_side, halves(g_pair))
    grad_k = nn(d_side, halves(q_pair, SCALE))
    grad_q = tn(jnp.concatenate(ds, axis=0), halves(k_pair, SCALE))
    return grad_q, grad_k, grad_v


def cross_body(q, g, theirs, k, v, stats, gq, gk, gv):
    rows, width = q.shape
    heads = width // HEAD
    seen = seen_mask(rows, True)
    for p in range(width // LANES):
        at = slice(p * LANES, (p + 1) * LANES)
        q_pair, k_pair, g_pair = q[:, at], k[:, at], g[:, at]
        ps, ds = [], []
        for j, (s, d) in enumerate(softened(k_pair, v[:, at], q_pair, g_pair, seen)):
            h = 2 * p + j
            e, top, norm, delta = row_sums(s, d)
            log_here = top + jnp.log(norm)
            stats[h : h + 1, :] = log_here
            stats[heads + h : heads + h + 1, :] = delta
            log_norm, delta = merged(
                log_here, delta, theirs[h : h + 1, :], theirs[heads + h : heads + h + 1, :]
            )
            prob = e * jnp.exp(top - log_norm)
            ps.append(prob.astype(BF))
            ds.append((prob * (d - delta)).astype(BF))
        a, b, c = products(ps, ds, q_pair, k_pair, g_pair)
        gq[:, at] = a.astype(BF)
        gk[:, at] = b
        gv[:, at] = c


def own_body(at_ref, q, k, v, g, ours, theirs, gk_far, gv_far, gq, gk, gv):
    rows, width = q.shape
    heads = width // HEAD
    seen = seen_mask(rows, False)
    begins = at_ref[2] == 0
    for p in range(width // LANES):
        at = slice(p * LANES, (p + 1) * LANES)
        q_pair, k_pair, g_pair = q[:, at], k[:, at], g[:, at]
        ps, ds = [], []
        for j, (s, d) in enumerate(softened(k_pair, v[:, at], q_pair, g_pair, seen)):
            h = 2 * p + j
            far = jnp.where(begins, LOW, theirs[h : h + 1, :])
            log_norm, delta = merged(
                ours[h : h + 1, :],
                ours[heads + h : heads + h + 1, :],
                far,
                theirs[heads + h : heads + h + 1, :],
            )
            prob = jnp.exp(s - log_norm)
            ps.append(prob.astype(BF))
            ds.append((prob * (d - delta)).astype(BF))
        a, b, c = products(ps, ds, q_pair, k_pair, g_pair)
        gq[:, at] = a
        gk[:, at] = (b + gk_far[:, at]).astype(BF)
        gv[:, at] = (c + gv_far[:, at]).astype(BF)


def after(value, *others):
    return lax.optimization_barrier((value,) + others)[0]


def local(
    frames_x, bc_weight, decay_codes, decay_rates, skip_gain, queries, keys, values, cotangent
):
    length, blocks, width = frames_x.shape
    rows = length * blocks
    heads = decay_rates.shape[0]
    tm = lax.axis_size(TM)
    ny, nx, nz = lax.axis_size("y"), lax.axis_size("x"), lax.axis_size(("zh", "zl"))
    y, z, core = lax.axis_index("y"), lax.axis_index("zh"), lax.axis_index("c")
    at = jnp.stack([z, y, 2 * y + z]).astype(jnp.int32)
    flip = [(0, 1), (1, 0)]
    to_prev = [(i, i - 1) for i in range(1, tm)]
    to_next = [(i - 1, i) for i in range(1, tm)]

    def flat(a):
        return a.reshape(rows, width)

    x2, g2, q2, k2, v2 = (flat(a) for a in (frames_x, cotangent, queries, keys, values))
    codes = decay_codes.reshape(rows, heads)
    pad = ((0, 0), (0, LANES - heads))
    codes = jnp.concatenate([jnp.pad(codes >> 8, pad), jnp.pad(codes & 255, pad)], axis=1)
    codes = codes.astype(BF)
    rate_wide = jnp.repeat(decay_rates, HEAD)[None]
    gain_wide = jnp.repeat(skip_gain, HEAD)[None]

    msg = (rows // 2, 2 * width + 2 * LANES)
    own, out = call(pack_body, [(msg, BF)] * 2, [at], [x2, g2, codes])
    got = lax.ppermute(out, "zh", flip)

    stats_own = call(stats_body, [((2 * heads, rows), F32)], [], [q2, k2, v2, g2])[0]
    stats_next = lax.ppermute(stats_own, TM, to_prev)
    q_next = lax.ppermute(after(q2, got), TM, to_prev)
    g_next = lax.ppermute(after(g2, got), TM, to_prev)

    wide = (rows, width)
    state = (LANES + 16, width)
    square = (rows, LANES)
    xs, gs, bc, sums, sums_t, scaled_x, scaled_g, leave, m1, m2, m3 = call(
        summary_body,
        [(wide, BF), (wide, BF), ((rows, 2 * LANES), BF), (square, F32), (square, F32)]
        + [(wide, BF), (wide, BF), (wide, F32)]
        + [(state, BF)] * 3,
        [at],
        [own, got, bc_weight, rate_wide],
    )
    m1, m2, m3 = (
        lax.ppermute(m, "y", [(i, (i + s) % ny) for i in range(ny)])
        for s, m in ((1, m1), (2, m2), (3, m3))
    )
    gx, gb, gc, x_t = call(
        inner_body,
        [(wide, F32), (square, F32), (square, F32), ((width, rows), BF)],
        [decay_rates],
        [xs, gs, bc, sums, sums_t],
    )
    order = 1.0 / (rows * tm * lax.axis_size(("zl", "x", "c")))
    keep, give, partial = call(
        lambda at_ref, *refs: carry_body(at_ref, order, *refs),
        [((rows // 2, width), BF)] * 2 + [((width // 8, 8, 2 * LANES), F32)],
        [at],
        [m1, m2, m3, rate_wide, gain_wide, bc_weight, gs, bc, scaled_x, scaled_g, leave, gx, gb, gc, x_t],
    )
    gx_far = lax.ppermute(give, "zh", flip)

    partial = partial.reshape(ny, nz, nx, 2, 8, 2 * LANES)
    mine = lax.dynamic_index_in_dim(partial, core, 3, False)
    yours = lax.dynamic_index_in_dim(partial, 1 - core, 3, False)
    chip = mine + lax.ppermute(yours, "c", flip)
    chip = jnp.swapaxes(chip, 1, 2).reshape(ny * nx, nz * 8, 2 * LANES).astype(BF)
    spread = lax.all_to_all(chip, ("y", "x"), 0, 0, tiled=True)
    plane = jnp.sum(spread.astype(F32), axis=0).astype(BF).reshape(nz, 8, 2 * LANES)
    spread = lax.all_to_all(plane, ("zh", "zl"), 0, 0, tiled=True)
    grad_bc = jnp.sum(spread.astype(F32), axis=0)

    stats_far, gq_out, gk_far, gv_far = call(
        cross_body,
        [((2 * heads, rows), F32), (wide, BF), (wide, F32), (wide, F32)],
        [],
        [q_next, g_next, stats_next, k2, v2],
    )
    stats_prev = lax.ppermute(stats_far, TM, to_next)
    gq_prev = lax.ppermute(gq_out, TM, to_next)
    gq, gk, gv = call(
        own_body,
        [(wide, F32), (wide, BF), (wide, BF)],
        [at],
        [q2, k2, v2, g2, stats_own, stats_prev, gk_far, gv_far],
    )
    gq = (gq + gq_prev.astype(F32)).astype(BF)
    shape = (length, blocks, width)
    grad_x = jnp.stack(
        [jnp.where(z == 0, keep, gx_far), jnp.where(z == 0, gx_far, keep)], axis=1
    )
    return grad_x, gq.reshape(shape), gk.reshape(shape), gv.reshape(shape), grad_bc


def solution(mesh):
    tm, blk = mesh.devices.shape
    fine = Mesh(
        mesh.devices.reshape(tm // 2, 2, blk // 8, 4, 2), TM + ("zl", "x", "c")
    )
    tokens = P(TM, ("zl", "x", "c"), None)
    return jax.shard_map(
        local,
        mesh=fine,
        in_specs=(tokens, P(), tokens, P(), P(), tokens, tokens, tokens, tokens),
        out_specs=(tokens,) * 4 + (P(TM + ("zl", "x", "c"), None),),
        check_vma=False,
    )
```

```python
import functools

import jax
import jax.numpy as jnp
from jax import lax
from jax.experimental import pallas as pl
from jax.experimental.pallas import tpu as pltpu
from jax.sharding import Mesh, PartitionSpec as P

HEAD = 64
LANES = 128
INJECT = 0.015625
CODE_UNIT = 4096.0
SCALE = 0.125
VMEM_BYTES = 60 * 1024 * 1024
LOW = -1e30
BF = jnp.bfloat16
F32 = jnp.float32
TM = ("y", "zh")
VM = pl.BlockSpec(memory_space=pltpu.VMEM)
SM = pl.BlockSpec(memory_space=pltpu.SMEM)


def call(body, outs, scalars, arrays, first=()):
    used = len(scalars) + len(arrays)

    def run(*refs):
        body(*refs[:used], *refs[used + len(first) :])

    return pl.pallas_call(
        run,
        out_shape=[jax.ShapeDtypeStruct(s, d) for s, d in outs],
        in_specs=[SM] * len(scalars) + [pl.BlockSpec(a.shape, lambda *_, n=a.ndim: (0,) * n) for a in arrays]
        + [pl.BlockSpec(memory_space=pl.ANY)] * len(first),
        out_specs=[pl.BlockSpec(s, lambda *_, n=len(s): (0,) * n) for s, d in outs],
        grid=(1,),
        cost_estimate=pl.CostEstimate(flops=1, bytes_accessed=1, transcendentals=0),
        compiler_params=pltpu.CompilerParams(vmem_limit_bytes=VMEM_BYTES),
    )(*scalars, *arrays, *first)


def nn(a, b):
    return lax.dot_general(a, b, (((1,), (0,)), ((), ())), preferred_element_type=F32)


def nt(a, b):
    return lax.dot_general(a, b, (((1,), (1,)), ((), ())), preferred_element_type=F32)


def tn(a, b):
    return lax.dot_general(a, b, (((0,), (0,)), ((), ())), preferred_element_type=F32)


def iota(shape, dim):
    return lax.broadcasted_iota(jnp.int32, shape, dim)


def one(cond):
    return jnp.where(cond, 1.0, 0.0).astype(BF)


def halves(value, scale=1.0):
    low = jnp.where(iota((1, LANES), 1) < HEAD, scale, 0.0).astype(BF)
    high = jnp.where(iota((1, LANES), 1) < HEAD, 0.0, scale).astype(BF)
    return jnp.concatenate([value * low, value * high], axis=0)


def side(value):
    n = value.shape[0] // 2
    return jnp.concatenate([value[:n], value[n:]], axis=1)


def join_body(q, g, stats, out):
    rows = q.shape[0]
    out[:rows, :] = q[...]
    out[rows : 2 * rows, :] = g[...]
    out[2 * rows :, :] = jnp.zeros((16, q.shape[1]), BF)
    rest = stats[...]
    groups = stats.shape[0] // 16
    for piece in range(3):
        part = rest.astype(BF)
        rest = rest - part.astype(F32)
        for k in range(groups):
            lane = (piece * groups + k) * LANES
            out[2 * rows :, lane : lane + LANES] = part[16 * k : 16 * k + 16]


def joined_stats(qg, rows, groups):
    found = []
    for k in range(groups):
        lanes = [(piece * groups + k) * LANES for piece in range(3)]
        a, b, c = (qg[2 * rows :, lane : lane + LANES].astype(F32) for lane in lanes)
        found.append(a + (b + c))
    return jnp.concatenate(found, axis=0)


def pack_body(at, x, g, codes, own, out):
    z = at[0]
    rows, width = x.shape
    n = rows // 2
    row, col = iota((n, rows), 0), iota((n, rows), 1)
    keep, give = one(col == 2 * row + z), one(col == 2 * row + 1 - z)
    here = z == 0
    for pick, code, ref in (
        (keep, jnp.where(here, codes[0], codes[1]), own),
        (give, jnp.where(here, codes[1], codes[0]), out),
    ):
        ref[:, :width] = nn(pick, x[...]).astype(BF)
        ref[:, width : 2 * width] = nn(pick, g[...]).astype(BF)
        both = jnp.concatenate([code >> 8, code & 255], axis=0).astype(F32)
        ref[:, 2 * width :] = jnp.concatenate([both, jnp.zeros_like(both)], axis=1).astype(BF)


def summary_body(
    at, own, got, w, rate, xs, gs, bc, sums, sums_t, scaled_x, scaled_g, leave, m1, m2, m3
):
    z, y = at[0], at[1]
    n = own.shape[0]
    rows = 2 * n
    width = xs.shape[1]
    mine = pl.multiple_of(z * n, n)
    other = pl.multiple_of((1 - z) * n, n)
    for src, start in ((own, mine), (got, other)):
        xs[pl.ds(start, n), :] = src[:, :width]
        gs[pl.ds(start, n), :] = src[:, width : 2 * width]
    mine_codes, other_codes = own[:, 2 * width :].astype(F32), got[:, 2 * width :].astype(F32)
    early = jnp.where(z == 0, mine_codes, other_codes)
    late = jnp.where(z == 0, other_codes, mine_codes)
    codes = jnp.concatenate([early[:, :n], late[:, :n]], axis=1)
    heads = codes.shape[0] // 2
    blank = jnp.zeros((LANES - heads, rows), F32)
    hi = jnp.concatenate([codes[:heads], blank], axis=0).astype(BF)
    lo = jnp.concatenate([codes[heads:], blank], axis=0).astype(BF)
    row, col = iota((rows, rows), 0), iota((rows, rows), 1)
    lower, upper = one(col <= row), one(row <= col)
    total = nt(lower, hi) * 256.0 + nt(lower, lo)
    sums[...] = total
    sums_t[...] = nn(hi, upper) * 256.0 + nn(lo, upper)
    whole = total.astype(jnp.int32)
    spread = one(iota((LANES, width), 1) // HEAD == iota((LANES, width), 0))
    wide = jnp.zeros((rows, width), F32)
    lasts = []
    for shift in (16, 8, 0):
        piece = ((whole >> shift) & 255).astype(F32).astype(BF)
        part = nn(piece, spread)
        lasts.append(part[rows - 1 :, :])
        wide = wide * 256.0 + part
    last = wide[rows - 1 :, :]
    slope = rate[...] * (-1.0 / CODE_UNIT)
    to_end = jnp.exp((last - wide) * slope)
    growth = jnp.exp(wide * slope)
    bc_rows = nn(xs[...], w[...]).astype(BF)
    bc[...] = bc_rows
    gone = xs[...].astype(F32) * to_end
    sx = gone.astype(BF)
    sg = (gs[...].astype(F32) * growth).astype(BF)
    scaled_x[...] = sx
    scaled_g[...] = sg
    leave[...] = to_end
    state = (tn(bc_rows[:, :LANES], sx) * INJECT).astype(BF)
    back = tn(bc_rows[:, LANES:], sg).astype(BF)
    tail = jnp.concatenate(lasts + [jnp.zeros((13, width), F32)], axis=0).astype(BF)
    for shift, ref in ((1, m1), (2, m2), (3, m3)):
        later = y + shift < 4

        @pl.when(later)
        def _():
            ref[:LANES, :] = state

        @pl.when(jnp.logical_not(later))
        def _():
            ref[:LANES, :] = back

        ref[LANES:, :] = tail


def inner_body(rate, xs, gs, bc, sums, sums_t, gx, gb, gc, x_t):
    rows, width = xs.shape
    row, col = iota((rows, rows), 0), iota((rows, rows), 1)
    ahead = row <= col
    b_rows, c_rows = bc[:, :LANES], bc[:, LANES:]
    kernel = nt(b_rows, c_rows) * INJECT
    mixing = jnp.zeros((rows, rows), F32)
    for p in range(width // LANES):
        at = slice(p * LANES, (p + 1) * LANES)
        x_pair, g_pair = xs[:, at], gs[:, at]
        both = nt(halves(x_pair), g_pair)
        parts = []
        for k in (0, 1):
            h = 2 * p + k
            gap = sums_t[h : h + 1, :] - sums[:, h : h + 1]
            decay = jnp.exp(jnp.where(ahead, gap * (rate[h] * (-1.0 / CODE_UNIT)), LOW))
            mixing = mixing + decay * both[k * rows : (k + 1) * rows]
            parts.append((decay * kernel).astype(BF))
        gx[:, at] = nn(jnp.concatenate(parts, axis=1), halves(g_pair))
        x_t[at, :] = x_pair.astype(F32).T.astype(BF)
    mixed = (mixing * INJECT).astype(BF)
    gb[...] = nn(mixed, c_rows)
    gc[...] = tn(mixed, b_rows)


def carry_body(
    at, order, m1, m2, m3, rate, gain, w, gs, bc, scaled_x, scaled_g, leave, gx, gb, gc, x_t,
    keep, give, mine, yours,
):
    z, y, core = at[0], at[1], at[3]
    n = keep.shape[0]
    slope = rate[...] * (-1.0 / CODE_UNIT)

    def fade(ref):
        v = ref[LANES : LANES + 16, :].astype(F32)
        return ((v[0:1] * 256.0 + v[1:2]) * 256.0 + v[2:3]) * slope

    l1, l2, l3 = fade(m1), fade(m2), fade(m3)
    s1, s2, s3 = (m[:LANES, :].astype(F32) for m in (m1, m2, m3))

    def use(cond, log):
        return jnp.where(cond, jnp.exp(log), 0.0)

    zero = jnp.zeros_like(l1)
    state = use(y >= 1, zero) * s1 + use(y >= 2, l1) * s2 + use(y >= 3, l1 + l2) * s3
    back = use(y < 3, zero) * s3 + use(y < 2, l3) * s2 + use(y < 1, l3 + l2) * s1
    state, back = state.astype(BF), back.astype(BF)
    b_cot = gb[...] + nt(scaled_x[...], back) * INJECT
    c_cot = gc[...] + nt(scaled_g[...], state)
    cot = jnp.concatenate([b_cot, c_cot], axis=1).astype(BF)
    out = gx[...] + leave[...] * (nn(bc[:, :LANES], back) * INJECT)
    out = out + gs[...].astype(F32) * gain[...] + nt(cot, w[...])

    @pl.when(z == 0)
    def _():
        keep[...] = out[:n].astype(BF)
        give[...] = out[n:].astype(BF)

    @pl.when(z == 1)
    def _():
        keep[...] = out[n:].astype(BF)
        give[...] = out[:n].astype(BF)

    grad = nn(x_t[...], cot) * order
    for side in (0, 1):

        @pl.when(core == side)
        def _():
            for index in range(mine.shape[0]):
                xy, nz = index // 8, index % 8
                block = (((xy // 4) * 8 + nz) * 4 + xy % 4) * 2
                for ref, c in ((mine, side), (yours, 1 - side)):
                    start = 8 * (block + c)
                    ref[index] = grad[start : start + 8]


def softened(k_pair, v_pair, q_pair, g_pair, seen):
    rows = q_pair.shape[0]
    score = nt(halves(k_pair, SCALE), q_pair)
    inner = nt(halves(v_pair), g_pair)
    result = []
    for k in (0, 1):
        s = jnp.where(seen, score[k * rows : (k + 1) * rows], LOW)
        result.append((s, inner[k * rows : (k + 1) * rows]))
    return result


def row_sums(s, d):
    top = jnp.max(s, axis=0, keepdims=True)
    e = jnp.exp(s - top)
    norm = jnp.sum(e, axis=0, keepdims=True)
    return e, top, norm, jnp.sum(e * d, axis=0, keepdims=True) / norm


def merged(log_a, delta_a, log_b, delta_b):
    top = jnp.maximum(log_a, log_b)
    a, b = jnp.exp(log_a - top), jnp.exp(log_b - top)
    norm = a + b
    return top + jnp.log(norm), (a * delta_a + b * delta_b) / norm


def seen_mask(rows, cross):
    key, query = iota((rows, rows), 0), iota((rows, rows), 1)
    order = key >= query if cross else key <= query
    return jnp.logical_and(order, (key & 1) == (query & 1))


def stats_body(q, k, v, g, stats):
    rows, width = q.shape
    heads = width // HEAD
    seen = seen_mask(rows, False)
    for p in range(width // LANES):
        at = slice(p * LANES, (p + 1) * LANES)
        for j, (s, d) in enumerate(softened(k[:, at], v[:, at], q[:, at], g[:, at], seen)):
            e, top, norm, delta = row_sums(s, d)
            stats[2 * p + j : 2 * p + j + 1, :] = top + jnp.log(norm)
            stats[heads + 2 * p + j : heads + 2 * p + j + 1, :] = delta


def products(ps, ds, q_pair, k_pair, g_pair):
    p_side = jnp.concatenate(ps, axis=1)
    d_side = jnp.concatenate(ds, axis=1)
    grad_v = nn(p_side, halves(g_pair))
    grad_k = nn(d_side, halves(q_pair, SCALE))
    grad_q = tn(jnp.concatenate(ds, axis=0), halves(k_pair, SCALE))
    return grad_q, grad_k, grad_v


def cross_body(qg, k, v, stats, gq, gk, gv):
    rows, width = k.shape
    heads = width // HEAD
    theirs = joined_stats(qg, rows, stats.shape[0] // 16)
    seen = seen_mask(rows, True)
    for p in range(width // LANES):
        at = slice(p * LANES, (p + 1) * LANES)
        q_pair, k_pair, g_pair = qg[:rows, at], k[:, at], qg[rows : 2 * rows, at]
        ps, ds = [], []
        for j, (s, d) in enumerate(softened(k_pair, v[:, at], q_pair, g_pair, seen)):
            h = 2 * p + j
            e, top, norm, delta = row_sums(s, d)
            log_here = top + jnp.log(norm)
            stats[h : h + 1, :] = log_here
            stats[heads + h : heads + h + 1, :] = delta
            log_norm, delta = merged(
                log_here, delta, theirs[h : h + 1, :], theirs[heads + h : heads + h + 1, :]
            )
            prob = e * jnp.exp(top - log_norm)
            ps.append(prob.astype(BF))
            ds.append((prob * (d - delta)).astype(BF))
        a, b, c = products(ps, ds, q_pair, k_pair, g_pair)
        gq[:, at] = a.astype(BF)
        gk[:, at] = b
        gv[:, at] = c


def own_body(at_ref, q, k, v, g, ours, theirs, gk_far, gv_far, gq, gk, gv):
    rows, width = q.shape
    heads = width // HEAD
    seen = seen_mask(rows, False)
    begins = at_ref[2] == 0
    for p in range(width // LANES):
        at = slice(p * LANES, (p + 1) * LANES)
        q_pair, k_pair, g_pair = q[:, at], k[:, at], g[:, at]
        ps, ds = [], []
        for j, (s, d) in enumerate(softened(k_pair, v[:, at], q_pair, g_pair, seen)):
            h = 2 * p + j
            far = jnp.where(begins, LOW, theirs[h : h + 1, :])
            log_norm, delta = merged(
                ours[h : h + 1, :],
                ours[heads + h : heads + h + 1, :],
                far,
                theirs[heads + h : heads + h + 1, :],
            )
            prob = jnp.exp(s - log_norm)
            ps.append(prob.astype(BF))
            ds.append((prob * (d - delta)).astype(BF))
        a, b, c = products(ps, ds, q_pair, k_pair, g_pair)
        gq[:, at] = a
        gk[:, at] = (b + gk_far[:, at]).astype(BF)
        gv[:, at] = (c + gv_far[:, at]).astype(BF)


def local(
    frames_x, bc_weight, decay_codes, decay_rates, skip_gain, queries, keys, values, cotangent
):
    length, blocks, width = frames_x.shape
    rows = length * blocks
    heads = decay_rates.shape[0]
    tm = lax.axis_size(TM)
    ny, nx, nz = lax.axis_size("y"), lax.axis_size("x"), lax.axis_size(("zh", "zl"))
    y, z, core = lax.axis_index("y"), lax.axis_index("zh"), lax.axis_index("c")
    at = jnp.stack([z, y, 2 * y + z, core]).astype(jnp.int32)
    flip = [(0, 1), (1, 0)]
    to_prev = [(i, i - 1) for i in range(1, tm)]
    to_next = [(i - 1, i) for i in range(1, tm)]

    def flat(a):
        return a.reshape(rows, width)

    x2, g2, q2, k2, v2 = (flat(a) for a in (frames_x, cotangent, queries, keys, values))
    codes = jnp.transpose(decay_codes, (1, 2, 0))
    rate_wide = jnp.repeat(decay_rates, HEAD)[None]
    gain_wide = jnp.repeat(skip_gain, HEAD)[None]

    msg = (rows // 2, 2 * width + LANES)
    own, out = call(pack_body, [(msg, BF)] * 2, [at], [x2, g2, codes])
    got = lax.ppermute(out, "zh", flip)

    stats_own = call(stats_body, [((2 * heads, rows), F32)], [], [q2, k2, v2, g2])[0]
    qg = call(join_body, [((2 * rows + 16, width), BF)], [], [q2, g2, stats_own], [got])[0]
    qg_next = lax.ppermute(qg, TM, to_prev)

    wide = (rows, width)
    state = (LANES + 16, width)
    square = (rows, LANES)
    xs, gs, bc, sums, sums_t, scaled_x, scaled_g, leave, m1, m2, m3 = call(
        summary_body,
        [(wide, BF), (wide, BF), ((rows, 2 * LANES), BF), (square, F32), (square, F32)]
        + [(wide, BF), (wide, BF), (wide, F32)]
        + [(state, BF)] * 3,
        [at],
        [own, got, bc_weight, rate_wide],
        [qg],
    )
    m1, m2, m3 = (
        lax.ppermute(m, "y", [(i, (i + s) % ny) for i in range(ny)])
        for s, m in ((1, m1), (2, m2), (3, m3))
    )
    gx, gb, gc, x_t = call(
        inner_body,
        [(wide, F32), (square, F32), (square, F32), ((width, rows), BF)],
        [decay_rates],
        [xs, gs, bc, sums, sums_t],
    )
    order = 1.0 / (rows * tm * lax.axis_size(("zl", "x", "c")))
    keep, give, mine, yours = call(
        lambda at_ref, *refs: carry_body(at_ref, order, *refs),
        [((rows // 2, width), BF)] * 2 + [((width // 16, 8, 2 * LANES), F32)] * 2,
        [at],
        [m1, m2, m3, rate_wide, gain_wide, bc_weight, gs, bc, scaled_x, scaled_g, leave, gx, gb, gc, x_t],
        [qg_next],
    )
    gx_far = lax.ppermute(give, "zh", flip)

    chip = (mine + lax.ppermute(yours, "c", flip)).astype(BF)
    chip = chip.reshape(ny * nx, nz * 8, 2 * LANES)
    spread = lax.all_to_all(chip, ("y", "x"), 0, 0, tiled=True)
    plane = jnp.sum(spread.astype(F32), axis=0).astype(BF).reshape(nz, 8, 2 * LANES)
    spread = lax.all_to_all(plane, ("zh", "zl"), 0, 0, tiled=True)
    grad_bc = jnp.sum(spread.astype(F32), axis=0)

    stats_far, gq_out, gk_far, gv_far = call(
        cross_body,
        [((2 * heads, rows), F32), (wide, BF), (wide, F32), (wide, F32)],
        [],
        [qg_next, k2, v2],
        [chip],
    )
    stats_prev = lax.ppermute(stats_far, TM, to_next)
    gq_prev = lax.ppermute(gq_out, TM, to_next)
    gq, gk, gv = call(
        own_body,
        [(wide, F32), (wide, BF), (wide, BF)],
        [at],
        [q2, k2, v2, g2, stats_own, stats_prev, gk_far, gv_far],
    )
    gq = (gq + gq_prev.astype(F32)).astype(BF)
    shape = (length, blocks, width)
    grad_x = jnp.stack(
        [jnp.where(z == 0, keep, gx_far), jnp.where(z == 0, gx_far, keep)], axis=1
    )
    return grad_x, gq.reshape(shape), gk.reshape(shape), gv.reshape(shape), grad_bc


def solution(mesh):
    tm, blk = mesh.devices.shape
    fine = Mesh(
        mesh.devices.reshape(tm // 2, 2, blk // 8, 4, 2), TM + ("zl", "x", "c")
    )
    tokens = P(TM, ("zl", "x", "c"), None)
    return jax.shard_map(
        local,
        mesh=fine,
        in_specs=(tokens, P(), tokens, P(), P(), tokens, tokens, tokens, tokens),
        out_specs=(tokens,) * 4 + (P(TM + ("zl", "x", "c"), None),),
        check_vma=False,
    )
```

```python
import functools

import jax
import jax.numpy as jnp
from jax import lax
from jax.experimental import pallas as pl
from jax.experimental.pallas import tpu as pltpu
from jax.sharding import Mesh, PartitionSpec as P

HEAD = 64
LANES = 128
INJECT = 0.015625
CODE_UNIT = 4096.0
SCALE = 0.125
VMEM_BYTES = 60 * 1024 * 1024
LOW = -1e30
BF = jnp.bfloat16
F32 = jnp.float32
TM = ("y", "zh")
SM = pl.BlockSpec(memory_space=pltpu.SMEM)


GROUP = 512


def call(body, outs, scalars, arrays, first=(), steps=1):
    used = len(scalars) + len(arrays)

    def run(*refs):
        body(*refs[:used], *refs[used + len(first) :])

    def spec(shape):
        if steps == 1:
            return pl.BlockSpec(shape, lambda i: (0,) * len(shape))
        if len(shape) == 3:
            return pl.BlockSpec((1,) + tuple(shape[1:]), lambda i: (i, 0, 0))
        return pl.BlockSpec((shape[0], shape[1] // steps), lambda i: (0, i))

    return pl.pallas_call(
        run,
        out_shape=[jax.ShapeDtypeStruct(s, d) for s, d in outs],
        in_specs=[SM] * len(scalars)
        + [spec(a.shape) for a in arrays]
        + [pl.BlockSpec(memory_space=pl.ANY)] * len(first),
        out_specs=[spec(s) for s, d in outs],
        grid=(steps,),
        cost_estimate=pl.CostEstimate(flops=1, bytes_accessed=1, transcendentals=0),
        compiler_params=pltpu.CompilerParams(vmem_limit_bytes=VMEM_BYTES),
    )(*scalars, *arrays, *first)


def held_until(value, event):
    anywhere = pl.BlockSpec(memory_space=pl.ANY)
    return pl.pallas_call(
        lambda *refs: None,
        out_shape=jax.ShapeDtypeStruct(value.shape, value.dtype),
        in_specs=[anywhere, anywhere],
        out_specs=anywhere,
        input_output_aliases={0: 0},
        cost_estimate=pl.CostEstimate(flops=1, bytes_accessed=1, transcendentals=0),
    )(value, event)


def nn(a, b):
    return lax.dot_general(a, b, (((1,), (0,)), ((), ())), preferred_element_type=F32)


def nt(a, b):
    return lax.dot_general(a, b, (((1,), (1,)), ((), ())), preferred_element_type=F32)


def tn(a, b):
    return lax.dot_general(a, b, (((0,), (0,)), ((), ())), preferred_element_type=F32)


def iota(shape, dim):
    return lax.broadcasted_iota(jnp.int32, shape, dim)


def one(cond):
    return jnp.where(cond, 1.0, 0.0).astype(BF)


def halves(value, scale=1.0):
    low = jnp.where(iota((1, LANES), 1) < HEAD, scale, 0.0).astype(BF)
    high = jnp.where(iota((1, LANES), 1) < HEAD, 0.0, scale).astype(BF)
    return jnp.concatenate([value * low, value * high], axis=0)


def side(value):
    n = value.shape[0] // 2
    return jnp.concatenate([value[:n], value[n:]], axis=1)


def join_body(q, g, stats, out):
    rows = q.shape[0]
    out[:rows, :] = q[...]
    out[rows : 2 * rows, :] = g[...]
    rest = stats[0]
    for piece in range(3):
        part = rest.astype(BF)
        rest = rest - part.astype(F32)
        out[2 * rows :, piece * LANES : (piece + 1) * LANES] = part
    out[2 * rows :, 3 * LANES :] = jnp.zeros((16, GROUP - 3 * LANES), BF)


def joined_stats(qg, rows):
    a, b, c = (
        qg[2 * rows :, piece * LANES : (piece + 1) * LANES].astype(F32) for piece in range(3)
    )
    return a + (b + c)


def pack_body(at, x, g, codes, own, out):
    z = at[0]
    rows, width = x.shape
    n = rows // 2
    row, col = iota((n, rows), 0), iota((n, rows), 1)
    keep, give = one(col == 2 * row + z), one(col == 2 * row + 1 - z)
    here = z == 0
    for pick, code, ref in (
        (keep, jnp.where(here, codes[0], codes[1]), own),
        (give, jnp.where(here, codes[1], codes[0]), out),
    ):
        ref[:, :width] = nn(pick, x[...]).astype(BF)
        ref[:, width : 2 * width] = nn(pick, g[...]).astype(BF)
        both = jnp.concatenate([code >> 8, code & 255], axis=0).astype(F32)
        ref[:, 2 * width :] = jnp.concatenate([both, jnp.zeros_like(both)], axis=1).astype(BF)


def summary_body(
    at, own, got, w, rate, xs, gs, bc, sums, sums_t, scaled_x, scaled_g, leave, m1, m2, m3
):
    z, y = at[0], at[1]
    n = own.shape[0]
    rows = 2 * n
    width = xs.shape[1]
    mine = pl.multiple_of(z * n, n)
    other = pl.multiple_of((1 - z) * n, n)
    for src, start in ((own, mine), (got, other)):
        xs[pl.ds(start, n), :] = src[:, :width]
        gs[pl.ds(start, n), :] = src[:, width : 2 * width]
    mine_codes, other_codes = own[:, 2 * width :].astype(F32), got[:, 2 * width :].astype(F32)
    early = jnp.where(z == 0, mine_codes, other_codes)
    late = jnp.where(z == 0, other_codes, mine_codes)
    codes = jnp.concatenate([early[:, :n], late[:, :n]], axis=1)
    heads = codes.shape[0] // 2
    blank = jnp.zeros((LANES - heads, rows), F32)
    hi = jnp.concatenate([codes[:heads], blank], axis=0).astype(BF)
    lo = jnp.concatenate([codes[heads:], blank], axis=0).astype(BF)
    row, col = iota((rows, rows), 0), iota((rows, rows), 1)
    lower, upper = one(col <= row), one(row <= col)
    total = nt(lower, hi) * 256.0 + nt(lower, lo)
    sums[...] = total
    sums_t[...] = nn(hi, upper) * 256.0 + nn(lo, upper)
    whole = total.astype(jnp.int32)
    spread = one(iota((LANES, width), 1) // HEAD == iota((LANES, width), 0))
    wide = jnp.zeros((rows, width), F32)
    lasts = []
    for shift in (16, 8, 0):
        piece = ((whole >> shift) & 255).astype(F32).astype(BF)
        part = nn(piece, spread)
        lasts.append(part[rows - 1 :, :])
        wide = wide * 256.0 + part
    last = wide[rows - 1 :, :]
    slope = rate[...] * (-1.0 / CODE_UNIT)
    to_end = jnp.exp((last - wide) * slope)
    growth = jnp.exp(wide * slope)
    bc_rows = nn(xs[...], w[...]).astype(BF)
    bc[...] = bc_rows
    gone = xs[...].astype(F32) * to_end
    sx = gone.astype(BF)
    sg = (gs[...].astype(F32) * growth).astype(BF)
    scaled_x[...] = sx
    scaled_g[...] = sg
    leave[...] = to_end
    state = (tn(bc_rows[:, :LANES], sx) * INJECT).astype(BF)
    back = tn(bc_rows[:, LANES:], sg).astype(BF)
    tail = jnp.concatenate(lasts + [jnp.zeros((13, width), F32)], axis=0).astype(BF)
    for shift, ref in ((1, m1), (2, m2), (3, m3)):
        later = y + shift < 4

        @pl.when(later)
        def _():
            ref[:LANES, :] = state

        @pl.when(jnp.logical_not(later))
        def _():
            ref[:LANES, :] = back

        ref[LANES:, :] = tail


def inner_body(rate, xs, gs, bc, sums, sums_t, gx, gb, gc, x_t):
    rows, width = xs.shape
    row, col = iota((rows, rows), 0), iota((rows, rows), 1)
    ahead = row <= col
    b_rows, c_rows = bc[:, :LANES], bc[:, LANES:]
    kernel = nt(b_rows, c_rows) * INJECT
    mixing = jnp.zeros((rows, rows), F32)
    for p in range(width // LANES):
        at = slice(p * LANES, (p + 1) * LANES)
        x_pair, g_pair = xs[:, at], gs[:, at]
        both = nt(halves(x_pair), g_pair)
        parts = []
        for k in (0, 1):
            h = 2 * p + k
            gap = sums_t[h : h + 1, :] - sums[:, h : h + 1]
            decay = jnp.exp(jnp.where(ahead, gap * (rate[h] * (-1.0 / CODE_UNIT)), LOW))
            mixing = mixing + decay * both[k * rows : (k + 1) * rows]
            parts.append((decay * kernel).astype(BF))
        gx[:, at] = nn(jnp.concatenate(parts, axis=1), halves(g_pair))
        x_t[at, :] = x_pair.astype(F32).T.astype(BF)
    mixed = (mixing * INJECT).astype(BF)
    gb[...] = nn(mixed, c_rows)
    gc[...] = tn(mixed, b_rows)


def carry_body(
    at, order, m1, m2, m3, rate, gain, w, gs, bc, scaled_x, scaled_g, leave, gx, gb, gc, x_t,
    keep, give, mine, yours,
):
    z, y, core = at[0], at[1], at[3]
    n = keep.shape[0]
    slope = rate[...] * (-1.0 / CODE_UNIT)

    def fade(ref):
        v = ref[LANES : LANES + 16, :].astype(F32)
        return ((v[0:1] * 256.0 + v[1:2]) * 256.0 + v[2:3]) * slope

    l1, l2, l3 = fade(m1), fade(m2), fade(m3)
    s1, s2, s3 = (m[:LANES, :].astype(F32) for m in (m1, m2, m3))

    def use(cond, log):
        return jnp.where(cond, jnp.exp(log), 0.0)

    zero = jnp.zeros_like(l1)
    state = use(y >= 1, zero) * s1 + use(y >= 2, l1) * s2 + use(y >= 3, l1 + l2) * s3
    back = use(y < 3, zero) * s3 + use(y < 2, l3) * s2 + use(y < 1, l3 + l2) * s1
    state, back = state.astype(BF), back.astype(BF)
    b_cot = gb[...] + nt(scaled_x[...], back) * INJECT
    c_cot = gc[...] + nt(scaled_g[...], state)
    cot = jnp.concatenate([b_cot, c_cot], axis=1).astype(BF)
    out = gx[...] + leave[...] * (nn(bc[:, :LANES], back) * INJECT)
    out = out + gs[...].astype(F32) * gain[...] + nt(cot, w[...])

    @pl.when(z == 0)
    def _():
        keep[...] = out[:n].astype(BF)
        give[...] = out[n:].astype(BF)

    @pl.when(z == 1)
    def _():
        keep[...] = out[n:].astype(BF)
        give[...] = out[:n].astype(BF)

    grad = nn(x_t[...], cot) * order
    grad = grad.reshape(4, 8, 4, 2, 8, 2 * LANES)
    for side in (0, 1):

        @pl.when(core == side)
        def _():
            for x in range(4):
                mine[:, x] = grad[:, :, x, side]
                yours[:, x] = grad[:, :, x, 1 - side]


def softened(k_pair, v_pair, q_pair, g_pair, seen):
    rows = q_pair.shape[0]
    score = nt(halves(k_pair, SCALE), q_pair)
    inner = nt(halves(v_pair), g_pair)
    result = []
    for k in (0, 1):
        s = jnp.where(seen, score[k * rows : (k + 1) * rows], LOW)
        result.append((s, inner[k * rows : (k + 1) * rows]))
    return result


def row_sums(s, d):
    top = jnp.max(s, axis=0, keepdims=True)
    e = jnp.exp(s - top)
    norm = jnp.sum(e, axis=0, keepdims=True)
    return e, top, norm, jnp.sum(e * d, axis=0, keepdims=True) / norm


def merged(log_a, delta_a, log_b, delta_b):
    top = jnp.maximum(log_a, log_b)
    a, b = jnp.exp(log_a - top), jnp.exp(log_b - top)
    norm = a + b
    return top + jnp.log(norm), (a * delta_a + b * delta_b) / norm


def seen_mask(rows, cross):
    key, query = iota((rows, rows), 0), iota((rows, rows), 1)
    order = key >= query if cross else key <= query
    return jnp.logical_and(order, (key & 1) == (query & 1))


def stats_body(q, k, v, g, stats):
    rows, width = q.shape
    seen = seen_mask(rows, False)
    logs, deltas = [], []
    for p in range(width // LANES):
        at = slice(p * LANES, (p + 1) * LANES)
        for s, d in softened(k[:, at], v[:, at], q[:, at], g[:, at], seen):
            e, top, norm, delta = row_sums(s, d)
            logs.append(top + jnp.log(norm))
            deltas.append(delta)
    stats[0] = jnp.concatenate(logs + deltas, axis=0)


def products(ps, ds, q_pair, k_pair, g_pair):
    p_side = jnp.concatenate(ps, axis=1)
    d_side = jnp.concatenate(ds, axis=1)
    grad_v = nn(p_side, halves(g_pair))
    grad_k = nn(d_side, halves(q_pair, SCALE))
    grad_q = tn(jnp.concatenate(ds, axis=0), halves(k_pair, SCALE))
    return grad_q, grad_k, grad_v


def cross_body(qg, k, v, stats, gq, gk, gv):
    rows, width = k.shape
    heads = width // HEAD
    theirs = joined_stats(qg, rows)
    seen = seen_mask(rows, True)
    logs, deltas = [], []
    for p in range(width // LANES):
        at = slice(p * LANES, (p + 1) * LANES)
        q_pair, k_pair, g_pair = qg[:rows, at], k[:, at], qg[rows : 2 * rows, at]
        ps, ds = [], []
        for j, (s, d) in enumerate(softened(k_pair, v[:, at], q_pair, g_pair, seen)):
            h = 2 * p + j
            e, top, norm, delta = row_sums(s, d)
            log_here = top + jnp.log(norm)
            logs.append(log_here)
            deltas.append(delta)
            log_norm, delta = merged(
                log_here, delta, theirs[h : h + 1, :], theirs[heads + h : heads + h + 1, :]
            )
            prob = e * jnp.exp(top - log_norm)
            ps.append(prob.astype(BF))
            ds.append((prob * (d - delta)).astype(BF))
        a, b, c = products(ps, ds, q_pair, k_pair, g_pair)
        gq[:, at] = a.astype(BF)
        gk[:, at] = b
        gv[:, at] = c
    stats[0] = jnp.concatenate(logs + deltas, axis=0)


def own_body(at_ref, q, k, v, g, ours, theirs, gk_far, gv_far, gq, gk, gv):
    rows, width = q.shape
    heads = width // HEAD
    seen = seen_mask(rows, False)
    begins = at_ref[2] == 0
    near, away = ours[0], theirs[0]
    for p in range(width // LANES):
        at = slice(p * LANES, (p + 1) * LANES)
        q_pair, k_pair, g_pair = q[:, at], k[:, at], g[:, at]
        ps, ds = [], []
        for j, (s, d) in enumerate(softened(k_pair, v[:, at], q_pair, g_pair, seen)):
            h = 2 * p + j
            far = jnp.where(begins, LOW, away[h : h + 1])
            log_norm, delta = merged(
                near[h : h + 1],
                near[heads + h : heads + h + 1],
                far,
                away[heads + h : heads + h + 1],
            )
            prob = jnp.exp(s - log_norm)
            ps.append(prob.astype(BF))
            ds.append((prob * (d - delta)).astype(BF))
        a, b, c = products(ps, ds, q_pair, k_pair, g_pair)
        gq[:, at] = a
        gk[:, at] = (b + gk_far[:, at]).astype(BF)
        gv[:, at] = (c + gv_far[:, at]).astype(BF)


def local(
    frames_x, bc_weight, decay_codes, decay_rates, skip_gain, queries, keys, values, cotangent
):
    length, blocks, width = frames_x.shape
    rows = length * blocks
    heads = decay_rates.shape[0]
    tm = lax.axis_size(TM)
    ny, nx, nz = lax.axis_size("y"), lax.axis_size("x"), lax.axis_size(("zh", "zl"))
    y, z, core = lax.axis_index("y"), lax.axis_index("zh"), lax.axis_index("c")
    at = jnp.stack([z, y, 2 * y + z, core]).astype(jnp.int32)
    flip = [(0, 1), (1, 0)]
    to_prev = [(i, i - 1) for i in range(1, tm)]
    to_next = [(i - 1, i) for i in range(1, tm)]

    def flat(a):
        return a.reshape(rows, width)

    x2, g2, q2, k2, v2 = (flat(a) for a in (frames_x, cotangent, queries, keys, values))
    codes = jnp.transpose(decay_codes, (1, 2, 0))
    rate_wide = jnp.repeat(decay_rates, HEAD)[None]
    gain_wide = jnp.repeat(skip_gain, HEAD)[None]

    msg = (rows // 2, 2 * width + LANES)
    own, out = call(pack_body, [(msg, BF)] * 2, [at], [x2, g2, codes])
    got = lax.ppermute(out, "zh", flip)

    steps = width // GROUP
    stats = ((steps, 2 * GROUP // HEAD, rows), F32)
    stats_own = call(stats_body, [stats], [], [q2, k2, v2, g2], steps=steps)[0]
    qg = call(join_body, [((2 * rows + 16, width), BF)], [], [q2, g2, stats_own], steps=steps)[0]
    qg = held_until(qg, got)
    qg_next = lax.ppermute(qg, TM, to_prev)

    wide = (rows, width)
    state = (LANES + 16, width)
    square = (rows, LANES)
    xs, gs, bc, sums, sums_t, scaled_x, scaled_g, leave, m1, m2, m3 = call(
        summary_body,
        [(wide, BF), (wide, BF), ((rows, 2 * LANES), BF), (square, F32), (square, F32)]
        + [(wide, BF), (wide, BF), (wide, F32)]
        + [(state, BF)] * 3,
        [at],
        [own, got, bc_weight, rate_wide],
        [qg],
    )
    m1, m2, m3 = (
        lax.ppermute(m, "y", [(i, (i + s) % ny) for i in range(ny)])
        for s, m in ((1, m1), (2, m2), (3, m3))
    )
    gx, gb, gc, x_t = call(
        inner_body,
        [(wide, F32), (square, F32), (square, F32), ((width, rows), BF)],
        [decay_rates],
        [xs, gs, bc, sums, sums_t],
    )
    order = 1.0 / (rows * tm * lax.axis_size(("zl", "x", "c")))
    keep, give, mine, yours = call(
        lambda at_ref, *refs: carry_body(at_ref, order, *refs),
        [((rows // 2, width), BF)] * 2 + [((ny, nx, nz, 8, 2 * LANES), F32)] * 2,
        [at],
        [m1, m2, m3, rate_wide, gain_wide, bc_weight, gs, bc, scaled_x, scaled_g, leave, gx, gb, gc, x_t],
        [qg_next],
    )
    gx_far = lax.ppermute(give, "zh", flip)

    chip = (mine + lax.ppermute(yours, "c", flip)).astype(BF)
    chip = chip.reshape(ny * nx, nz * 8, 2 * LANES)
    spread = lax.all_to_all(chip, ("y", "x"), 0, 0, tiled=True)
    plane = jnp.sum(spread.astype(F32), axis=0).astype(BF).reshape(nz, 8, 2 * LANES)
    spread = lax.all_to_all(plane, ("zh", "zl"), 0, 0, tiled=True)
    grad_bc = jnp.sum(spread.astype(F32), axis=0)

    stats_far, gq_out, gk_far, gv_far = call(
        cross_body,
        [stats, (wide, BF), (wide, F32), (wide, F32)],
        [],
        [qg_next, k2, v2],
        steps=steps,
    )
    stats_prev = lax.ppermute(stats_far, TM, to_next)
    gq_prev = lax.ppermute(gq_out, TM, to_next)
    gq, gk, gv = call(
        own_body,
        [(wide, F32), (wide, BF), (wide, BF)],
        [at],
        [q2, k2, v2, g2, stats_own, stats_prev, gk_far, gv_far],
        [chip],
        steps=steps,
    )
    gq = (gq + gq_prev.astype(F32)).astype(BF)
    shape = (length, blocks, width)
    grad_x = jnp.stack(
        [jnp.where(z == 0, keep, gx_far), jnp.where(z == 0, gx_far, keep)], axis=1
    )
    return grad_x, gq.reshape(shape), gk.reshape(shape), gv.reshape(shape), grad_bc


def solution(mesh):
    tm, blk = mesh.devices.shape
    fine = Mesh(
        mesh.devices.reshape(tm // 2, 2, blk // 8, 4, 2), TM + ("zl", "x", "c")
    )
    tokens = P(TM, ("zl", "x", "c"), None)
    return jax.shard_map(
        local,
        mesh=fine,
        in_specs=(tokens, P(), tokens, P(), P(), tokens, tokens, tokens, tokens),
        out_specs=(tokens,) * 4 + (P(TM + ("zl", "x", "c"), None),),
        check_vma=False,
    )
```

```python
import functools

import jax
import jax.numpy as jnp
from jax import lax
from jax.experimental import pallas as pl
from jax.experimental.pallas import tpu as pltpu
from jax.sharding import Mesh, PartitionSpec as P

HEAD = 64
LANES = 128
INJECT = 0.015625
CODE_UNIT = 4096.0
SCALE = 0.125
VMEM_BYTES = 60 * 1024 * 1024
LOW = -1e30
BF = jnp.bfloat16
F32 = jnp.float32
TM = ("y", "zh")
SM = pl.BlockSpec(memory_space=pltpu.SMEM)


GROUP = 512


def call(body, outs, scalars, arrays, first=(), steps=1):
    used = len(scalars) + len(arrays)

    def run(*refs):
        body(*refs[:used], *refs[used + len(first) :])

    def spec(shape):
        if steps == 1:
            return pl.BlockSpec(shape, lambda i: (0,) * len(shape))
        if len(shape) == 3:
            return pl.BlockSpec((1,) + tuple(shape[1:]), lambda i: (i, 0, 0))
        return pl.BlockSpec((shape[0], shape[1] // steps), lambda i: (0, i))

    return pl.pallas_call(
        run,
        out_shape=[jax.ShapeDtypeStruct(s, d) for s, d in outs],
        in_specs=[SM] * len(scalars)
        + [spec(a.shape) for a in arrays]
        + [pl.BlockSpec(memory_space=pl.ANY)] * len(first),
        out_specs=[spec(s) for s, d in outs],
        grid=(steps,),
        cost_estimate=pl.CostEstimate(flops=1, bytes_accessed=1, transcendentals=0),
        compiler_params=pltpu.CompilerParams(vmem_limit_bytes=VMEM_BYTES),
    )(*scalars, *arrays, *first)


def nn(a, b):
    return lax.dot_general(a, b, (((1,), (0,)), ((), ())), preferred_element_type=F32)


def nt(a, b):
    return lax.dot_general(a, b, (((1,), (1,)), ((), ())), preferred_element_type=F32)


def tn(a, b):
    return lax.dot_general(a, b, (((0,), (0,)), ((), ())), preferred_element_type=F32)


def iota(shape, dim):
    return lax.broadcasted_iota(jnp.int32, shape, dim)


def one(cond):
    return jnp.where(cond, 1.0, 0.0).astype(BF)


def halves(value, scale=1.0):
    low = jnp.where(iota((1, LANES), 1) < HEAD, scale, 0.0).astype(BF)
    high = jnp.where(iota((1, LANES), 1) < HEAD, 0.0, scale).astype(BF)
    return jnp.concatenate([value * low, value * high], axis=0)


def side(value):
    n = value.shape[0] // 2
    return jnp.concatenate([value[:n], value[n:]], axis=1)


def join_body(q, g, out):
    rows = q.shape[0]
    out[:rows, :] = q[...]
    out[rows:, :] = g[...]


def pack_body(at, x, g, codes, own, out):
    z = at[0]
    rows, width = x.shape
    n = rows // 2
    row, col = iota((n, rows), 0), iota((n, rows), 1)
    keep, give = one(col == 2 * row + z), one(col == 2 * row + 1 - z)
    here = z == 0
    for pick, code, ref in (
        (keep, jnp.where(here, codes[0], codes[1]), own),
        (give, jnp.where(here, codes[1], codes[0]), out),
    ):
        ref[:, :width] = nn(pick, x[...]).astype(BF)
        ref[:, width : 2 * width] = nn(pick, g[...]).astype(BF)
        both = jnp.concatenate([code >> 8, code & 255], axis=0).astype(F32)
        ref[:, 2 * width :] = jnp.concatenate([both, jnp.zeros_like(both)], axis=1).astype(BF)


def summary_body(
    at, own, got, w, rate, xs, gs, bc, sums, sums_t, scaled_x, scaled_g, leave, m1, m2, m3
):
    z, y = at[0], at[1]
    n = own.shape[0]
    rows = 2 * n
    width = xs.shape[1]
    mine = pl.multiple_of(z * n, n)
    other = pl.multiple_of((1 - z) * n, n)
    for src, start in ((own, mine), (got, other)):
        xs[pl.ds(start, n), :] = src[:, :width]
        gs[pl.ds(start, n), :] = src[:, width : 2 * width]
    mine_codes, other_codes = own[:, 2 * width :].astype(F32), got[:, 2 * width :].astype(F32)
    early = jnp.where(z == 0, mine_codes, other_codes)
    late = jnp.where(z == 0, other_codes, mine_codes)
    codes = jnp.concatenate([early[:, :n], late[:, :n]], axis=1)
    heads = codes.shape[0] // 2
    blank = jnp.zeros((LANES - heads, rows), F32)
    hi = jnp.concatenate([codes[:heads], blank], axis=0).astype(BF)
    lo = jnp.concatenate([codes[heads:], blank], axis=0).astype(BF)
    row, col = iota((rows, rows), 0), iota((rows, rows), 1)
    lower, upper = one(col <= row), one(row <= col)
    total = nt(lower, hi) * 256.0 + nt(lower, lo)
    sums[...] = total
    sums_t[...] = nn(hi, upper) * 256.0 + nn(lo, upper)
    whole = total.astype(jnp.int32)
    spread = one(iota((LANES, width), 1) // HEAD == iota((LANES, width), 0))
    wide = jnp.zeros((rows, width), F32)
    lasts = []
    for shift in (16, 8, 0):
        piece = ((whole >> shift) & 255).astype(F32).astype(BF)
        part = nn(piece, spread)
        lasts.append(part[rows - 1 :, :])
        wide = wide * 256.0 + part
    last = wide[rows - 1 :, :]
    slope = rate[...] * (-1.0 / CODE_UNIT)
    to_end = jnp.exp((last - wide) * slope)
    growth = jnp.exp(wide * slope)
    bc_rows = nn(xs[...], w[...]).astype(BF)
    bc[...] = bc_rows
    gone = xs[...].astype(F32) * to_end
    sx = gone.astype(BF)
    sg = (gs[...].astype(F32) * growth).astype(BF)
    scaled_x[...] = sx
    scaled_g[...] = sg
    leave[...] = to_end
    state = (tn(bc_rows[:, :LANES], sx) * INJECT).astype(BF)
    back = tn(bc_rows[:, LANES:], sg).astype(BF)
    tail = jnp.concatenate(lasts + [jnp.zeros((13, width), F32)], axis=0).astype(BF)
    for shift, ref in ((1, m1), (2, m2), (3, m3)):
        later = y + shift < 4

        @pl.when(later)
        def _():
            ref[:LANES, :] = state

        @pl.when(jnp.logical_not(later))
        def _():
            ref[:LANES, :] = back

        ref[LANES:, :] = tail


def inner_body(rate, xs, gs, bc, sums, sums_t, gx, gb, gc, x_t):
    rows, width = xs.shape
    row, col = iota((rows, rows), 0), iota((rows, rows), 1)
    ahead = row <= col
    b_rows, c_rows = bc[:, :LANES], bc[:, LANES:]
    kernel = nt(b_rows, c_rows) * INJECT
    mixing = jnp.zeros((rows, rows), F32)
    for p in range(width // LANES):
        at = slice(p * LANES, (p + 1) * LANES)
        x_pair, g_pair = xs[:, at], gs[:, at]
        both = nt(halves(x_pair), g_pair)
        parts = []
        for k in (0, 1):
            h = 2 * p + k
            gap = sums_t[h : h + 1, :] - sums[:, h : h + 1]
            decay = jnp.exp(jnp.where(ahead, gap * (rate[h] * (-1.0 / CODE_UNIT)), LOW))
            mixing = mixing + decay * both[k * rows : (k + 1) * rows]
            parts.append((decay * kernel).astype(BF))
        gx[:, at] = nn(jnp.concatenate(parts, axis=1), halves(g_pair))
        x_t[at, :] = x_pair.astype(F32).T.astype(BF)
    mixed = (mixing * INJECT).astype(BF)
    gb[...] = nn(mixed, c_rows)
    gc[...] = tn(mixed, b_rows)


def carry_body(
    at, order, m1, m2, m3, rate, gain, w, gs, bc, scaled_x, scaled_g, leave, gx, gb, gc, x_t,
    keep, give, mine, yours,
):
    z, y, core = at[0], at[1], at[3]
    n = keep.shape[0]
    slope = rate[...] * (-1.0 / CODE_UNIT)

    def fade(ref):
        v = ref[LANES : LANES + 16, :].astype(F32)
        return ((v[0:1] * 256.0 + v[1:2]) * 256.0 + v[2:3]) * slope

    l1, l2, l3 = fade(m1), fade(m2), fade(m3)
    s1, s2, s3 = (m[:LANES, :].astype(F32) for m in (m1, m2, m3))

    def use(cond, log):
        return jnp.where(cond, jnp.exp(log), 0.0)

    zero = jnp.zeros_like(l1)
    state = use(y >= 1, zero) * s1 + use(y >= 2, l1) * s2 + use(y >= 3, l1 + l2) * s3
    back = use(y < 3, zero) * s3 + use(y < 2, l3) * s2 + use(y < 1, l3 + l2) * s1
    state, back = state.astype(BF), back.astype(BF)
    b_cot = gb[...] + nt(scaled_x[...], back) * INJECT
    c_cot = gc[...] + nt(scaled_g[...], state)
    cot = jnp.concatenate([b_cot, c_cot], axis=1).astype(BF)
    out = gx[...] + leave[...] * (nn(bc[:, :LANES], back) * INJECT)
    out = out + gs[...].astype(F32) * gain[...] + nt(cot, w[...])

    @pl.when(z == 0)
    def _():
        keep[...] = out[:n].astype(BF)
        give[...] = out[n:].astype(BF)

    @pl.when(z == 1)
    def _():
        keep[...] = out[n:].astype(BF)
        give[...] = out[:n].astype(BF)

    grad = nn(x_t[...], cot) * order
    grad = grad.reshape(4, 8, 4, 2, 8, 2 * LANES)
    for side in (0, 1):

        @pl.when(core == side)
        def _():
            for x in range(4):
                mine[:, x] = grad[:, :, x, side]
                yours[:, x] = grad[:, :, x, 1 - side]


def unpack_body(at, keep, far, out):
    z = at[0]
    n = keep.shape[0]
    row, col = iota((2 * n, n), 0), iota((2 * n, n), 1)
    ours, theirs = one(row == 2 * col + z), one(row == 2 * col + 1 - z)
    out[...] = (nn(ours, keep[...]) + nn(theirs, far[...])).astype(BF)


def softened(k_pair, v_pair, q_pair, g_pair, seen):
    rows = q_pair.shape[0]
    score = nt(halves(k_pair, SCALE), q_pair)
    inner = nt(halves(v_pair), g_pair)
    result = []
    for k in (0, 1):
        s = jnp.where(seen, score[k * rows : (k + 1) * rows], LOW)
        result.append((s, inner[k * rows : (k + 1) * rows]))
    return result


def row_sums(s, d):
    top = jnp.max(s, axis=0, keepdims=True)
    e = jnp.exp(s - top)
    norm = jnp.sum(e, axis=0, keepdims=True)
    return e, top, norm, jnp.sum(e * d, axis=0, keepdims=True) / norm


def merged(log_a, delta_a, log_b, delta_b):
    top = jnp.maximum(log_a, log_b)
    a, b = jnp.exp(log_a - top), jnp.exp(log_b - top)
    norm = a + b
    return top + jnp.log(norm), (a * delta_a + b * delta_b) / norm


def seen_mask(rows, cross):
    key, query = iota((rows, rows), 0), iota((rows, rows), 1)
    order = key >= query if cross else key <= query
    return jnp.logical_and(order, (key & 1) == (query & 1))


def stats_body(q, k, v, g, stats):
    rows, width = q.shape
    seen = seen_mask(rows, False)
    logs, deltas = [], []
    for p in range(width // LANES):
        at = slice(p * LANES, (p + 1) * LANES)
        for s, d in softened(k[:, at], v[:, at], q[:, at], g[:, at], seen):
            e, top, norm, delta = row_sums(s, d)
            logs.append(top + jnp.log(norm))
            deltas.append(delta)
    stats[0] = jnp.concatenate(logs + deltas, axis=0)


def products(ps, ds, q_pair, k_pair, g_pair):
    p_side = jnp.concatenate(ps, axis=1)
    d_side = jnp.concatenate(ds, axis=1)
    grad_v = nn(p_side, halves(g_pair))
    grad_k = nn(d_side, halves(q_pair, SCALE))
    grad_q = tn(jnp.concatenate(ds, axis=0), halves(k_pair, SCALE))
    return grad_q, grad_k, grad_v


def cross_body(qg, before, k, v, gq, gk, gv):
    rows, width = k.shape
    heads = width // HEAD
    theirs = before[0]
    seen = seen_mask(rows, True)
    logs, deltas = [], []
    for p in range(width // LANES):
        at = slice(p * LANES, (p + 1) * LANES)
        q_pair, k_pair, g_pair = qg[:rows, at], k[:, at], qg[rows:, at]
        ps, ds = [], []
        for j, (s, d) in enumerate(softened(k_pair, v[:, at], q_pair, g_pair, seen)):
            h = 2 * p + j
            e, top, norm, delta = row_sums(s, d)
            log_here = top + jnp.log(norm)
            logs.append(log_here)
            deltas.append(delta)
            log_norm, delta = merged(
                log_here, delta, theirs[h : h + 1, :], theirs[heads + h : heads + h + 1, :]
            )
            prob = e * jnp.exp(top - log_norm)
            ps.append(prob.astype(BF))
            ds.append((prob * (d - delta)).astype(BF))
        a, b, c = products(ps, ds, q_pair, k_pair, g_pair)
        gq[:rows, at] = a.astype(BF)
        gk[:, at] = b
        gv[:, at] = c
    rest = jnp.concatenate(logs + deltas, axis=0)
    for piece in range(3):
        part = rest.astype(BF)
        rest = rest - part.astype(F32)
        gq[rows:, piece * LANES : (piece + 1) * LANES] = part
    gq[rows:, 3 * LANES :] = jnp.zeros((16, GROUP - 3 * LANES), BF)


def own_body(at_ref, q, k, v, g, ours, gq_far, gk_far, gv_far, gq, gk, gv):
    rows, width = q.shape
    heads = width // HEAD
    seen = seen_mask(rows, False)
    begins = at_ref[2] == 0
    near = ours[0]
    pieces = (gq_far[rows:, i * LANES : (i + 1) * LANES].astype(F32) for i in range(3))
    away = functools.reduce(lambda a, b: a + b, pieces)
    for p in range(width // LANES):
        at = slice(p * LANES, (p + 1) * LANES)
        q_pair, k_pair, g_pair = q[:, at], k[:, at], g[:, at]
        ps, ds = [], []
        for j, (s, d) in enumerate(softened(k_pair, v[:, at], q_pair, g_pair, seen)):
            h = 2 * p + j
            far = jnp.where(begins, LOW, away[h : h + 1])
            log_norm, delta = merged(
                near[h : h + 1],
                near[heads + h : heads + h + 1],
                far,
                away[heads + h : heads + h + 1],
            )
            prob = jnp.exp(s - log_norm)
            ps.append(prob.astype(BF))
            ds.append((prob * (d - delta)).astype(BF))
        a, b, c = products(ps, ds, q_pair, k_pair, g_pair)
        gq[:, at] = (a + gq_far[:rows, at].astype(F32)).astype(BF)
        gk[:, at] = (b + gk_far[:, at]).astype(BF)
        gv[:, at] = (c + gv_far[:, at]).astype(BF)


def local(
    frames_x, bc_weight, decay_codes, decay_rates, skip_gain, queries, keys, values, cotangent
):
    length, blocks, width = frames_x.shape
    rows = length * blocks
    heads = decay_rates.shape[0]
    tm = lax.axis_size(TM)
    ny, nx, nz = lax.axis_size("y"), lax.axis_size("x"), lax.axis_size(("zh", "zl"))
    y, z, core = lax.axis_index("y"), lax.axis_index("zh"), lax.axis_index("c")
    at = jnp.stack([z, y, 2 * y + z, core]).astype(jnp.int32)
    flip = [(0, 1), (1, 0)]
    to_prev = [(i, i - 1) for i in range(1, tm)]
    to_next = [(i - 1, i) for i in range(1, tm)]

    def flat(a):
        return a.reshape(rows, width)

    x2, g2, q2, k2, v2 = (flat(a) for a in (frames_x, cotangent, queries, keys, values))
    codes = jnp.transpose(decay_codes, (1, 2, 0))
    rate_wide = jnp.repeat(decay_rates, HEAD)[None]
    gain_wide = jnp.repeat(skip_gain, HEAD)[None]

    msg = (rows // 2, 2 * width + LANES)
    own, out = call(pack_body, [(msg, BF)] * 2, [at], [x2, g2, codes])
    got = lax.ppermute(out, "zh", flip)

    steps = width // GROUP
    stats = ((steps, 2 * GROUP // HEAD, rows), F32)
    stats_own = call(stats_body, [stats], [], [q2, k2, v2, g2], steps=steps)[0]
    stats_next = lax.ppermute(stats_own, TM, to_prev)
    qg = call(join_body, [((2 * rows, width), BF)], [], [q2, g2])[0]
    qg_next = lax.ppermute(qg, TM, to_prev)

    wide = (rows, width)
    state = (LANES + 16, width)
    square = (rows, LANES)
    xs, gs, bc, sums, sums_t, scaled_x, scaled_g, leave, m1, m2, m3 = call(
        summary_body,
        [(wide, BF), (wide, BF), ((rows, 2 * LANES), BF), (square, F32), (square, F32)]
        + [(wide, BF), (wide, BF), (wide, F32)]
        + [(state, BF)] * 3,
        [at],
        [own, got, bc_weight, rate_wide],
        [stats_own],
    )
    m1, m2, m3 = (
        lax.ppermute(m, "y", [(i, (i + s) % ny) for i in range(ny)])
        for s, m in ((1, m1), (2, m2), (3, m3))
    )
    gx, gb, gc, x_t = call(
        inner_body,
        [(wide, F32), (square, F32), (square, F32), ((width, rows), BF)],
        [decay_rates],
        [xs, gs, bc, sums, sums_t],
        [stats_next],
    )
    order = 1.0 / (rows * tm * lax.axis_size(("zl", "x", "c")))
    keep, give, mine, yours = call(
        lambda at_ref, *refs: carry_body(at_ref, order, *refs),
        [((rows // 2, width), BF)] * 2 + [((ny, nx, nz, 8, 2 * LANES), F32)] * 2,
        [at],
        [m1, m2, m3, rate_wide, gain_wide, bc_weight, gs, bc, scaled_x, scaled_g, leave, gx, gb, gc, x_t],
        [qg_next],
    )
    gx_far = lax.ppermute(give, "zh", flip)

    chip = (mine + lax.ppermute(yours, "c", flip)).astype(BF)
    chip = chip.reshape(ny * nx, nz * 8, 2 * LANES)
    spread = lax.all_to_all(chip, ("y", "x"), 0, 0, tiled=True)
    plane = jnp.sum(spread.astype(F32), axis=0).astype(BF).reshape(nz, 8, 2 * LANES)
    spread = lax.all_to_all(plane, ("zh", "zl"), 0, 0, tiled=True)
    grad_bc = jnp.sum(spread.astype(F32), axis=0)

    gq_out, gk_far, gv_far = call(
        cross_body,
        [((rows + 16, width), BF), (wide, F32), (wide, F32)],
        [],
        [qg_next, stats_next, k2, v2],
        steps=steps,
    )
    gq_far = lax.ppermute(gq_out, TM, to_next)
    gq, gk, gv = call(
        own_body,
        [(wide, BF)] * 3,
        [at],
        [q2, k2, v2, g2, stats_own, gq_far, gk_far, gv_far],
        [chip],
        steps=steps,
    )
    shape = (length, blocks, width)
    grad_x = call(unpack_body, [(wide, BF)], [at], [keep, gx_far], [gk])[0]
    return grad_x.reshape(shape), gq.reshape(shape), gk.reshape(shape), gv.reshape(shape), grad_bc


def solution(mesh):
    tm, blk = mesh.devices.shape
    fine = Mesh(
        mesh.devices.reshape(tm // 2, 2, blk // 8, 4, 2), TM + ("zl", "x", "c")
    )
    tokens = P(TM, ("zl", "x", "c"), None)
    return jax.shard_map(
        local,
        mesh=fine,
        in_specs=(tokens, P(), tokens, P(), P(), tokens, tokens, tokens, tokens),
        out_specs=(tokens,) * 4 + (P(TM + ("zl", "x", "c"), None),),
        check_vma=False,
    )
```

```python
import jax
import jax.numpy as jnp
from jax import lax
from jax.experimental import pallas as pl
from jax.experimental.pallas import tpu as pltpu
from jax.sharding import Mesh, PartitionSpec as P

HEAD = 64
LANES = 128
INJECT = 0.015625
CODE_UNIT = 4096.0
SCALE = 0.125
VMEM_BYTES = 60 * 1024 * 1024
LOW = -1e30
BF = jnp.bfloat16
F32 = jnp.float32
TM = ("y", "zh")
SM = pl.BlockSpec(memory_space=pltpu.SMEM)


GROUP = 512


def call(body, outs, scalars, arrays, first=(), steps=1):
    used = len(scalars) + len(arrays)

    def run(*refs):
        body(*refs[:used], *refs[used + len(first) :])

    def spec(shape):
        if steps == 1:
            return pl.BlockSpec(shape, lambda i: (0,) * len(shape))
        if len(shape) == 3:
            return pl.BlockSpec((1,) + tuple(shape[1:]), lambda i: (i, 0, 0))
        return pl.BlockSpec((shape[0], shape[1] // steps), lambda i: (0, i))

    return pl.pallas_call(
        run,
        out_shape=[jax.ShapeDtypeStruct(s, d) for s, d in outs],
        in_specs=[SM] * len(scalars)
        + [spec(a.shape) for a in arrays]
        + [pl.BlockSpec(memory_space=pl.ANY)] * len(first),
        out_specs=[spec(s) for s, d in outs],
        grid=(steps,),
        cost_estimate=pl.CostEstimate(flops=1, bytes_accessed=1, transcendentals=0),
        compiler_params=pltpu.CompilerParams(vmem_limit_bytes=VMEM_BYTES),
    )(*scalars, *arrays, *first)


def nn(a, b):
    return lax.dot_general(a, b, (((1,), (0,)), ((), ())), preferred_element_type=F32)


def nt(a, b):
    return lax.dot_general(a, b, (((1,), (1,)), ((), ())), preferred_element_type=F32)


def tn(a, b):
    return lax.dot_general(a, b, (((0,), (0,)), ((), ())), preferred_element_type=F32)


def iota(shape, dim):
    return lax.broadcasted_iota(jnp.int32, shape, dim)


def one(cond):
    return jnp.where(cond, 1.0, 0.0).astype(BF)


def halves(value, scale=1.0):
    low = jnp.where(iota((1, LANES), 1) < HEAD, scale, 0.0).astype(BF)
    high = jnp.where(iota((1, LANES), 1) < HEAD, 0.0, scale).astype(BF)
    return jnp.concatenate([value * low, value * high], axis=0)


def side(value):
    n = value.shape[0] // 2
    return jnp.concatenate([value[:n], value[n:]], axis=1)


def add_pieces(value, ref, rows):
    for piece in range(3):
        part = value.astype(BF)
        value = value - part.astype(F32)
        ref[rows:, piece * LANES : (piece + 1) * LANES] = part
    ref[rows:, 3 * LANES :] = jnp.zeros((16, GROUP - 3 * LANES), BF)


def from_pieces(ref, rows):
    a, b, c = (ref[rows:, i * LANES : (i + 1) * LANES].astype(F32) for i in range(3))
    return a + (b + c)


def join_body(q, g, stats, out):
    rows = q.shape[0]
    out[:rows, :] = q[...]
    out[rows : 2 * rows, :] = g[...]
    add_pieces(stats[0], out, 2 * rows)


def pack_body(at, x, g, codes, own, out):
    z = at[0]
    rows, width = x.shape
    n = rows // 2
    row, col = iota((n, rows), 0), iota((n, rows), 1)
    keep, give = one(col == 2 * row + z), one(col == 2 * row + 1 - z)
    here = z == 0
    for pick, code, ref in (
        (keep, jnp.where(here, codes[0], codes[1]), own),
        (give, jnp.where(here, codes[1], codes[0]), out),
    ):
        ref[:, :width] = nn(pick, x[...]).astype(BF)
        ref[:, width : 2 * width] = nn(pick, g[...]).astype(BF)
        both = jnp.concatenate([code >> 8, code & 255], axis=0).astype(F32)
        ref[:, 2 * width :] = jnp.concatenate([both, jnp.zeros_like(both)], axis=1).astype(BF)


def summary_body(
    at, own, got, w, rate, xs, gs, bc, sums, sums_t, scaled_x, scaled_g, leave, m1, m2, m3
):
    z, y = at[0], at[1]
    n = own.shape[0]
    rows = 2 * n
    width = xs.shape[1]
    mine = pl.multiple_of(z * n, n)
    other = pl.multiple_of((1 - z) * n, n)
    for src, start in ((own, mine), (got, other)):
        xs[pl.ds(start, n), :] = src[:, :width]
        gs[pl.ds(start, n), :] = src[:, width : 2 * width]
    mine_codes, other_codes = own[:, 2 * width :].astype(F32), got[:, 2 * width :].astype(F32)
    early = jnp.where(z == 0, mine_codes, other_codes)
    late = jnp.where(z == 0, other_codes, mine_codes)
    codes = jnp.concatenate([early[:, :n], late[:, :n]], axis=1)
    heads = codes.shape[0] // 2
    blank = jnp.zeros((LANES - heads, rows), F32)
    hi = jnp.concatenate([codes[:heads], blank], axis=0).astype(BF)
    lo = jnp.concatenate([codes[heads:], blank], axis=0).astype(BF)
    row, col = iota((rows, rows), 0), iota((rows, rows), 1)
    lower, upper = one(col <= row), one(row <= col)
    total = nt(lower, hi) * 256.0 + nt(lower, lo)
    sums[...] = total
    sums_t[...] = nn(hi, upper) * 256.0 + nn(lo, upper)
    whole = total.astype(jnp.int32)
    spread = one(iota((LANES, width), 1) // HEAD == iota((LANES, width), 0))
    wide = jnp.zeros((rows, width), F32)
    lasts = []
    for shift in (16, 8, 0):
        piece = ((whole >> shift) & 255).astype(F32).astype(BF)
        part = nn(piece, spread)
        lasts.append(part[rows - 1 :, :])
        wide = wide * 256.0 + part
    last = wide[rows - 1 :, :]
    slope = rate[...] * (-1.0 / CODE_UNIT)
    to_end = jnp.exp((last - wide) * slope)
    growth = jnp.exp(wide * slope)
    bc_rows = nn(xs[...], w[...]).astype(BF)
    bc[...] = bc_rows
    gone = xs[...].astype(F32) * to_end
    sx = gone.astype(BF)
    sg = (gs[...].astype(F32) * growth).astype(BF)
    scaled_x[...] = sx
    scaled_g[...] = sg
    leave[...] = to_end
    state = (tn(bc_rows[:, :LANES], sx) * INJECT).astype(BF)
    back = tn(bc_rows[:, LANES:], sg).astype(BF)
    tail = jnp.concatenate(lasts + [jnp.zeros((13, width), F32)], axis=0).astype(BF)
    for shift, ref in ((1, m1), (2, m2), (3, m3)):
        later = y + shift < 4

        @pl.when(later)
        def _():
            ref[:LANES, :] = state

        @pl.when(jnp.logical_not(later))
        def _():
            ref[:LANES, :] = back

        ref[LANES:, :] = tail


def inner_body(rate, xs, gs, bc, sums, sums_t, gx, gb, gc, x_t):
    rows, width = xs.shape
    row, col = iota((rows, rows), 0), iota((rows, rows), 1)
    ahead = row <= col
    b_rows, c_rows = bc[:, :LANES], bc[:, LANES:]
    kernel = nt(b_rows, c_rows) * INJECT
    mixing = jnp.zeros((rows, rows), F32)
    for p in range(width // LANES):
        at = slice(p * LANES, (p + 1) * LANES)
        x_pair, g_pair = xs[:, at], gs[:, at]
        both = nt(halves(x_pair), g_pair)
        parts = []
        for k in (0, 1):
            h = 2 * p + k
            gap = sums_t[h : h + 1, :] - sums[:, h : h + 1]
            decay = jnp.exp(jnp.where(ahead, gap * (rate[h] * (-1.0 / CODE_UNIT)), LOW))
            mixing = mixing + decay * both[k * rows : (k + 1) * rows]
            parts.append((decay * kernel).astype(BF))
        gx[:, at] = nn(jnp.concatenate(parts, axis=1), halves(g_pair))
        x_t[at, :] = x_pair.astype(F32).T.astype(BF)
    mixed = (mixing * INJECT).astype(BF)
    gb[...] = nn(mixed, c_rows)
    gc[...] = tn(mixed, b_rows)


def carry_body(
    at, order, m1, m2, m3, rate, gain, w, gs, bc, scaled_x, scaled_g, leave, gx, gb, gc, x_t,
    keep, give, mine, yours,
):
    z, y, core = at[0], at[1], at[3]
    n = keep.shape[0]
    slope = rate[...] * (-1.0 / CODE_UNIT)

    def fade(ref):
        v = ref[LANES : LANES + 16, :].astype(F32)
        return ((v[0:1] * 256.0 + v[1:2]) * 256.0 + v[2:3]) * slope

    l1, l2, l3 = fade(m1), fade(m2), fade(m3)
    s1, s2, s3 = (m[:LANES, :].astype(F32) for m in (m1, m2, m3))

    def use(cond, log):
        return jnp.where(cond, jnp.exp(log), 0.0)

    zero = jnp.zeros_like(l1)
    state = use(y >= 1, zero) * s1 + use(y >= 2, l1) * s2 + use(y >= 3, l1 + l2) * s3
    back = use(y < 3, zero) * s3 + use(y < 2, l3) * s2 + use(y < 1, l3 + l2) * s1
    state, back = state.astype(BF), back.astype(BF)
    b_cot = gb[...] + nt(scaled_x[...], back) * INJECT
    c_cot = gc[...] + nt(scaled_g[...], state)
    cot = jnp.concatenate([b_cot, c_cot], axis=1).astype(BF)
    out = gx[...] + leave[...] * (nn(bc[:, :LANES], back) * INJECT)
    out = out + gs[...].astype(F32) * gain[...] + nt(cot, w[...])

    @pl.when(z == 0)
    def _():
        keep[...] = out[:n].astype(BF)
        give[...] = out[n:].astype(BF)

    @pl.when(z == 1)
    def _():
        keep[...] = out[n:].astype(BF)
        give[...] = out[:n].astype(BF)

    grad = nn(x_t[...], cot) * order
    grad = grad.reshape(4, 8, 4, 2, 8, 2 * LANES)
    for side in (0, 1):

        @pl.when(core == side)
        def _():
            for x in range(4):
                mine[:, x] = grad[:, :, x, side]
                yours[:, x] = grad[:, :, x, 1 - side]


def unpack_body(at, keep, far, out):
    z = at[0]
    n = keep.shape[0]
    row, col = iota((2 * n, n), 0), iota((2 * n, n), 1)
    ours, theirs = one(row == 2 * col + z), one(row == 2 * col + 1 - z)
    out[...] = (nn(ours, keep[...]) + nn(theirs, far[...])).astype(BF)


def softened(k_pair, v_pair, q_pair, g_pair, seen):
    rows = q_pair.shape[0]
    score = nt(halves(k_pair, SCALE), q_pair)
    inner = nt(halves(v_pair), g_pair)
    result = []
    for k in (0, 1):
        s = jnp.where(seen, score[k * rows : (k + 1) * rows], LOW)
        result.append((s, inner[k * rows : (k + 1) * rows]))
    return result


def row_sums(s, d):
    top = jnp.max(s, axis=0, keepdims=True)
    e = jnp.exp(s - top)
    norm = jnp.sum(e, axis=0, keepdims=True)
    return e, top, norm, jnp.sum(e * d, axis=0, keepdims=True) / norm


def merged(log_a, delta_a, log_b, delta_b):
    top = jnp.maximum(log_a, log_b)
    a, b = jnp.exp(log_a - top), jnp.exp(log_b - top)
    norm = a + b
    return top + jnp.log(norm), (a * delta_a + b * delta_b) / norm


def seen_mask(rows, cross):
    key, query = iota((rows, rows), 0), iota((rows, rows), 1)
    order = key >= query if cross else key <= query
    return jnp.logical_and(order, (key & 1) == (query & 1))


def stats_body(q, k, v, g, stats):
    rows, width = q.shape
    seen = seen_mask(rows, False)
    logs, deltas = [], []
    for p in range(width // LANES):
        at = slice(p * LANES, (p + 1) * LANES)
        for s, d in softened(k[:, at], v[:, at], q[:, at], g[:, at], seen):
            e, top, norm, delta = row_sums(s, d)
            logs.append(top + jnp.log(norm))
            deltas.append(delta)
    stats[0] = jnp.concatenate(logs + deltas, axis=0)


def products(ps, ds, q_pair, k_pair, g_pair):
    p_side = jnp.concatenate(ps, axis=1)
    d_side = jnp.concatenate(ds, axis=1)
    grad_v = nn(p_side, halves(g_pair))
    grad_k = nn(d_side, halves(q_pair, SCALE))
    grad_q = tn(jnp.concatenate(ds, axis=0), halves(k_pair, SCALE))
    return grad_q, grad_k, grad_v


def cross_body(qg, k, v, gq, gk, gv):
    rows, width = k.shape
    heads = width // HEAD
    theirs = from_pieces(qg, 2 * rows)
    seen = seen_mask(rows, True)
    logs, deltas = [], []
    for p in range(width // LANES):
        at = slice(p * LANES, (p + 1) * LANES)
        q_pair, k_pair, g_pair = qg[:rows, at], k[:, at], qg[rows : 2 * rows, at]
        ps, ds = [], []
        for j, (s, d) in enumerate(softened(k_pair, v[:, at], q_pair, g_pair, seen)):
            h = 2 * p + j
            e, top, norm, delta = row_sums(s, d)
            log_here = top + jnp.log(norm)
            logs.append(log_here)
            deltas.append(delta)
            log_norm, delta = merged(
                log_here, delta, theirs[h : h + 1, :], theirs[heads + h : heads + h + 1, :]
            )
            prob = e * jnp.exp(top - log_norm)
            ps.append(prob.astype(BF))
            ds.append((prob * (d - delta)).astype(BF))
        a, b, c = products(ps, ds, q_pair, k_pair, g_pair)
        gq[:rows, at] = a.astype(BF)
        gk[:, at] = b
        gv[:, at] = c
    add_pieces(jnp.concatenate(logs + deltas, axis=0), gq, rows)


def own_body(at_ref, q, k, v, g, ours, gq_far, gk_far, gv_far, gq, gk, gv):
    rows, width = q.shape
    heads = width // HEAD
    seen = seen_mask(rows, False)
    begins = at_ref[2] == 0
    near = ours[0]
    away = from_pieces(gq_far, rows)
    for p in range(width // LANES):
        at = slice(p * LANES, (p + 1) * LANES)
        q_pair, k_pair, g_pair = q[:, at], k[:, at], g[:, at]
        ps, ds = [], []
        for j, (s, d) in enumerate(softened(k_pair, v[:, at], q_pair, g_pair, seen)):
            h = 2 * p + j
            far = jnp.where(begins, LOW, away[h : h + 1])
            log_norm, delta = merged(
                near[h : h + 1],
                near[heads + h : heads + h + 1],
                far,
                away[heads + h : heads + h + 1],
            )
            prob = jnp.exp(s - log_norm)
            ps.append(prob.astype(BF))
            ds.append((prob * (d - delta)).astype(BF))
        a, b, c = products(ps, ds, q_pair, k_pair, g_pair)
        gq[:, at] = (a + gq_far[:rows, at].astype(F32)).astype(BF)
        gk[:, at] = (b + gk_far[:, at]).astype(BF)
        gv[:, at] = (c + gv_far[:, at]).astype(BF)


def local(
    frames_x, bc_weight, decay_codes, decay_rates, skip_gain, queries, keys, values, cotangent
):
    length, blocks, width = frames_x.shape
    rows = length * blocks
    heads = decay_rates.shape[0]
    tm = lax.axis_size(TM)
    ny, nx, nz = lax.axis_size("y"), lax.axis_size("x"), lax.axis_size(("zh", "zl"))
    y, z, core = lax.axis_index("y"), lax.axis_index("zh"), lax.axis_index("c")
    at = jnp.stack([z, y, 2 * y + z, core]).astype(jnp.int32)
    flip = [(0, 1), (1, 0)]
    to_prev = [(i, i - 1) for i in range(1, tm)]
    to_next = [(i - 1, i) for i in range(1, tm)]

    def flat(a):
        return a.reshape(rows, width)

    x2, g2, q2, k2, v2 = (flat(a) for a in (frames_x, cotangent, queries, keys, values))
    codes = jnp.transpose(decay_codes, (1, 2, 0))
    rate_wide = jnp.repeat(decay_rates, HEAD)[None]
    gain_wide = jnp.repeat(skip_gain, HEAD)[None]

    msg = (rows // 2, 2 * width + LANES)
    own, out = call(pack_body, [(msg, BF)] * 2, [at], [x2, g2, codes])
    got = lax.ppermute(out, "zh", flip)

    steps = width // GROUP
    stats = ((steps, 2 * GROUP // HEAD, rows), F32)
    stats_own = call(stats_body, [stats], [], [q2, k2, v2, g2], steps=steps)[0]
    qg = call(join_body, [((2 * rows + 16, width), BF)], [], [q2, g2, stats_own], steps=steps)[0]
    qg_next = lax.ppermute(qg, TM, to_prev)

    wide = (rows, width)
    state = (LANES + 16, width)
    square = (rows, LANES)
    xs, gs, bc, sums, sums_t, scaled_x, scaled_g, leave, m1, m2, m3 = call(
        summary_body,
        [(wide, BF), (wide, BF), ((rows, 2 * LANES), BF), (square, F32), (square, F32)]
        + [(wide, BF), (wide, BF), (wide, F32)]
        + [(state, BF)] * 3,
        [at],
        [own, got, bc_weight, rate_wide],
        [qg],
    )
    m1, m2, m3 = (
        lax.ppermute(m, "y", [(i, (i + s) % ny) for i in range(ny)])
        for s, m in ((1, m1), (2, m2), (3, m3))
    )
    gx, gb, gc, x_t = call(
        inner_body,
        [(wide, F32), (square, F32), (square, F32), ((width, rows), BF)],
        [decay_rates],
        [xs, gs, bc, sums, sums_t],
    )
    order = 1.0 / (rows * tm * lax.axis_size(("zl", "x", "c")))
    keep, give, mine, yours = call(
        lambda at_ref, *refs: carry_body(at_ref, order, *refs),
        [((rows // 2, width), BF)] * 2 + [((ny, nx, nz, 8, 2 * LANES), F32)] * 2,
        [at],
        [m1, m2, m3, rate_wide, gain_wide, bc_weight, gs, bc, scaled_x, scaled_g, leave, gx, gb, gc, x_t],
        [qg_next],
    )
    gx_far = lax.ppermute(give, "zh", flip)

    chip = (mine + lax.ppermute(yours, "c", flip)).astype(BF)
    chip = chip.reshape(ny * nx, nz * 8, 2 * LANES)
    spread = lax.all_to_all(chip, ("y", "x"), 0, 0, tiled=True)
    plane = jnp.sum(spread.astype(F32), axis=0).astype(BF).reshape(nz, 8, 2 * LANES)
    spread = lax.all_to_all(plane, ("zh", "zl"), 0, 0, tiled=True)
    grad_bc = jnp.sum(spread.astype(F32), axis=0)

    gq_out, gk_far, gv_far = call(
        cross_body,
        [((rows + 16, width), BF), (wide, F32), (wide, F32)],
        [],
        [qg_next, k2, v2],
        steps=steps,
    )
    gq_far = lax.ppermute(gq_out, TM, to_next)
    grad_x = call(unpack_body, [(wide, BF)], [at], [keep, gx_far], [chip])[0]
    grad_x = grad_x.reshape(length, blocks, width)
    gq, gk, gv = call(
        own_body,
        [(wide, BF)] * 3,
        [at],
        [q2, k2, v2, g2, stats_own, gq_far, gk_far, gv_far],
        [chip, grad_x],
        steps=steps,
    )
    shape = (length, blocks, width)
    return grad_x, gq.reshape(shape), gk.reshape(shape), gv.reshape(shape), grad_bc


def solution(mesh):
    tm, blk = mesh.devices.shape
    fine = Mesh(
        mesh.devices.reshape(tm // 2, 2, blk // 8, 4, 2), TM + ("zl", "x", "c")
    )
    tokens = P(TM, ("zl", "x", "c"), None)
    return jax.shard_map(
        local,
        mesh=fine,
        in_specs=(tokens, P(), tokens, P(), P(), tokens, tokens, tokens, tokens),
        out_specs=(tokens,) * 4 + (P(TM + ("zl", "x", "c"), None),),
        check_vma=False,
    )
```

```python
import jax
import jax.numpy as jnp
from jax import lax
from jax.experimental import pallas as pl
from jax.experimental.pallas import tpu as pltpu
from jax.sharding import Mesh, PartitionSpec as P

HEAD = 64
LANES = 128
INJECT = 0.015625
CODE_UNIT = 4096.0
SCALE = 0.125
VMEM_BYTES = 60 * 1024 * 1024
LOW = -1e30
BF = jnp.bfloat16
F32 = jnp.float32
TM = ("y", "zh")
SM = pl.BlockSpec(memory_space=pltpu.SMEM)


GROUP = 512


def call(body, outs, scalars, arrays, first=(), steps=1):
    used = len(scalars) + len(arrays)

    def run(*refs):
        body(*refs[:used], *refs[used + len(first) :])

    def spec(shape):
        if steps == 1:
            return pl.BlockSpec(shape, lambda i: (0,) * len(shape))
        if len(shape) == 3:
            return pl.BlockSpec((1,) + tuple(shape[1:]), lambda i: (i, 0, 0))
        return pl.BlockSpec((shape[0], shape[1] // steps), lambda i: (0, i))

    return pl.pallas_call(
        run,
        out_shape=[jax.ShapeDtypeStruct(s, d) for s, d in outs],
        in_specs=[SM] * len(scalars)
        + [spec(a.shape) for a in arrays]
        + [pl.BlockSpec(memory_space=pl.ANY)] * len(first),
        out_specs=[spec(s) for s, d in outs],
        grid=(steps,),
        cost_estimate=pl.CostEstimate(flops=1, bytes_accessed=1, transcendentals=0),
        compiler_params=pltpu.CompilerParams(vmem_limit_bytes=VMEM_BYTES),
    )(*scalars, *arrays, *first)


def nn(a, b):
    return lax.dot_general(a, b, (((1,), (0,)), ((), ())), preferred_element_type=F32)


def nt(a, b):
    return lax.dot_general(a, b, (((1,), (1,)), ((), ())), preferred_element_type=F32)


def tn(a, b):
    return lax.dot_general(a, b, (((0,), (0,)), ((), ())), preferred_element_type=F32)


def iota(shape, dim):
    return lax.broadcasted_iota(jnp.int32, shape, dim)


def one(cond):
    return jnp.where(cond, 1.0, 0.0).astype(BF)


def halves(value, scale=1.0):
    low = jnp.where(iota((1, LANES), 1) < HEAD, scale, 0.0).astype(BF)
    high = jnp.where(iota((1, LANES), 1) < HEAD, 0.0, scale).astype(BF)
    return jnp.concatenate([value * low, value * high], axis=0)


def side(value):
    n = value.shape[0] // 2
    return jnp.concatenate([value[:n], value[n:]], axis=1)


def add_pieces(value, ref, rows):
    for piece in range(3):
        part = value.astype(BF)
        value = value - part.astype(F32)
        ref[rows:, piece * LANES : (piece + 1) * LANES] = part
    ref[rows:, 3 * LANES :] = jnp.zeros((16, GROUP - 3 * LANES), BF)


def from_pieces(ref, rows):
    a, b, c = (ref[rows:, i * LANES : (i + 1) * LANES].astype(F32) for i in range(3))
    return a + (b + c)


def join_body(q, g, stats, out):
    rows = q.shape[0]
    out[:rows, :] = q[...]
    out[rows : 2 * rows, :] = g[...]
    add_pieces(stats[0], out, 2 * rows)


def pack_body(at, x, g, codes, own, out):
    z = at[0]
    rows, width = x.shape
    n = rows // 2
    row, col = iota((n, rows), 0), iota((n, rows), 1)
    keep, give = one(col == 2 * row + z), one(col == 2 * row + 1 - z)
    here = z == 0
    for pick, code, ref in (
        (keep, jnp.where(here, codes[0], codes[1]), own),
        (give, jnp.where(here, codes[1], codes[0]), out),
    ):
        ref[:, :width] = nn(pick, x[...]).astype(BF)
        ref[:, width : 2 * width] = nn(pick, g[...]).astype(BF)
        both = jnp.concatenate([code >> 8, code & 255], axis=0).astype(F32)
        ref[:, 2 * width :] = jnp.concatenate([both, jnp.zeros_like(both)], axis=1).astype(BF)


def summary_body(
    at, own, got, w, rate, xs, gs, bc, sums, sums_t, scaled_x, scaled_g, leave, m1, m2, m3
):
    z, y = at[0], at[1]
    n = own.shape[0]
    rows = 2 * n
    width = xs.shape[1]
    mine = pl.multiple_of(z * n, n)
    other = pl.multiple_of((1 - z) * n, n)
    for src, start in ((own, mine), (got, other)):
        xs[pl.ds(start, n), :] = src[:, :width]
        gs[pl.ds(start, n), :] = src[:, width : 2 * width]
    mine_codes, other_codes = own[:, 2 * width :].astype(F32), got[:, 2 * width :].astype(F32)
    early = jnp.where(z == 0, mine_codes, other_codes)
    late = jnp.where(z == 0, other_codes, mine_codes)
    codes = jnp.concatenate([early[:, :n], late[:, :n]], axis=1)
    heads = codes.shape[0] // 2
    blank = jnp.zeros((LANES - heads, rows), F32)
    hi = jnp.concatenate([codes[:heads], blank], axis=0).astype(BF)
    lo = jnp.concatenate([codes[heads:], blank], axis=0).astype(BF)
    row, col = iota((rows, rows), 0), iota((rows, rows), 1)
    lower, upper = one(col <= row), one(row <= col)
    total = nt(lower, hi) * 256.0 + nt(lower, lo)
    sums[...] = total
    sums_t[...] = nn(hi, upper) * 256.0 + nn(lo, upper)
    whole = total.astype(jnp.int32)
    spread = one(iota((LANES, width), 1) // HEAD == iota((LANES, width), 0))
    wide = jnp.zeros((rows, width), F32)
    lasts = []
    for shift in (16, 8, 0):
        piece = ((whole >> shift) & 255).astype(F32).astype(BF)
        part = nn(piece, spread)
        lasts.append(part[rows - 1 :, :])
        wide = wide * 256.0 + part
    last = wide[rows - 1 :, :]
    slope = rate[...] * (-1.0 / CODE_UNIT)
    to_end = jnp.exp((last - wide) * slope)
    growth = jnp.exp(wide * slope)
    bc_rows = nn(xs[...], w[...]).astype(BF)
    bc[...] = bc_rows
    gone = xs[...].astype(F32) * to_end
    sx = gone.astype(BF)
    sg = (gs[...].astype(F32) * growth).astype(BF)
    scaled_x[...] = sx
    scaled_g[...] = sg
    leave[...] = to_end
    state = (tn(bc_rows[:, :LANES], sx) * INJECT).astype(BF)
    back = tn(bc_rows[:, LANES:], sg).astype(BF)
    tail = jnp.concatenate(lasts + [jnp.zeros((13, width), F32)], axis=0).astype(BF)
    for shift, ref in ((1, m1), (2, m2), (3, m3)):
        later = y + shift < 4

        @pl.when(later)
        def _():
            ref[:LANES, :] = state

        @pl.when(jnp.logical_not(later))
        def _():
            ref[:LANES, :] = back

        ref[LANES:, :] = tail


def inner_body(rate, xs, gs, bc, sums, sums_t, gx, gb, gc, x_t):
    rows, width = xs.shape
    row, col = iota((rows, rows), 0), iota((rows, rows), 1)
    ahead = row <= col
    b_rows, c_rows = bc[:, :LANES], bc[:, LANES:]
    kernel = nt(b_rows, c_rows) * INJECT
    mixing = jnp.zeros((rows, rows), F32)
    for p in range(width // LANES):
        at = slice(p * LANES, (p + 1) * LANES)
        x_pair, g_pair = xs[:, at], gs[:, at]
        both = nt(halves(x_pair), g_pair)
        parts = []
        for k in (0, 1):
            h = 2 * p + k
            gap = sums_t[h : h + 1, :] - sums[:, h : h + 1]
            decay = jnp.exp(jnp.where(ahead, gap * (rate[h] * (-1.0 / CODE_UNIT)), LOW))
            mixing = mixing + decay * both[k * rows : (k + 1) * rows]
            parts.append((decay * kernel).astype(BF))
        gx[:, at] = nn(jnp.concatenate(parts, axis=1), halves(g_pair))
        x_t[at, :] = x_pair.astype(F32).T.astype(BF)
    mixed = (mixing * INJECT).astype(BF)
    gb[...] = nn(mixed, c_rows)
    gc[...] = tn(mixed, b_rows)


def carry_body(
    at, order, m1, m2, m3, rate, gain, w, gs, bc, scaled_x, scaled_g, leave, gx, gb, gc, x_t,
    keep, give, mine, yours,
):
    z, y, core = at[0], at[1], at[3]
    n = keep.shape[0]
    slope = rate[...] * (-1.0 / CODE_UNIT)

    def fade(ref):
        v = ref[LANES : LANES + 16, :].astype(F32)
        return ((v[0:1] * 256.0 + v[1:2]) * 256.0 + v[2:3]) * slope

    l1, l2, l3 = fade(m1), fade(m2), fade(m3)
    s1, s2, s3 = (m[:LANES, :].astype(F32) for m in (m1, m2, m3))

    def use(cond, log):
        return jnp.where(cond, jnp.exp(log), 0.0)

    zero = jnp.zeros_like(l1)
    state = use(y >= 1, zero) * s1 + use(y >= 2, l1) * s2 + use(y >= 3, l1 + l2) * s3
    back = use(y < 3, zero) * s3 + use(y < 2, l3) * s2 + use(y < 1, l3 + l2) * s1
    state, back = state.astype(BF), back.astype(BF)
    b_cot = gb[...] + nt(scaled_x[...], back) * INJECT
    c_cot = gc[...] + nt(scaled_g[...], state)
    cot = jnp.concatenate([b_cot, c_cot], axis=1).astype(BF)
    out = gx[...] + leave[...] * (nn(bc[:, :LANES], back) * INJECT)
    out = out + gs[...].astype(F32) * gain[...] + nt(cot, w[...])

    @pl.when(z == 0)
    def _():
        keep[...] = out[:n].astype(BF)
        give[...] = out[n:].astype(BF)

    @pl.when(z == 1)
    def _():
        keep[...] = out[n:].astype(BF)
        give[...] = out[:n].astype(BF)

    grad = nn(x_t[...], cot) * order
    grad = grad.reshape(4, 8, 4, 2, 8, 2 * LANES)
    for side in (0, 1):

        @pl.when(core == side)
        def _():
            for x in range(4):
                mine[:, x] = grad[:, :, x, side]
                yours[:, x] = grad[:, :, x, 1 - side]


def unpack_body(at, keep, far, out):
    z = at[0]
    n = keep.shape[0]
    row, col = iota((2 * n, n), 0), iota((2 * n, n), 1)
    ours, theirs = one(row == 2 * col + z), one(row == 2 * col + 1 - z)
    out[...] = (nn(ours, keep[...]) + nn(theirs, far[...])).astype(BF)


def softened(k_pair, v_pair, q_pair, g_pair, seen):
    rows = q_pair.shape[0]
    score = nt(halves(k_pair, SCALE), q_pair)
    inner = nt(halves(v_pair), g_pair)
    result = []
    for k in (0, 1):
        s = jnp.where(seen, score[k * rows : (k + 1) * rows], LOW)
        result.append((s, inner[k * rows : (k + 1) * rows]))
    return result


def row_sums(s, d):
    top = jnp.max(s, axis=0, keepdims=True)
    e = jnp.exp(s - top)
    norm = jnp.sum(e, axis=0, keepdims=True)
    return e, top, norm, jnp.sum(e * d, axis=0, keepdims=True) / norm


def merged(log_a, delta_a, log_b, delta_b):
    top = jnp.maximum(log_a, log_b)
    a, b = jnp.exp(log_a - top), jnp.exp(log_b - top)
    norm = a + b
    return top + jnp.log(norm), (a * delta_a + b * delta_b) / norm


def seen_mask(rows, cross):
    key, query = iota((rows, rows), 0), iota((rows, rows), 1)
    order = key >= query if cross else key <= query
    return jnp.logical_and(order, (key & 1) == (query & 1))


def stats_body(q, k, v, g, stats):
    rows, width = q.shape
    seen = seen_mask(rows, False)
    logs, deltas = [], []
    for p in range(width // LANES):
        at = slice(p * LANES, (p + 1) * LANES)
        for s, d in softened(k[:, at], v[:, at], q[:, at], g[:, at], seen):
            e, top, norm, delta = row_sums(s, d)
            logs.append(top + jnp.log(norm))
            deltas.append(delta)
    stats[0] = jnp.concatenate(logs + deltas, axis=0)


def products(ps, ds, q_pair, k_pair, g_pair):
    p_side = jnp.concatenate(ps, axis=1)
    d_side = jnp.concatenate(ds, axis=1)
    grad_v = nn(p_side, halves(g_pair))
    grad_k = nn(d_side, halves(q_pair, SCALE))
    grad_q = tn(jnp.concatenate(ds, axis=0), halves(k_pair, SCALE))
    return grad_q, grad_k, grad_v


def cross_body(qg, k, v, gq, gk, gv):
    rows, width = k.shape
    heads = width // HEAD
    theirs = from_pieces(qg, 2 * rows)
    seen = seen_mask(rows, True)
    logs, deltas = [], []
    for p in range(width // LANES):
        at = slice(p * LANES, (p + 1) * LANES)
        q_pair, k_pair, g_pair = qg[:rows, at], k[:, at], qg[rows : 2 * rows, at]
        ps, ds = [], []
        for j, (s, d) in enumerate(softened(k_pair, v[:, at], q_pair, g_pair, seen)):
            h = 2 * p + j
            e, top, norm, delta = row_sums(s, d)
            log_here = top + jnp.log(norm)
            logs.append(log_here)
            deltas.append(delta)
            log_norm, delta = merged(
                log_here, delta, theirs[h : h + 1, :], theirs[heads + h : heads + h + 1, :]
            )
            prob = e * jnp.exp(top - log_norm)
            ps.append(prob.astype(BF))
            ds.append((prob * (d - delta)).astype(BF))
        a, b, c = products(ps, ds, q_pair, k_pair, g_pair)
        gq[:rows, at] = a.astype(BF)
        gk[:, at] = b
        gv[:, at] = c
    add_pieces(jnp.concatenate(logs + deltas, axis=0), gq, rows)


def own_body(at_ref, q, k, v, g, ours, gq_far, gk_far, gv_far, gq, gk, gv):
    rows, width = q.shape
    heads = width // HEAD
    seen = seen_mask(rows, False)
    begins = at_ref[2] == 0
    near = ours[0]
    away = from_pieces(gq_far, rows)
    for p in range(width // LANES):
        at = slice(p * LANES, (p + 1) * LANES)
        q_pair, k_pair, g_pair = q[:, at], k[:, at], g[:, at]
        ps, ds = [], []
        for j, (s, d) in enumerate(softened(k_pair, v[:, at], q_pair, g_pair, seen)):
            h = 2 * p + j
            far = jnp.where(begins, LOW, away[h : h + 1])
            log_norm, delta = merged(
                near[h : h + 1],
                near[heads + h : heads + h + 1],
                far,
                away[heads + h : heads + h + 1],
            )
            prob = jnp.exp(s - log_norm)
            ps.append(prob.astype(BF))
            ds.append((prob * (d - delta)).astype(BF))
        a, b, c = products(ps, ds, q_pair, k_pair, g_pair)
        gq[:, at] = (a + gq_far[:rows, at].astype(F32)).astype(BF)
        gk[:, at] = (b + gk_far[:, at]).astype(BF)
        gv[:, at] = (c + gv_far[:, at]).astype(BF)


def local(
    frames_x, bc_weight, decay_codes, decay_rates, skip_gain, queries, keys, values, cotangent
):
    length, blocks, width = frames_x.shape
    rows = length * blocks
    heads = decay_rates.shape[0]
    tm = lax.axis_size(TM)
    ny, nx, nz = lax.axis_size("y"), lax.axis_size("x"), lax.axis_size(("zh", "zl"))
    y, z, core = lax.axis_index("y"), lax.axis_index("zh"), lax.axis_index("c")
    at = jnp.stack([z, y, 2 * y + z, core]).astype(jnp.int32)
    flip = [(0, 1), (1, 0)]
    to_prev = [(i, i - 1) for i in range(1, tm)]
    to_next = [(i - 1, i) for i in range(1, tm)]

    def flat(a):
        return a.reshape(rows, width)

    x2, g2, q2, k2, v2 = (flat(a) for a in (frames_x, cotangent, queries, keys, values))
    codes = jnp.transpose(decay_codes, (1, 2, 0))
    rate_wide = jnp.repeat(decay_rates, HEAD)[None]
    gain_wide = jnp.repeat(skip_gain, HEAD)[None]

    msg = (rows // 2, 2 * width + LANES)
    own, out = call(pack_body, [(msg, BF)] * 2, [at], [x2, g2, codes])
    got = lax.ppermute(out, "zh", flip)

    steps = width // GROUP
    stats = ((steps, 2 * GROUP // HEAD, rows), F32)
    stats_own = call(stats_body, [stats], [], [q2, k2, v2, g2], steps=steps)[0]
    qg = call(join_body, [((2 * rows + 16, width), BF)], [], [q2, g2, stats_own], steps=steps)[0]
    qg_next = lax.ppermute(qg, TM, to_prev)

    wide = (rows, width)
    state = (LANES + 16, width)
    square = (rows, LANES)
    xs, gs, bc, sums, sums_t, scaled_x, scaled_g, leave, m1, m2, m3 = call(
        summary_body,
        [(wide, BF), (wide, BF), ((rows, 2 * LANES), BF), (square, F32), (square, F32)]
        + [(wide, BF), (wide, BF), (wide, F32)]
        + [(state, BF)] * 3,
        [at],
        [own, got, bc_weight, rate_wide],
        [qg],
    )
    m1, m2, m3 = (
        lax.ppermute(m, "y", [(i, (i + s) % ny) for i in range(ny)])
        for s, m in ((1, m1), (2, m2), (3, m3))
    )
    gx, gb, gc, x_t = call(
        inner_body,
        [(wide, F32), (square, F32), (square, F32), ((width, rows), BF)],
        [decay_rates],
        [xs, gs, bc, sums, sums_t],
    )
    gq_out, gk_far, gv_far = call(
        cross_body,
        [((rows + 16, width), BF), (wide, F32), (wide, F32)],
        [],
        [qg_next, k2, v2],
        steps=steps,
    )
    order = 1.0 / (rows * tm * lax.axis_size(("zl", "x", "c")))
    keep, give, mine, yours = call(
        lambda at_ref, *refs: carry_body(at_ref, order, *refs),
        [((rows // 2, width), BF)] * 2 + [((ny, nx, nz, 8, 2 * LANES), F32)] * 2,
        [at],
        [m1, m2, m3, rate_wide, gain_wide, bc_weight, gs, bc, scaled_x, scaled_g, leave, gx, gb, gc, x_t],
        [gq_out],
    )
    gx_far = lax.ppermute(give, "zh", flip)

    chip = (mine + lax.ppermute(yours, "c", flip)).astype(BF)
    chip = chip.reshape(ny * nx, nz * 8, 2 * LANES)
    spread = lax.all_to_all(chip, ("y", "x"), 0, 0, tiled=True)
    plane = jnp.sum(spread.astype(F32), axis=0).astype(BF).reshape(nz, 8, 2 * LANES)
    spread = lax.all_to_all(plane, ("zh", "zl"), 0, 0, tiled=True)
    grad_bc = jnp.sum(spread.astype(F32), axis=0)

    gq_far = lax.ppermute(gq_out, TM, to_next)
    gq, gk, gv = call(
        own_body,
        [(wide, BF)] * 3,
        [at],
        [q2, k2, v2, g2, stats_own, gq_far, gk_far, gv_far],
        [chip],
        steps=steps,
    )
    shape = (length, blocks, width)
    grad_x = call(unpack_body, [(wide, BF)], [at], [keep, gx_far], [gk])[0]
    return grad_x.reshape(shape), gq.reshape(shape), gk.reshape(shape), gv.reshape(shape), grad_bc


def solution(mesh):
    tm, blk = mesh.devices.shape
    fine = Mesh(
        mesh.devices.reshape(tm // 2, 2, blk // 8, 4, 2), TM + ("zl", "x", "c")
    )
    tokens = P(TM, ("zl", "x", "c"), None)
    return jax.shard_map(
        local,
        mesh=fine,
        in_specs=(tokens, P(), tokens, P(), P(), tokens, tokens, tokens, tokens),
        out_specs=(tokens,) * 4 + (P(TM + ("zl", "x", "c"), None),),
        check_vma=False,
    )
```

```python
import jax
import jax.numpy as jnp
from jax import lax
from jax.experimental import pallas as pl
from jax.experimental.pallas import tpu as pltpu
from jax.sharding import Mesh, PartitionSpec as P

HEAD = 64
LANES = 128
INJECT = 0.015625
CODE_UNIT = 4096.0
SCALE = 0.125
VMEM_BYTES = 60 * 1024 * 1024
LOW = -1e30
BF = jnp.bfloat16
F32 = jnp.float32
TM = ("y", "zh")
SM = pl.BlockSpec(memory_space=pltpu.SMEM)


GROUP = 512


def call(body, outs, scalars, arrays, first=(), steps=1):
    used = len(scalars) + len(arrays)

    def run(*refs):
        body(*refs[:used], *refs[used + len(first) :])

    def spec(shape):
        if steps == 1:
            return pl.BlockSpec(shape, lambda i: (0,) * len(shape))
        if len(shape) == 3:
            return pl.BlockSpec((1,) + tuple(shape[1:]), lambda i: (i, 0, 0))
        return pl.BlockSpec((shape[0], shape[1] // steps), lambda i: (0, i))

    return pl.pallas_call(
        run,
        out_shape=[jax.ShapeDtypeStruct(s, d) for s, d in outs],
        in_specs=[SM] * len(scalars)
        + [spec(a.shape) for a in arrays]
        + [pl.BlockSpec(memory_space=pl.ANY)] * len(first),
        out_specs=[spec(s) for s, d in outs],
        grid=(steps,),
        cost_estimate=pl.CostEstimate(flops=1, bytes_accessed=1, transcendentals=0),
        compiler_params=pltpu.CompilerParams(vmem_limit_bytes=VMEM_BYTES),
    )(*scalars, *arrays, *first)


def nn(a, b):
    return lax.dot_general(a, b, (((1,), (0,)), ((), ())), preferred_element_type=F32)


def nt(a, b):
    return lax.dot_general(a, b, (((1,), (1,)), ((), ())), preferred_element_type=F32)


def tn(a, b):
    return lax.dot_general(a, b, (((0,), (0,)), ((), ())), preferred_element_type=F32)


def iota(shape, dim):
    return lax.broadcasted_iota(jnp.int32, shape, dim)


def one(cond):
    return jnp.where(cond, 1.0, 0.0).astype(BF)


def halves(value, scale=1.0):
    low = jnp.where(iota((1, LANES), 1) < HEAD, scale, 0.0).astype(BF)
    high = jnp.where(iota((1, LANES), 1) < HEAD, 0.0, scale).astype(BF)
    return jnp.concatenate([value * low, value * high], axis=0)


def side(value):
    n = value.shape[0] // 2
    return jnp.concatenate([value[:n], value[n:]], axis=1)


def add_pieces(value, ref, rows):
    for piece in range(3):
        part = value.astype(BF)
        value = value - part.astype(F32)
        ref[rows:, piece * LANES : (piece + 1) * LANES] = part
    ref[rows:, 3 * LANES :] = jnp.zeros((16, GROUP - 3 * LANES), BF)


def from_pieces(ref, rows):
    a, b, c = (ref[rows:, i * LANES : (i + 1) * LANES].astype(F32) for i in range(3))
    return a + (b + c)


def join_body(q, g, stats, out):
    rows = q.shape[0]
    out[:rows, :] = q[...]
    out[rows : 2 * rows, :] = g[...]
    add_pieces(stats[0], out, 2 * rows)


def pack_body(at, x, g, codes, own, out):
    z = at[0]
    rows, width = x.shape
    n = rows // 2
    row, col = iota((n, rows), 0), iota((n, rows), 1)
    keep, give = one(col == 2 * row + z), one(col == 2 * row + 1 - z)
    here = z == 0
    for pick, code, ref in (
        (keep, jnp.where(here, codes[0], codes[1]), own),
        (give, jnp.where(here, codes[1], codes[0]), out),
    ):
        ref[:, :width] = nn(pick, x[...]).astype(BF)
        ref[:, width : 2 * width] = nn(pick, g[...]).astype(BF)
        both = jnp.concatenate([code >> 8, code & 255], axis=0).astype(F32)
        ref[:, 2 * width :] = jnp.concatenate([both, jnp.zeros_like(both)], axis=1).astype(BF)


def summary_body(
    at, own, got, w, rate, xs, gs, bc, sums, sums_t, scaled_x, scaled_g, leave, m1, m2, m3
):
    z, y = at[0], at[1]
    n = own.shape[0]
    rows = 2 * n
    width = xs.shape[1]
    mine = pl.multiple_of(z * n, n)
    other = pl.multiple_of((1 - z) * n, n)
    for src, start in ((own, mine), (got, other)):
        xs[pl.ds(start, n), :] = src[:, :width]
        gs[pl.ds(start, n), :] = src[:, width : 2 * width]
    mine_codes, other_codes = own[:, 2 * width :].astype(F32), got[:, 2 * width :].astype(F32)
    early = jnp.where(z == 0, mine_codes, other_codes)
    late = jnp.where(z == 0, other_codes, mine_codes)
    codes = jnp.concatenate([early[:, :n], late[:, :n]], axis=1)
    heads = codes.shape[0] // 2
    blank = jnp.zeros((LANES - heads, rows), F32)
    hi = jnp.concatenate([codes[:heads], blank], axis=0).astype(BF)
    lo = jnp.concatenate([codes[heads:], blank], axis=0).astype(BF)
    row, col = iota((rows, rows), 0), iota((rows, rows), 1)
    lower, upper = one(col <= row), one(row <= col)
    total = nt(lower, hi) * 256.0 + nt(lower, lo)
    sums[...] = total
    sums_t[...] = nn(hi, upper) * 256.0 + nn(lo, upper)
    whole = total.astype(jnp.int32)
    spread = one(iota((LANES, width), 1) // HEAD == iota((LANES, width), 0))
    wide = jnp.zeros((rows, width), F32)
    lasts = []
    for shift in (16, 8, 0):
        piece = ((whole >> shift) & 255).astype(F32).astype(BF)
        part = nn(piece, spread)
        lasts.append(part[rows - 1 :, :])
        wide = wide * 256.0 + part
    last = wide[rows - 1 :, :]
    slope = rate[...] * (-1.0 / CODE_UNIT)
    to_end = jnp.exp((last - wide) * slope)
    growth = jnp.exp(wide * slope)
    bc_rows = nn(xs[...], w[...]).astype(BF)
    bc[...] = bc_rows
    gone = xs[...].astype(F32) * to_end
    sx = gone.astype(BF)
    sg = (gs[...].astype(F32) * growth).astype(BF)
    scaled_x[...] = sx
    scaled_g[...] = sg
    leave[...] = to_end.astype(BF)
    state = (tn(bc_rows[:, :LANES], sx) * INJECT).astype(BF)
    back = tn(bc_rows[:, LANES:], sg).astype(BF)
    tail = jnp.concatenate(lasts + [jnp.zeros((13, width), F32)], axis=0).astype(BF)
    for shift, ref in ((1, m1), (2, m2), (3, m3)):
        later = y + shift < 4

        @pl.when(later)
        def _():
            ref[:LANES, :] = state

        @pl.when(jnp.logical_not(later))
        def _():
            ref[:LANES, :] = back

        ref[LANES:, :] = tail


def inner_body(rate, xs, gs, bc, sums, sums_t, gx, gb, gc, x_t):
    rows, width = xs.shape
    row, col = iota((rows, rows), 0), iota((rows, rows), 1)
    ahead = row <= col
    b_rows, c_rows = bc[:, :LANES], bc[:, LANES:]
    kernel = nt(b_rows, c_rows) * INJECT
    mixing = jnp.zeros((rows, rows), F32)
    for p in range(width // LANES):
        at = slice(p * LANES, (p + 1) * LANES)
        x_pair, g_pair = xs[:, at], gs[:, at]
        both = nt(halves(x_pair), g_pair)
        parts = []
        for k in (0, 1):
            h = 2 * p + k
            gap = sums_t[h : h + 1, :] - sums[:, h : h + 1]
            decay = jnp.exp(jnp.where(ahead, gap * (rate[h] * (-1.0 / CODE_UNIT)), LOW))
            mixing = mixing + decay * both[k * rows : (k + 1) * rows]
            parts.append((decay * kernel).astype(BF))
        gx[:, at] = nn(jnp.concatenate(parts, axis=1), halves(g_pair)).astype(BF)
        x_t[at, :] = x_pair.astype(F32).T.astype(BF)
    mixed = (mixing * INJECT).astype(BF)
    gb[...] = nn(mixed, c_rows)
    gc[...] = tn(mixed, b_rows)


def carry_body(
    at, order, m1, m2, m3, rate, gain, w, gs, bc, scaled_x, scaled_g, leave, gx, gb, gc, x_t,
    keep, give, mine, yours,
):
    z, y, core = at[0], at[1], at[3]
    n = keep.shape[0]
    slope = rate[...] * (-1.0 / CODE_UNIT)

    def fade(ref):
        v = ref[LANES : LANES + 16, :].astype(F32)
        return ((v[0:1] * 256.0 + v[1:2]) * 256.0 + v[2:3]) * slope

    l1, l2, l3 = fade(m1), fade(m2), fade(m3)
    s1, s2, s3 = (m[:LANES, :].astype(F32) for m in (m1, m2, m3))

    def use(cond, log):
        return jnp.where(cond, jnp.exp(log), 0.0)

    zero = jnp.zeros_like(l1)
    state = use(y >= 1, zero) * s1 + use(y >= 2, l1) * s2 + use(y >= 3, l1 + l2) * s3
    back = use(y < 3, zero) * s3 + use(y < 2, l3) * s2 + use(y < 1, l3 + l2) * s1
    state, back = state.astype(BF), back.astype(BF)
    b_cot = gb[...] + nt(scaled_x[...], back) * INJECT
    c_cot = gc[...] + nt(scaled_g[...], state)
    cot = jnp.concatenate([b_cot, c_cot], axis=1).astype(BF)
    out = gx[...].astype(F32) + leave[...].astype(F32) * (nn(bc[:, :LANES], back) * INJECT)
    out = out + gs[...].astype(F32) * gain[...] + nt(cot, w[...])

    @pl.when(z == 0)
    def _():
        keep[...] = out[:n].astype(BF)
        give[...] = out[n:].astype(BF)

    @pl.when(z == 1)
    def _():
        keep[...] = out[n:].astype(BF)
        give[...] = out[:n].astype(BF)

    grad = nn(x_t[...], cot) * order
    grad = grad.reshape(4, 8, 4, 2, 8, 2 * LANES)
    for side in (0, 1):

        @pl.when(core == side)
        def _():
            for x in range(4):
                for ref, c in ((mine, side), (yours, 1 - side)):
                    ref[:, x] = grad[:, :, x, c].reshape(4, 64, 2 * LANES).astype(BF)


def unpack_body(at, keep, far, out):
    z = at[0]
    n = keep.shape[0]
    row, col = iota((2 * n, n), 0), iota((2 * n, n), 1)
    ours, theirs = one(row == 2 * col + z), one(row == 2 * col + 1 - z)
    out[...] = (nn(ours, keep[...]) + nn(theirs, far[...])).astype(BF)


def softened(k_pair, v_pair, q_pair, g_pair, seen):
    rows = q_pair.shape[0]
    score = nt(halves(k_pair, SCALE), q_pair)
    inner = nt(halves(v_pair), g_pair)
    result = []
    for k in (0, 1):
        s = jnp.where(seen, score[k * rows : (k + 1) * rows], LOW)
        result.append((s, inner[k * rows : (k + 1) * rows]))
    return result


def row_sums(s, d):
    top = jnp.max(s, axis=0, keepdims=True)
    e = jnp.exp(s - top)
    norm = jnp.sum(e, axis=0, keepdims=True)
    return e, top, norm, jnp.sum(e * d, axis=0, keepdims=True) / norm


def merged(log_a, delta_a, log_b, delta_b):
    top = jnp.maximum(log_a, log_b)
    a, b = jnp.exp(log_a - top), jnp.exp(log_b - top)
    norm = a + b
    return top + jnp.log(norm), (a * delta_a + b * delta_b) / norm


def seen_mask(rows, cross):
    key, query = iota((rows, rows), 0), iota((rows, rows), 1)
    order = key >= query if cross else key <= query
    return jnp.logical_and(order, (key & 1) == (query & 1))


def stats_body(q, k, v, g, stats):
    rows, width = q.shape
    seen = seen_mask(rows, False)
    logs, deltas = [], []
    for p in range(width // LANES):
        at = slice(p * LANES, (p + 1) * LANES)
        for s, d in softened(k[:, at], v[:, at], q[:, at], g[:, at], seen):
            e, top, norm, delta = row_sums(s, d)
            logs.append(top + jnp.log(norm))
            deltas.append(delta)
    stats[0] = jnp.concatenate(logs + deltas, axis=0)


def products(ps, ds, q_pair, k_pair, g_pair):
    p_side = jnp.concatenate(ps, axis=1)
    d_side = jnp.concatenate(ds, axis=1)
    grad_v = nn(p_side, halves(g_pair))
    grad_k = nn(d_side, halves(q_pair, SCALE))
    grad_q = tn(jnp.concatenate(ds, axis=0), halves(k_pair, SCALE))
    return grad_q, grad_k, grad_v


def cross_body(qg, k, v, gq, gk, gv):
    rows, width = k.shape
    heads = width // HEAD
    theirs = from_pieces(qg, 2 * rows)
    seen = seen_mask(rows, True)
    logs, deltas = [], []
    for p in range(width // LANES):
        at = slice(p * LANES, (p + 1) * LANES)
        q_pair, k_pair, g_pair = qg[:rows, at], k[:, at], qg[rows : 2 * rows, at]
        ps, ds = [], []
        for j, (s, d) in enumerate(softened(k_pair, v[:, at], q_pair, g_pair, seen)):
            h = 2 * p + j
            e, top, norm, delta = row_sums(s, d)
            log_here = top + jnp.log(norm)
            logs.append(log_here)
            deltas.append(delta)
            log_norm, delta = merged(
                log_here, delta, theirs[h : h + 1, :], theirs[heads + h : heads + h + 1, :]
            )
            prob = e * jnp.exp(top - log_norm)
            ps.append(prob.astype(BF))
            ds.append((prob * (d - delta)).astype(BF))
        a, b, c = products(ps, ds, q_pair, k_pair, g_pair)
        gq[:rows, at] = a.astype(BF)
        gk[:, at] = b.astype(BF)
        gv[:, at] = c.astype(BF)
    add_pieces(jnp.concatenate(logs + deltas, axis=0), gq, rows)


def own_body(at_ref, q, k, v, g, ours, gq_far, gk_far, gv_far, gq, gk, gv):
    rows, width = q.shape
    heads = width // HEAD
    seen = seen_mask(rows, False)
    begins = at_ref[2] == 0
    near = ours[0]
    away = from_pieces(gq_far, rows)
    for p in range(width // LANES):
        at = slice(p * LANES, (p + 1) * LANES)
        q_pair, k_pair, g_pair = q[:, at], k[:, at], g[:, at]
        ps, ds = [], []
        for j, (s, d) in enumerate(softened(k_pair, v[:, at], q_pair, g_pair, seen)):
            h = 2 * p + j
            far = jnp.where(begins, LOW, away[h : h + 1])
            log_norm, delta = merged(
                near[h : h + 1],
                near[heads + h : heads + h + 1],
                far,
                away[heads + h : heads + h + 1],
            )
            prob = jnp.exp(s - log_norm)
            ps.append(prob.astype(BF))
            ds.append((prob * (d - delta)).astype(BF))
        a, b, c = products(ps, ds, q_pair, k_pair, g_pair)
        gq[:, at] = (a + gq_far[:rows, at].astype(F32)).astype(BF)
        gk[:, at] = (b + gk_far[:, at].astype(F32)).astype(BF)
        gv[:, at] = (c + gv_far[:, at].astype(F32)).astype(BF)


def local(
    frames_x, bc_weight, decay_codes, decay_rates, skip_gain, queries, keys, values, cotangent
):
    length, blocks, width = frames_x.shape
    rows = length * blocks
    heads = decay_rates.shape[0]
    tm = lax.axis_size(TM)
    ny, nx, nz = lax.axis_size("y"), lax.axis_size("x"), lax.axis_size(("zh", "zl"))
    y, z, core = lax.axis_index("y"), lax.axis_index("zh"), lax.axis_index("c")
    at = jnp.stack([z, y, 2 * y + z, core]).astype(jnp.int32)
    flip = [(0, 1), (1, 0)]
    to_prev = [(i, i - 1) for i in range(1, tm)]
    to_next = [(i - 1, i) for i in range(1, tm)]

    def flat(a):
        return a.reshape(rows, width)

    x2, g2, q2, k2, v2 = (flat(a) for a in (frames_x, cotangent, queries, keys, values))
    codes = jnp.transpose(decay_codes, (1, 2, 0))
    rate_wide = jnp.repeat(decay_rates, HEAD)[None]
    gain_wide = jnp.repeat(skip_gain, HEAD)[None]

    msg = (rows // 2, 2 * width + LANES)
    own, out = call(pack_body, [(msg, BF)] * 2, [at], [x2, g2, codes])
    got = lax.ppermute(out, "zh", flip)

    steps = width // GROUP
    stats = ((steps, 2 * GROUP // HEAD, rows), F32)
    stats_own = call(stats_body, [stats], [], [q2, k2, v2, g2], steps=steps)[0]
    qg = call(join_body, [((2 * rows + 16, width), BF)], [], [q2, g2, stats_own], steps=steps)[0]
    qg_next = lax.ppermute(qg, TM, to_prev)

    wide = (rows, width)
    state = (LANES + 16, width)
    square = (rows, LANES)
    xs, gs, bc, sums, sums_t, scaled_x, scaled_g, leave, m1, m2, m3 = call(
        summary_body,
        [(wide, BF), (wide, BF), ((rows, 2 * LANES), BF), (square, F32), (square, F32)]
        + [(wide, BF)] * 3
        + [(state, BF)] * 3,
        [at],
        [own, got, bc_weight, rate_wide],
        [qg],
    )
    m1, m2, m3 = (
        lax.ppermute(m, "y", [(i, (i + s) % ny) for i in range(ny)])
        for s, m in ((1, m1), (2, m2), (3, m3))
    )
    gx, gb, gc, x_t = call(
        inner_body,
        [(wide, BF), (square, F32), (square, F32), ((width, rows), BF)],
        [decay_rates],
        [xs, gs, bc, sums, sums_t],
    )
    gq_out, gk_far, gv_far = call(
        cross_body,
        [((rows + 16, width), BF), (wide, BF), (wide, BF)],
        [],
        [qg_next, k2, v2],
        steps=steps,
    )
    order = 1.0 / (rows * tm * lax.axis_size(("zl", "x", "c")))
    keep, give, mine, yours = call(
        lambda at_ref, *refs: carry_body(at_ref, order, *refs),
        [((rows // 2, width), BF)] * 2 + [((ny, nx, nz * 8, 2 * LANES), BF)] * 2,
        [at],
        [m1, m2, m3, rate_wide, gain_wide, bc_weight, gs, bc, scaled_x, scaled_g, leave, gx, gb, gc, x_t],
        [gq_out],
    )
    gx_far = lax.ppermute(give, "zh", flip)

    chip = (mine.astype(F32) + lax.ppermute(yours, "c", flip).astype(F32)).astype(BF)
    chip = chip.reshape(ny * nx, nz * 8, 2 * LANES)
    spread = lax.all_to_all(chip, ("y", "x"), 0, 0, tiled=True)
    plane = jnp.sum(spread.astype(F32), axis=0).astype(BF).reshape(nz, 8, 2 * LANES)
    spread = lax.all_to_all(plane, ("zh", "zl"), 0, 0, tiled=True)
    grad_bc = jnp.sum(spread.astype(F32), axis=0)

    gq_far = lax.ppermute(gq_out, TM, to_next)
    gq, gk, gv = call(
        own_body,
        [(wide, BF)] * 3,
        [at],
        [q2, k2, v2, g2, stats_own, gq_far, gk_far, gv_far],
        [chip],
        steps=steps,
    )
    shape = (length, blocks, width)
    grad_x = call(unpack_body, [(wide, BF)], [at], [keep, gx_far], [gk])[0]
    return grad_x.reshape(shape), gq.reshape(shape), gk.reshape(shape), gv.reshape(shape), grad_bc


def solution(mesh):
    tm, blk = mesh.devices.shape
    fine = Mesh(
        mesh.devices.reshape(tm // 2, 2, blk // 8, 4, 2), TM + ("zl", "x", "c")
    )
    tokens = P(TM, ("zl", "x", "c"), None)
    return jax.shard_map(
        local,
        mesh=fine,
        in_specs=(tokens, P(), tokens, P(), P(), tokens, tokens, tokens, tokens),
        out_specs=(tokens,) * 4 + (P(TM + ("zl", "x", "c"), None),),
        check_vma=False,
    )
```

```python
import jax
import jax.numpy as jnp
from jax import lax
from jax.experimental import pallas as pl
from jax.experimental.pallas import tpu as pltpu
from jax.sharding import Mesh, PartitionSpec as P

HEAD = 64
LANES = 128
INJECT = 0.015625
CODE_UNIT = 4096.0
SCALE = 0.125
VMEM_BYTES = 60 * 1024 * 1024
LOW = -1e30
BF = jnp.bfloat16
F32 = jnp.float32
TM = ("y", "zh")
SM = pl.BlockSpec(memory_space=pltpu.SMEM)


GROUP = 512


def call(body, outs, scalars, arrays, first=(), steps=1):
    used = len(scalars) + len(arrays)

    def run(*refs):
        body(*refs[:used], *refs[used + len(first) :])

    def spec(shape):
        if steps == 1:
            return pl.BlockSpec(shape, lambda i: (0,) * len(shape))
        if len(shape) == 3:
            return pl.BlockSpec((1,) + tuple(shape[1:]), lambda i: (i, 0, 0))
        return pl.BlockSpec((shape[0], shape[1] // steps), lambda i: (0, i))

    return pl.pallas_call(
        run,
        out_shape=[jax.ShapeDtypeStruct(s, d) for s, d in outs],
        in_specs=[SM] * len(scalars)
        + [spec(a.shape) for a in arrays]
        + [pl.BlockSpec(memory_space=pl.ANY)] * len(first),
        out_specs=[spec(s) for s, d in outs],
        grid=(steps,),
        cost_estimate=pl.CostEstimate(flops=1, bytes_accessed=1, transcendentals=0),
        compiler_params=pltpu.CompilerParams(vmem_limit_bytes=VMEM_BYTES),
    )(*scalars, *arrays, *first)


def held_until(value, event):
    anywhere = pl.BlockSpec(memory_space=pl.ANY)
    return pl.pallas_call(
        lambda *refs: None,
        out_shape=jax.ShapeDtypeStruct(value.shape, value.dtype),
        in_specs=[anywhere, anywhere],
        out_specs=anywhere,
        input_output_aliases={0: 0},
    )(value, event)


def nn(a, b):
    return lax.dot_general(a, b, (((1,), (0,)), ((), ())), preferred_element_type=F32)


def nt(a, b):
    return lax.dot_general(a, b, (((1,), (1,)), ((), ())), preferred_element_type=F32)


def tn(a, b):
    return lax.dot_general(a, b, (((0,), (0,)), ((), ())), preferred_element_type=F32)


def iota(shape, dim):
    return lax.broadcasted_iota(jnp.int32, shape, dim)


def one(cond):
    return jnp.where(cond, 1.0, 0.0).astype(BF)


def halves(value, scale=1.0):
    low = jnp.where(iota((1, LANES), 1) < HEAD, scale, 0.0).astype(BF)
    high = jnp.where(iota((1, LANES), 1) < HEAD, 0.0, scale).astype(BF)
    return jnp.concatenate([value * low, value * high], axis=0)


def side(value):
    n = value.shape[0] // 2
    return jnp.concatenate([value[:n], value[n:]], axis=1)


def add_pieces(value, ref, rows):
    for piece in range(3):
        part = value.astype(BF)
        value = value - part.astype(F32)
        ref[rows:, piece * LANES : (piece + 1) * LANES] = part
    ref[rows:, 3 * LANES :] = jnp.zeros((16, GROUP - 3 * LANES), BF)


def from_pieces(ref, rows):
    a, b, c = (ref[rows:, i * LANES : (i + 1) * LANES].astype(F32) for i in range(3))
    return a + (b + c)


def join_body(q, g, stats, out):
    rows = q.shape[0]
    out[:rows, :] = q[...]
    out[rows : 2 * rows, :] = g[...]
    add_pieces(stats[0], out, 2 * rows)


def pack_body(at, x, g, codes, own, out):
    z = at[0]
    rows, width = x.shape
    n = rows // 2
    row, col = iota((n, rows), 0), iota((n, rows), 1)
    keep, give = one(col == 2 * row + z), one(col == 2 * row + 1 - z)
    here = z == 0
    for pick, code, ref in (
        (keep, jnp.where(here, codes[0], codes[1]), own),
        (give, jnp.where(here, codes[1], codes[0]), out),
    ):
        ref[:, :width] = nn(pick, x[...]).astype(BF)
        ref[:, width : 2 * width] = nn(pick, g[...]).astype(BF)
        both = jnp.concatenate([code >> 8, code & 255], axis=0).astype(F32)
        ref[:, 2 * width :] = jnp.concatenate([both, jnp.zeros_like(both)], axis=1).astype(BF)


def summary_body(
    at, own, got, w, rate, xs, gs, bc, sums, sums_t, scaled_x, scaled_g, leave, m1, m2, m3
):
    z, y = at[0], at[1]
    n = own.shape[0]
    rows = 2 * n
    width = xs.shape[1]
    mine = pl.multiple_of(z * n, n)
    other = pl.multiple_of((1 - z) * n, n)
    for src, start in ((own, mine), (got, other)):
        xs[pl.ds(start, n), :] = src[:, :width]
        gs[pl.ds(start, n), :] = src[:, width : 2 * width]
    mine_codes, other_codes = own[:, 2 * width :].astype(F32), got[:, 2 * width :].astype(F32)
    early = jnp.where(z == 0, mine_codes, other_codes)
    late = jnp.where(z == 0, other_codes, mine_codes)
    codes = jnp.concatenate([early[:, :n], late[:, :n]], axis=1)
    heads = codes.shape[0] // 2
    blank = jnp.zeros((LANES - heads, rows), F32)
    hi = jnp.concatenate([codes[:heads], blank], axis=0).astype(BF)
    lo = jnp.concatenate([codes[heads:], blank], axis=0).astype(BF)
    row, col = iota((rows, rows), 0), iota((rows, rows), 1)
    lower, upper = one(col <= row), one(row <= col)
    total = nt(lower, hi) * 256.0 + nt(lower, lo)
    sums[...] = total
    sums_t[...] = nn(hi, upper) * 256.0 + nn(lo, upper)
    whole = total.astype(jnp.int32)
    spread = one(iota((LANES, width), 1) // HEAD == iota((LANES, width), 0))
    wide = jnp.zeros((rows, width), F32)
    lasts = []
    for shift in (16, 8, 0):
        piece = ((whole >> shift) & 255).astype(F32).astype(BF)
        part = nn(piece, spread)
        lasts.append(part[rows - 1 :, :])
        wide = wide * 256.0 + part
    last = wide[rows - 1 :, :]
    slope = rate[...] * (-1.0 / CODE_UNIT)
    to_end = jnp.exp((last - wide) * slope)
    growth = jnp.exp(wide * slope)
    bc_rows = nn(xs[...], w[...]).astype(BF)
    bc[...] = bc_rows
    gone = xs[...].astype(F32) * to_end
    sx = gone.astype(BF)
    sg = (gs[...].astype(F32) * growth).astype(BF)
    scaled_x[...] = sx
    scaled_g[...] = sg
    leave[...] = to_end.astype(BF)
    state = (tn(bc_rows[:, :LANES], sx) * INJECT).astype(BF)
    back = tn(bc_rows[:, LANES:], sg).astype(BF)
    tail = jnp.concatenate(lasts + [jnp.zeros((13, width), F32)], axis=0).astype(BF)
    for shift, ref in ((1, m1), (2, m2), (3, m3)):
        later = y + shift < 4

        @pl.when(later)
        def _():
            ref[:LANES, :] = state

        @pl.when(jnp.logical_not(later))
        def _():
            ref[:LANES, :] = back

        ref[LANES:, :] = tail


def inner_body(rate, xs, gs, bc, sums, sums_t, gx, gb, gc, x_t):
    rows, width = xs.shape
    row, col = iota((rows, rows), 0), iota((rows, rows), 1)
    ahead = row <= col
    b_rows, c_rows = bc[:, :LANES], bc[:, LANES:]
    kernel = nt(b_rows, c_rows) * INJECT
    mixing = jnp.zeros((rows, rows), F32)
    for p in range(width // LANES):
        at = slice(p * LANES, (p + 1) * LANES)
        x_pair, g_pair = xs[:, at], gs[:, at]
        both = nt(halves(x_pair), g_pair)
        parts = []
        for k in (0, 1):
            h = 2 * p + k
            gap = sums_t[h : h + 1, :] - sums[:, h : h + 1]
            decay = jnp.exp(jnp.where(ahead, gap * (rate[h] * (-1.0 / CODE_UNIT)), LOW))
            mixing = mixing + decay * both[k * rows : (k + 1) * rows]
            parts.append((decay * kernel).astype(BF))
        gx[:, at] = nn(jnp.concatenate(parts, axis=1), halves(g_pair)).astype(BF)
        x_t[at, :] = x_pair.astype(F32).T.astype(BF)
    mixed = (mixing * INJECT).astype(BF)
    gb[...] = nn(mixed, c_rows)
    gc[...] = tn(mixed, b_rows)


def carry_body(
    at, order, m1, m2, m3, rate, gain, w, gs, bc, scaled_x, scaled_g, leave, gx, gb, gc, x_t,
    keep, give, mine, yours,
):
    z, y, core = at[0], at[1], at[3]
    n = keep.shape[0]
    slope = rate[...] * (-1.0 / CODE_UNIT)

    def fade(ref):
        v = ref[LANES : LANES + 16, :].astype(F32)
        return ((v[0:1] * 256.0 + v[1:2]) * 256.0 + v[2:3]) * slope

    l1, l2, l3 = fade(m1), fade(m2), fade(m3)
    s1, s2, s3 = (m[:LANES, :].astype(F32) for m in (m1, m2, m3))

    def use(cond, log):
        return jnp.where(cond, jnp.exp(log), 0.0)

    zero = jnp.zeros_like(l1)
    state = use(y >= 1, zero) * s1 + use(y >= 2, l1) * s2 + use(y >= 3, l1 + l2) * s3
    back = use(y < 3, zero) * s3 + use(y < 2, l3) * s2 + use(y < 1, l3 + l2) * s1
    state, back = state.astype(BF), back.astype(BF)
    b_cot = gb[...] + nt(scaled_x[...], back) * INJECT
    c_cot = gc[...] + nt(scaled_g[...], state)
    cot = jnp.concatenate([b_cot, c_cot], axis=1).astype(BF)
    out = gx[...].astype(F32) + leave[...].astype(F32) * (nn(bc[:, :LANES], back) * INJECT)
    out = out + gs[...].astype(F32) * gain[...] + nt(cot, w[...])

    @pl.when(z == 0)
    def _():
        keep[...] = out[:n].astype(BF)
        give[...] = out[n:].astype(BF)

    @pl.when(z == 1)
    def _():
        keep[...] = out[n:].astype(BF)
        give[...] = out[:n].astype(BF)

    grad = nn(x_t[...], cot) * order
    grad = grad.reshape(4, 8, 4, 2, 8, 2 * LANES)
    for side in (0, 1):

        @pl.when(core == side)
        def _():
            for x in range(4):
                for ref, c in ((mine, side), (yours, 1 - side)):
                    ref[:, x] = grad[:, :, x, c].reshape(4, 64, 2 * LANES).astype(BF)


def unpack_body(at, keep, far, out):
    z = at[0]
    n = keep.shape[0]
    row, col = iota((2 * n, n), 0), iota((2 * n, n), 1)
    ours, theirs = one(row == 2 * col + z), one(row == 2 * col + 1 - z)
    out[...] = (nn(ours, keep[...]) + nn(theirs, far[...])).astype(BF)


def softened(k_pair, v_pair, q_pair, g_pair, seen):
    rows = q_pair.shape[0]
    score = nt(halves(k_pair, SCALE), q_pair)
    inner = nt(halves(v_pair), g_pair)
    result = []
    for k in (0, 1):
        s = jnp.where(seen, score[k * rows : (k + 1) * rows], LOW)
        result.append((s, inner[k * rows : (k + 1) * rows]))
    return result


def row_sums(s, d):
    top = jnp.max(s, axis=0, keepdims=True)
    e = jnp.exp(s - top)
    norm = jnp.sum(e, axis=0, keepdims=True)
    return e, top, norm, jnp.sum(e * d, axis=0, keepdims=True) / norm


def merged(log_a, delta_a, log_b, delta_b):
    top = jnp.maximum(log_a, log_b)
    a, b = jnp.exp(log_a - top), jnp.exp(log_b - top)
    norm = a + b
    return top + jnp.log(norm), (a * delta_a + b * delta_b) / norm


def seen_mask(rows, cross):
    key, query = iota((rows, rows), 0), iota((rows, rows), 1)
    order = key >= query if cross else key <= query
    return jnp.logical_and(order, (key & 1) == (query & 1))


def stats_body(q, k, v, g, stats):
    rows, width = q.shape
    seen = seen_mask(rows, False)
    logs, deltas = [], []
    for p in range(width // LANES):
        at = slice(p * LANES, (p + 1) * LANES)
        for s, d in softened(k[:, at], v[:, at], q[:, at], g[:, at], seen):
            e, top, norm, delta = row_sums(s, d)
            logs.append(top + jnp.log(norm))
            deltas.append(delta)
    stats[0] = jnp.concatenate(logs + deltas, axis=0)


def products(ps, ds, q_pair, k_pair, g_pair):
    p_side = jnp.concatenate(ps, axis=1)
    d_side = jnp.concatenate(ds, axis=1)
    grad_v = nn(p_side, halves(g_pair))
    grad_k = nn(d_side, halves(q_pair, SCALE))
    grad_q = tn(jnp.concatenate(ds, axis=0), halves(k_pair, SCALE))
    return grad_q, grad_k, grad_v


def cross_body(qg, k, v, stats, gq, gk, gv):
    rows, width = k.shape
    heads = width // HEAD
    theirs = from_pieces(qg, 2 * rows)
    seen = seen_mask(rows, True)
    logs, deltas = [], []
    for p in range(width // LANES):
        at = slice(p * LANES, (p + 1) * LANES)
        q_pair, k_pair, g_pair = qg[:rows, at], k[:, at], qg[rows : 2 * rows, at]
        ps, ds = [], []
        for j, (s, d) in enumerate(softened(k_pair, v[:, at], q_pair, g_pair, seen)):
            h = 2 * p + j
            e, top, norm, delta = row_sums(s, d)
            log_here = top + jnp.log(norm)
            logs.append(log_here)
            deltas.append(delta)
            log_norm, delta = merged(
                log_here, delta, theirs[h : h + 1, :], theirs[heads + h : heads + h + 1, :]
            )
            prob = e * jnp.exp(top - log_norm)
            ps.append(prob.astype(BF))
            ds.append((prob * (d - delta)).astype(BF))
        a, b, c = products(ps, ds, q_pair, k_pair, g_pair)
        gq[:, at] = a.astype(BF)
        gk[:, at] = b.astype(BF)
        gv[:, at] = c.astype(BF)
    stats[0] = jnp.concatenate(logs + deltas, axis=0)


def own_body(at_ref, q, k, v, g, ours, theirs, gk_far, gv_far, gq, gk, gv):
    rows, width = q.shape
    heads = width // HEAD
    seen = seen_mask(rows, False)
    begins = at_ref[2] == 0
    near = ours[0]
    away = theirs[0]
    for p in range(width // LANES):
        at = slice(p * LANES, (p + 1) * LANES)
        q_pair, k_pair, g_pair = q[:, at], k[:, at], g[:, at]
        ps, ds = [], []
        for j, (s, d) in enumerate(softened(k_pair, v[:, at], q_pair, g_pair, seen)):
            h = 2 * p + j
            far = jnp.where(begins, LOW, away[h : h + 1])
            log_norm, delta = merged(
                near[h : h + 1],
                near[heads + h : heads + h + 1],
                far,
                away[heads + h : heads + h + 1],
            )
            prob = jnp.exp(s - log_norm)
            ps.append(prob.astype(BF))
            ds.append((prob * (d - delta)).astype(BF))
        a, b, c = products(ps, ds, q_pair, k_pair, g_pair)
        gq[:, at] = a
        gk[:, at] = (b + gk_far[:, at].astype(F32)).astype(BF)
        gv[:, at] = (c + gv_far[:, at].astype(F32)).astype(BF)


def local(
    frames_x, bc_weight, decay_codes, decay_rates, skip_gain, queries, keys, values, cotangent
):
    length, blocks, width = frames_x.shape
    rows = length * blocks
    heads = decay_rates.shape[0]
    tm = lax.axis_size(TM)
    ny, nx, nz = lax.axis_size("y"), lax.axis_size("x"), lax.axis_size(("zh", "zl"))
    y, z, core = lax.axis_index("y"), lax.axis_index("zh"), lax.axis_index("c")
    at = jnp.stack([z, y, 2 * y + z, core]).astype(jnp.int32)
    flip = [(0, 1), (1, 0)]
    to_prev = [(i, i - 1) for i in range(1, tm)]
    to_next = [(i - 1, i) for i in range(1, tm)]

    def flat(a):
        return a.reshape(rows, width)

    x2, g2, q2, k2, v2 = (flat(a) for a in (frames_x, cotangent, queries, keys, values))
    codes = jnp.transpose(decay_codes, (1, 2, 0))
    rate_wide = jnp.repeat(decay_rates, HEAD)[None]
    gain_wide = jnp.repeat(skip_gain, HEAD)[None]

    msg = (rows // 2, 2 * width + LANES)
    own, out = call(pack_body, [(msg, BF)] * 2, [at], [x2, g2, codes])
    got = lax.ppermute(out, "zh", flip)

    steps = width // GROUP
    stats = ((steps, 2 * GROUP // HEAD, rows), F32)
    stats_own = call(stats_body, [stats], [], [q2, k2, v2, g2], steps=steps)[0]
    qg = call(join_body, [((2 * rows + 16, width), BF)], [], [q2, g2, stats_own], steps=steps)[0]
    qg_next = lax.ppermute(qg, TM, to_prev)

    wide = (rows, width)
    state = (LANES + 16, width)
    square = (rows, LANES)
    xs, gs, bc, sums, sums_t, scaled_x, scaled_g, leave, m1, m2, m3 = call(
        summary_body,
        [(wide, BF), (wide, BF), ((rows, 2 * LANES), BF), (square, F32), (square, F32)]
        + [(wide, BF)] * 3
        + [(state, BF)] * 3,
        [at],
        [own, got, bc_weight, rate_wide],
        [qg],
    )
    m1, m2, m3 = (
        lax.ppermute(m, "y", [(i, (i + s) % ny) for i in range(ny)])
        for s, m in ((1, m1), (2, m2), (3, m3))
    )
    gx, gb, gc, x_t = call(
        inner_body,
        [(wide, BF), (square, F32), (square, F32), ((width, rows), BF)],
        [decay_rates],
        [xs, gs, bc, sums, sums_t],
    )
    stats_out, gq_out, gk_far, gv_far = call(
        cross_body,
        [stats, (wide, BF), (wide, BF), (wide, BF)],
        [],
        [qg_next, k2, v2],
        steps=steps,
    )
    order = 1.0 / (rows * tm * lax.axis_size(("zl", "x", "c")))
    keep, give, mine, yours = call(
        lambda at_ref, *refs: carry_body(at_ref, order, *refs),
        [((rows // 2, width), BF)] * 2 + [((ny, nx, nz * 8, 2 * LANES), BF)] * 2,
        [at],
        [m1, m2, m3, rate_wide, gain_wide, bc_weight, gs, bc, scaled_x, scaled_g, leave, gx, gb, gc, x_t],
        [gq_out],
    )
    gx_far = lax.ppermute(give, "zh", flip)

    chip = (mine.astype(F32) + lax.ppermute(yours, "c", flip).astype(F32)).astype(BF)
    chip = chip.reshape(ny * nx, nz * 8, 2 * LANES)
    spread = lax.all_to_all(chip, ("y", "x"), 0, 0, tiled=True)
    plane = jnp.sum(spread.astype(F32), axis=0).astype(BF).reshape(nz, 8, 2 * LANES)
    spread = lax.all_to_all(plane, ("zh", "zl"), 0, 0, tiled=True)
    grad_bc = jnp.sum(spread.astype(F32), axis=0)

    stats_far = lax.ppermute(stats_out, TM, to_next)
    gq_far = lax.ppermute(held_until(gq_out, stats_far), TM, to_next)
    gq, gk, gv = call(
        own_body,
        [(wide, F32), (wide, BF), (wide, BF)],
        [at],
        [q2, k2, v2, g2, stats_own, stats_far, gk_far, gv_far],
        [chip],
        steps=steps,
    )
    gq = (gq + gq_far.astype(F32)).astype(BF)
    shape = (length, blocks, width)
    grad_x = call(unpack_body, [(wide, BF)], [at], [keep, gx_far], [plane])[0]
    return grad_x.reshape(shape), gq.reshape(shape), gk.reshape(shape), gv.reshape(shape), grad_bc


def solution(mesh):
    tm, blk = mesh.devices.shape
    fine = Mesh(
        mesh.devices.reshape(tm // 2, 2, blk // 8, 4, 2), TM + ("zl", "x", "c")
    )
    tokens = P(TM, ("zl", "x", "c"), None)
    return jax.shard_map(
        local,
        mesh=fine,
        in_specs=(tokens, P(), tokens, P(), P(), tokens, tokens, tokens, tokens),
        out_specs=(tokens,) * 4 + (P(TM + ("zl", "x", "c"), None),),
        check_vma=False,
    )
```

```python
import jax
import jax.numpy as jnp
from jax import lax
from jax.experimental import pallas as pl
from jax.experimental.pallas import tpu as pltpu
from jax.sharding import Mesh, PartitionSpec as P

HEAD = 64
LANES = 128
INJECT = 0.015625
CODE_UNIT = 4096.0
SCALE = 0.125
VMEM_BYTES = 60 * 1024 * 1024
LOW = -1e30
BF = jnp.bfloat16
F32 = jnp.float32
TM = ("y", "zh")
SM = pl.BlockSpec(memory_space=pltpu.SMEM)


GROUP = 512


def call(body, outs, scalars, arrays, first=(), steps=1):
    used = len(scalars) + len(arrays)

    def run(*refs):
        body(*refs[:used], *refs[used + len(first) :])

    def spec(shape):
        if steps == 1:
            return pl.BlockSpec(shape, lambda i: (0,) * len(shape))
        if len(shape) == 3:
            return pl.BlockSpec((1,) + tuple(shape[1:]), lambda i: (i, 0, 0))
        return pl.BlockSpec((shape[0], shape[1] // steps), lambda i: (0, i))

    return pl.pallas_call(
        run,
        out_shape=[jax.ShapeDtypeStruct(s, d) for s, d in outs],
        in_specs=[SM] * len(scalars)
        + [spec(a.shape) for a in arrays]
        + [pl.BlockSpec(memory_space=pl.ANY)] * len(first),
        out_specs=[spec(s) for s, d in outs],
        grid=(steps,),
        cost_estimate=pl.CostEstimate(flops=1, bytes_accessed=1, transcendentals=0),
        compiler_params=pltpu.CompilerParams(vmem_limit_bytes=VMEM_BYTES),
    )(*scalars, *arrays, *first)


def nn(a, b):
    return lax.dot_general(a, b, (((1,), (0,)), ((), ())), preferred_element_type=F32)


def nt(a, b):
    return lax.dot_general(a, b, (((1,), (1,)), ((), ())), preferred_element_type=F32)


def tn(a, b):
    return lax.dot_general(a, b, (((0,), (0,)), ((), ())), preferred_element_type=F32)


def iota(shape, dim):
    return lax.broadcasted_iota(jnp.int32, shape, dim)


def one(cond):
    return jnp.where(cond, 1.0, 0.0).astype(BF)


def halves(value, scale=1.0):
    low = jnp.where(iota((1, LANES), 1) < HEAD, scale, 0.0).astype(BF)
    high = jnp.where(iota((1, LANES), 1) < HEAD, 0.0, scale).astype(BF)
    return jnp.concatenate([value * low, value * high], axis=0)


def side(value):
    n = value.shape[0] // 2
    return jnp.concatenate([value[:n], value[n:]], axis=1)


def add_pieces(value, ref, rows):
    for piece in range(3):
        part = value.astype(BF)
        value = value - part.astype(F32)
        ref[rows:, piece * LANES : (piece + 1) * LANES] = part
    ref[rows:, 3 * LANES :] = jnp.zeros((16, GROUP - 3 * LANES), BF)


def from_pieces(ref, rows):
    a, b, c = (ref[rows:, i * LANES : (i + 1) * LANES].astype(F32) for i in range(3))
    return a + (b + c)


def join_body(q, g, stats, out):
    rows = q.shape[0]
    out[:rows, :] = q[...]
    out[rows : 2 * rows, :] = g[...]
    add_pieces(stats[0], out, 2 * rows)


def pack_body(at, x, g, codes, own, out):
    z = at[0]
    rows, width = x.shape
    n = rows // 2
    row, col = iota((n, rows), 0), iota((n, rows), 1)
    keep, give = one(col == 2 * row + z), one(col == 2 * row + 1 - z)
    here = z == 0
    for pick, code, ref in (
        (keep, jnp.where(here, codes[0], codes[1]), own),
        (give, jnp.where(here, codes[1], codes[0]), out),
    ):
        ref[:, :width] = nn(pick, x[...]).astype(BF)
        ref[:, width : 2 * width] = nn(pick, g[...]).astype(BF)
        both = jnp.concatenate([code >> 8, code & 255], axis=0).astype(F32)
        ref[:, 2 * width :] = jnp.concatenate([both, jnp.zeros_like(both)], axis=1).astype(BF)


def summary_body(
    at, own, got, w, rate, xs, gs, bc, sums, sums_t, scaled_x, scaled_g, leave, m1, m2, m3
):
    z, y = at[0], at[1]
    n = own.shape[0]
    rows = 2 * n
    width = xs.shape[1]
    mine = pl.multiple_of(z * n, n)
    other = pl.multiple_of((1 - z) * n, n)
    for src, start in ((own, mine), (got, other)):
        xs[pl.ds(start, n), :] = src[:, :width]
        gs[pl.ds(start, n), :] = src[:, width : 2 * width]
    mine_codes, other_codes = own[:, 2 * width :].astype(F32), got[:, 2 * width :].astype(F32)
    early = jnp.where(z == 0, mine_codes, other_codes)
    late = jnp.where(z == 0, other_codes, mine_codes)
    codes = jnp.concatenate([early[:, :n], late[:, :n]], axis=1)
    heads = codes.shape[0] // 2
    blank = jnp.zeros((LANES - heads, rows), F32)
    hi = jnp.concatenate([codes[:heads], blank], axis=0).astype(BF)
    lo = jnp.concatenate([codes[heads:], blank], axis=0).astype(BF)
    row, col = iota((rows, rows), 0), iota((rows, rows), 1)
    lower, upper = one(col <= row), one(row <= col)
    total = nt(lower, hi) * 256.0 + nt(lower, lo)
    sums[...] = total
    sums_t[...] = nn(hi, upper) * 256.0 + nn(lo, upper)
    whole = total.astype(jnp.int32)
    spread = one(iota((LANES, width), 1) // HEAD == iota((LANES, width), 0))
    wide = jnp.zeros((rows, width), F32)
    lasts = []
    for shift in (16, 8, 0):
        piece = ((whole >> shift) & 255).astype(F32).astype(BF)
        part = nn(piece, spread)
        lasts.append(part[rows - 1 :, :])
        wide = wide * 256.0 + part
    last = wide[rows - 1 :, :]
    slope = rate[...] * (-1.0 / CODE_UNIT)
    to_end = jnp.exp((last - wide) * slope)
    growth = jnp.exp(wide * slope)
    bc_rows = nn(xs[...], w[...]).astype(BF)
    bc[...] = bc_rows
    gone = xs[...].astype(F32) * to_end
    sx = gone.astype(BF)
    sg = (gs[...].astype(F32) * growth).astype(BF)
    scaled_x[...] = sx
    scaled_g[...] = sg
    leave[...] = to_end.astype(BF)
    state = (tn(bc_rows[:, :LANES], sx) * INJECT).astype(BF)
    back = tn(bc_rows[:, LANES:], sg).astype(BF)
    tail = jnp.concatenate(lasts + [jnp.zeros((13, width), F32)], axis=0).astype(BF)
    for shift, ref in ((1, m1), (2, m2), (3, m3)):
        later = y + shift < 4

        @pl.when(later)
        def _():
            ref[:LANES, :] = state

        @pl.when(jnp.logical_not(later))
        def _():
            ref[:LANES, :] = back

        ref[LANES:, :] = tail


def inner_body(rate, xs, gs, bc, sums, sums_t, gx, gb, gc, x_t):
    rows, width = xs.shape
    row, col = iota((rows, rows), 0), iota((rows, rows), 1)
    ahead = row <= col
    b_rows, c_rows = bc[:, :LANES], bc[:, LANES:]
    kernel = nt(b_rows, c_rows) * INJECT
    mixing = jnp.zeros((rows, rows), F32)
    for p in range(width // LANES):
        at = slice(p * LANES, (p + 1) * LANES)
        x_pair, g_pair = xs[:, at], gs[:, at]
        both = nt(halves(x_pair), g_pair)
        parts = []
        for k in (0, 1):
            h = 2 * p + k
            gap = sums_t[h : h + 1, :] - sums[:, h : h + 1]
            decay = jnp.exp(jnp.where(ahead, gap * (rate[h] * (-1.0 / CODE_UNIT)), LOW))
            mixing = mixing + decay * both[k * rows : (k + 1) * rows]
            parts.append((decay * kernel).astype(BF))
        gx[:, at] = nn(jnp.concatenate(parts, axis=1), halves(g_pair)).astype(BF)
        x_t[at, :] = x_pair.astype(F32).T.astype(BF)
    mixed = (mixing * INJECT).astype(BF)
    gb[...] = nn(mixed, c_rows)
    gc[...] = tn(mixed, b_rows)


def carry_body(
    at, order, m1, m2, m3, rate, gain, w, gs, bc, scaled_x, scaled_g, leave, gx, gb, gc, x_t,
    keep, give, mine, yours,
):
    z, y, core = at[0], at[1], at[3]
    n = keep.shape[0]
    slope = rate[...] * (-1.0 / CODE_UNIT)

    def fade(ref):
        v = ref[LANES : LANES + 16, :].astype(F32)
        return ((v[0:1] * 256.0 + v[1:2]) * 256.0 + v[2:3]) * slope

    l1, l2, l3 = fade(m1), fade(m2), fade(m3)
    s1, s2, s3 = (m[:LANES, :].astype(F32) for m in (m1, m2, m3))

    def use(cond, log):
        return jnp.where(cond, jnp.exp(log), 0.0)

    zero = jnp.zeros_like(l1)
    state = use(y >= 1, zero) * s1 + use(y >= 2, l1) * s2 + use(y >= 3, l1 + l2) * s3
    back = use(y < 3, zero) * s3 + use(y < 2, l3) * s2 + use(y < 1, l3 + l2) * s1
    state, back = state.astype(BF), back.astype(BF)
    b_cot = gb[...] + nt(scaled_x[...], back) * INJECT
    c_cot = gc[...] + nt(scaled_g[...], state)
    cot = jnp.concatenate([b_cot, c_cot], axis=1).astype(BF)
    out = gx[...].astype(F32) + leave[...].astype(F32) * (nn(bc[:, :LANES], back) * INJECT)
    out = out + gs[...].astype(F32) * gain[...] + nt(cot, w[...])

    @pl.when(z == 0)
    def _():
        keep[...] = out[:n].astype(BF)
        give[...] = out[n:].astype(BF)

    @pl.when(z == 1)
    def _():
        keep[...] = out[n:].astype(BF)
        give[...] = out[:n].astype(BF)

    grad = nn(x_t[...], cot) * order
    grad = grad.reshape(4, 8, 4, 2, 8, 2 * LANES)
    for side in (0, 1):

        @pl.when(core == side)
        def _():
            for x in range(4):
                for ref, c in ((mine, side), (yours, 1 - side)):
                    ref[:, x] = grad[:, :, x, c].reshape(4, 64, 2 * LANES).astype(BF)


def unpack_body(at, keep, far, out):
    z = at[0]
    n = keep.shape[0]
    row, col = iota((2 * n, n), 0), iota((2 * n, n), 1)
    ours, theirs = one(row == 2 * col + z), one(row == 2 * col + 1 - z)
    out[...] = (nn(ours, keep[...]) + nn(theirs, far[...])).astype(BF)


def softened(k_pair, v_pair, q_pair, g_pair, seen):
    rows = q_pair.shape[0]
    score = nt(halves(k_pair, SCALE), q_pair)
    inner = nt(halves(v_pair), g_pair)
    result = []
    for k in (0, 1):
        s = jnp.where(seen, score[k * rows : (k + 1) * rows], LOW)
        result.append((s, inner[k * rows : (k + 1) * rows]))
    return result


def row_sums(s, d):
    top = jnp.max(s, axis=0, keepdims=True)
    e = jnp.exp(s - top)
    norm = jnp.sum(e, axis=0, keepdims=True)
    return e, top, norm, jnp.sum(e * d, axis=0, keepdims=True) / norm


def merged(log_a, delta_a, log_b, delta_b):
    top = jnp.maximum(log_a, log_b)
    a, b = jnp.exp(log_a - top), jnp.exp(log_b - top)
    norm = a + b
    return top + jnp.log(norm), (a * delta_a + b * delta_b) / norm


def seen_mask(rows, cross):
    key, query = iota((rows, rows), 0), iota((rows, rows), 1)
    order = key >= query if cross else key <= query
    return jnp.logical_and(order, (key & 1) == (query & 1))


def stats_body(q, k, v, g, stats):
    rows, width = q.shape
    seen = seen_mask(rows, False)
    logs, deltas = [], []
    for p in range(width // LANES):
        at = slice(p * LANES, (p + 1) * LANES)
        for s, d in softened(k[:, at], v[:, at], q[:, at], g[:, at], seen):
            e, top, norm, delta = row_sums(s, d)
            logs.append(top + jnp.log(norm))
            deltas.append(delta)
    stats[0] = jnp.concatenate(logs + deltas, axis=0)


def products(ps, ds, q_pair, k_pair, g_pair):
    p_side = jnp.concatenate(ps, axis=1)
    d_side = jnp.concatenate(ds, axis=1)
    grad_v = nn(p_side, halves(g_pair))
    grad_k = nn(d_side, halves(q_pair, SCALE))
    grad_q = tn(jnp.concatenate(ds, axis=0), halves(k_pair, SCALE))
    return grad_q, grad_k, grad_v


def cross_body(qg, k, v, stats, gq, gk, gv):
    rows, width = k.shape
    heads = width // HEAD
    theirs = from_pieces(qg, 2 * rows)
    seen = seen_mask(rows, True)
    logs, deltas = [], []
    for p in range(width // LANES):
        at = slice(p * LANES, (p + 1) * LANES)
        q_pair, k_pair, g_pair = qg[:rows, at], k[:, at], qg[rows : 2 * rows, at]
        ps, ds = [], []
        for j, (s, d) in enumerate(softened(k_pair, v[:, at], q_pair, g_pair, seen)):
            h = 2 * p + j
            e, top, norm, delta = row_sums(s, d)
            log_here = top + jnp.log(norm)
            logs.append(log_here)
            deltas.append(delta)
            log_norm, delta = merged(
                log_here, delta, theirs[h : h + 1, :], theirs[heads + h : heads + h + 1, :]
            )
            prob = e * jnp.exp(top - log_norm)
            ps.append(prob.astype(BF))
            ds.append((prob * (d - delta)).astype(BF))
        a, b, c = products(ps, ds, q_pair, k_pair, g_pair)
        gq[:, at] = a.astype(BF)
        gk[:, at] = b.astype(BF)
        gv[:, at] = c.astype(BF)
    stats[0] = jnp.concatenate(logs + deltas, axis=0)


def own_body(at_ref, q, k, v, g, ours, theirs, gk_far, gv_far, gq, gk, gv):
    rows, width = q.shape
    heads = width // HEAD
    seen = seen_mask(rows, False)
    begins = at_ref[2] == 0
    near = ours[0]
    away = theirs[0]
    for p in range(width // LANES):
        at = slice(p * LANES, (p + 1) * LANES)
        q_pair, k_pair, g_pair = q[:, at], k[:, at], g[:, at]
        ps, ds = [], []
        for j, (s, d) in enumerate(softened(k_pair, v[:, at], q_pair, g_pair, seen)):
            h = 2 * p + j
            far = jnp.where(begins, LOW, away[h : h + 1])
            log_norm, delta = merged(
                near[h : h + 1],
                near[heads + h : heads + h + 1],
                far,
                away[heads + h : heads + h + 1],
            )
            prob = jnp.exp(s - log_norm)
            ps.append(prob.astype(BF))
            ds.append((prob * (d - delta)).astype(BF))
        a, b, c = products(ps, ds, q_pair, k_pair, g_pair)
        gq[:, at] = a
        gk[:, at] = (b + gk_far[:, at].astype(F32)).astype(BF)
        gv[:, at] = (c + gv_far[:, at].astype(F32)).astype(BF)


def local(
    frames_x, bc_weight, decay_codes, decay_rates, skip_gain, queries, keys, values, cotangent
):
    length, blocks, width = frames_x.shape
    rows = length * blocks
    heads = decay_rates.shape[0]
    tm = lax.axis_size(TM)
    ny, nx, nz = lax.axis_size("y"), lax.axis_size("x"), lax.axis_size(("zh", "zl"))
    y, z, core = lax.axis_index("y"), lax.axis_index("zh"), lax.axis_index("c")
    at = jnp.stack([z, y, 2 * y + z, core]).astype(jnp.int32)
    flip = [(0, 1), (1, 0)]
    to_prev = [(i, i - 1) for i in range(1, tm)]
    to_next = [(i - 1, i) for i in range(1, tm)]

    def flat(a):
        return a.reshape(rows, width)

    x2, g2, q2, k2, v2 = (flat(a) for a in (frames_x, cotangent, queries, keys, values))
    codes = jnp.transpose(decay_codes, (1, 2, 0))
    rate_wide = jnp.repeat(decay_rates, HEAD)[None]
    gain_wide = jnp.repeat(skip_gain, HEAD)[None]

    msg = (rows // 2, 2 * width + LANES)
    own, out = call(pack_body, [(msg, BF)] * 2, [at], [x2, g2, codes])
    got = lax.ppermute(out, "zh", flip)

    steps = width // GROUP
    stats = ((steps, 2 * GROUP // HEAD, rows), F32)
    stats_own = call(stats_body, [stats], [], [q2, k2, v2, g2], steps=steps)[0]
    qg = call(join_body, [((2 * rows + 16, width), BF)], [], [q2, g2, stats_own], steps=steps)[0]
    qg_next = lax.ppermute(qg, TM, to_prev)

    wide = (rows, width)
    state = (LANES + 16, width)
    square = (rows, LANES)
    xs, gs, bc, sums, sums_t, scaled_x, scaled_g, leave, m1, m2, m3 = call(
        summary_body,
        [(wide, BF), (wide, BF), ((rows, 2 * LANES), BF), (square, F32), (square, F32)]
        + [(wide, BF)] * 3
        + [(state, BF)] * 3,
        [at],
        [own, got, bc_weight, rate_wide],
        [qg],
    )
    m1, m2, m3 = (
        lax.ppermute(m, "y", [(i, (i + s) % ny) for i in range(ny)])
        for s, m in ((1, m1), (2, m2), (3, m3))
    )
    gx, gb, gc, x_t = call(
        inner_body,
        [(wide, BF), (square, F32), (square, F32), ((width, rows), BF)],
        [decay_rates],
        [xs, gs, bc, sums, sums_t],
    )
    stats_out, gq_out, gk_far, gv_far = call(
        cross_body,
        [stats, (wide, BF), (wide, BF), (wide, BF)],
        [],
        [qg_next, k2, v2],
        steps=steps,
    )
    stats_far = lax.ppermute(stats_out, TM, to_next)
    order = 1.0 / (rows * tm * lax.axis_size(("zl", "x", "c")))
    keep, give, mine, yours = call(
        lambda at_ref, *refs: carry_body(at_ref, order, *refs),
        [((rows // 2, width), BF)] * 2 + [((ny, nx, nz * 8, 2 * LANES), BF)] * 2,
        [at],
        [m1, m2, m3, rate_wide, gain_wide, bc_weight, gs, bc, scaled_x, scaled_g, leave, gx, gb, gc, x_t],
        [stats_far],
    )
    gx_far = lax.ppermute(give, "zh", flip)

    chip = (mine.astype(F32) + lax.ppermute(yours, "c", flip).astype(F32)).astype(BF)
    chip = chip.reshape(ny * nx, nz * 8, 2 * LANES)
    spread = lax.all_to_all(chip, ("y", "x"), 0, 0, tiled=True)
    plane = jnp.sum(spread.astype(F32), axis=0).astype(BF).reshape(nz, 8, 2 * LANES)
    spread = lax.all_to_all(plane, ("zh", "zl"), 0, 0, tiled=True)
    grad_bc = jnp.sum(spread.astype(F32), axis=0)

    gq_far = lax.ppermute(gq_out, TM, to_next)
    gq, gk, gv = call(
        own_body,
        [(wide, F32), (wide, BF), (wide, BF)],
        [at],
        [q2, k2, v2, g2, stats_own, stats_far, gk_far, gv_far],
        [chip],
        steps=steps,
    )
    gq = (gq + gq_far.astype(F32)).astype(BF)
    shape = (length, blocks, width)
    grad_x = call(unpack_body, [(wide, BF)], [at], [keep, gx_far], [plane])[0]
    return grad_x.reshape(shape), gq.reshape(shape), gk.reshape(shape), gv.reshape(shape), grad_bc


def solution(mesh):
    tm, blk = mesh.devices.shape
    fine = Mesh(
        mesh.devices.reshape(tm // 2, 2, blk // 8, 4, 2), TM + ("zl", "x", "c")
    )
    tokens = P(TM, ("zl", "x", "c"), None)
    return jax.shard_map(
        local,
        mesh=fine,
        in_specs=(tokens, P(), tokens, P(), P(), tokens, tokens, tokens, tokens),
        out_specs=(tokens,) * 4 + (P(TM + ("zl", "x", "c"), None),),
        check_vma=False,
    )
```

```python
import jax
import jax.numpy as jnp
from jax import lax
from jax.experimental import pallas as pl
from jax.experimental.pallas import tpu as pltpu
from jax.sharding import Mesh, PartitionSpec as P

HEAD = 64
LANES = 128
INJECT = 0.015625
CODE_UNIT = 4096.0
SCALE = 0.125
VMEM_BYTES = 60 * 1024 * 1024
LOW = -1e30
BF = jnp.bfloat16
F32 = jnp.float32
TM = ("y", "zh")
SM = pl.BlockSpec(memory_space=pltpu.SMEM)


GROUP = 512


def call(body, outs, scalars, arrays, first=(), steps=1):
    used = len(scalars) + len(arrays)

    def run(*refs):
        body(*refs[:used], *refs[used + len(first) :])

    def spec(shape):
        if steps > 1 and len(shape) == 3 and shape[2] > GROUP:
            return pl.BlockSpec(tuple(shape[:2]) + (GROUP,), lambda i: (0, 0, i))
        if steps == 1:
            return pl.BlockSpec(shape, lambda i: (0,) * len(shape))
        if len(shape) == 3:
            return pl.BlockSpec((1,) + tuple(shape[1:]), lambda i: (i, 0, 0))
        return pl.BlockSpec((shape[0], shape[1] // steps), lambda i: (0, i))

    return pl.pallas_call(
        run,
        out_shape=[jax.ShapeDtypeStruct(s, d) for s, d in outs],
        in_specs=[SM] * len(scalars)
        + [spec(a.shape) for a in arrays]
        + [pl.BlockSpec(memory_space=pl.ANY)] * len(first),
        out_specs=[spec(s) for s, d in outs],
        grid=(steps,),
        cost_estimate=pl.CostEstimate(flops=1, bytes_accessed=1, transcendentals=0),
        compiler_params=pltpu.CompilerParams(vmem_limit_bytes=VMEM_BYTES),
    )(*scalars, *arrays, *first)


def nn(a, b):
    return lax.dot_general(a, b, (((1,), (0,)), ((), ())), preferred_element_type=F32)


def nt(a, b):
    return lax.dot_general(a, b, (((1,), (1,)), ((), ())), preferred_element_type=F32)


def tn(a, b):
    return lax.dot_general(a, b, (((0,), (0,)), ((), ())), preferred_element_type=F32)


def iota(shape, dim):
    return lax.broadcasted_iota(jnp.int32, shape, dim)


def one(cond):
    return jnp.where(cond, 1.0, 0.0).astype(BF)


def halves(value, scale=1.0):
    low = jnp.where(iota((1, LANES), 1) < HEAD, scale, 0.0).astype(BF)
    high = jnp.where(iota((1, LANES), 1) < HEAD, 0.0, scale).astype(BF)
    return jnp.concatenate([value * low, value * high], axis=0)


def side(value):
    n = value.shape[0] // 2
    return jnp.concatenate([value[:n], value[n:]], axis=1)


def add_pieces(value, ref, rows):
    for piece in range(3):
        part = value.astype(BF)
        value = value - part.astype(F32)
        ref[rows:, piece * LANES : (piece + 1) * LANES] = part
    ref[rows:, 3 * LANES :] = jnp.zeros((16, GROUP - 3 * LANES), BF)


def from_pieces(ref, rows):
    a, b, c = (ref[rows:, i * LANES : (i + 1) * LANES].astype(F32) for i in range(3))
    return a + (b + c)


def join_body(q, g, stats, out):
    rows = q.shape[0]
    out[:rows, :] = q[...]
    out[rows : 2 * rows, :] = g[...]
    add_pieces(stats[0], out, 2 * rows)


def pack_body(at, x, g, codes, own, out):
    z = at[0]
    rows, width = x.shape
    n = rows // 2
    row, col = iota((n, rows), 0), iota((n, rows), 1)
    keep, give = one(col == 2 * row + z), one(col == 2 * row + 1 - z)
    here = z == 0
    for pick, code, ref in (
        (keep, jnp.where(here, codes[0], codes[1]), own),
        (give, jnp.where(here, codes[1], codes[0]), out),
    ):
        ref[:, :width] = nn(pick, x[...]).astype(BF)
        ref[:, width : 2 * width] = nn(pick, g[...]).astype(BF)
        both = jnp.concatenate([code >> 8, code & 255], axis=0).astype(F32)
        ref[:, 2 * width :] = jnp.concatenate([both, jnp.zeros_like(both)], axis=1).astype(BF)


def summary_body(
    at, own, got, w, rate, xs, gs, bc, sums, sums_t, scaled_x, scaled_g, leave, m1, m2, m3
):
    z, y = at[0], at[1]
    n = own.shape[0]
    rows = 2 * n
    width = xs.shape[1]
    mine = pl.multiple_of(z * n, n)
    other = pl.multiple_of((1 - z) * n, n)
    for src, start in ((own, mine), (got, other)):
        xs[pl.ds(start, n), :] = src[:, :width]
        gs[pl.ds(start, n), :] = src[:, width : 2 * width]
    mine_codes, other_codes = own[:, 2 * width :].astype(F32), got[:, 2 * width :].astype(F32)
    early = jnp.where(z == 0, mine_codes, other_codes)
    late = jnp.where(z == 0, other_codes, mine_codes)
    codes = jnp.concatenate([early[:, :n], late[:, :n]], axis=1)
    heads = codes.shape[0] // 2
    blank = jnp.zeros((LANES - heads, rows), F32)
    hi = jnp.concatenate([codes[:heads], blank], axis=0).astype(BF)
    lo = jnp.concatenate([codes[heads:], blank], axis=0).astype(BF)
    row, col = iota((rows, rows), 0), iota((rows, rows), 1)
    lower, upper = one(col <= row), one(row <= col)
    total = nt(lower, hi) * 256.0 + nt(lower, lo)
    sums[...] = total
    sums_t[...] = nn(hi, upper) * 256.0 + nn(lo, upper)
    whole = total.astype(jnp.int32)
    spread = one(iota((LANES, width), 1) // HEAD == iota((LANES, width), 0))
    wide = jnp.zeros((rows, width), F32)
    lasts = []
    for shift in (16, 8, 0):
        piece = ((whole >> shift) & 255).astype(F32).astype(BF)
        part = nn(piece, spread)
        lasts.append(part[rows - 1 :, :])
        wide = wide * 256.0 + part
    last = wide[rows - 1 :, :]
    slope = rate[...] * (-1.0 / CODE_UNIT)
    to_end = jnp.exp((last - wide) * slope)
    growth = jnp.exp(wide * slope)
    bc_rows = nn(xs[...], w[...]).astype(BF)
    bc[...] = bc_rows
    gone = xs[...].astype(F32) * to_end
    sx = gone.astype(BF)
    sg = (gs[...].astype(F32) * growth).astype(BF)
    scaled_x[...] = sx
    scaled_g[...] = sg
    leave[...] = to_end.astype(BF)
    state = (tn(bc_rows[:, :LANES], sx) * INJECT).astype(BF)
    back = tn(bc_rows[:, LANES:], sg).astype(BF)
    tail = jnp.concatenate(lasts + [jnp.zeros((13, width), F32)], axis=0).astype(BF)
    for shift, ref in ((1, m1), (2, m2), (3, m3)):
        later = y + shift < 4

        @pl.when(later)
        def _():
            ref[:LANES, :] = state

        @pl.when(jnp.logical_not(later))
        def _():
            ref[:LANES, :] = back

        ref[LANES:, :] = tail


def inner_body(rate, xs, gs, bc, sums, sums_t, gx, gb, gc, x_t):
    rows, width = xs.shape
    row, col = iota((rows, rows), 0), iota((rows, rows), 1)
    ahead = row <= col
    b_rows, c_rows = bc[:, :LANES], bc[:, LANES:]
    kernel = nt(b_rows, c_rows) * INJECT
    mixing = jnp.zeros((rows, rows), F32)
    for p in range(width // LANES):
        at = slice(p * LANES, (p + 1) * LANES)
        x_pair, g_pair = xs[:, at], gs[:, at]
        both = nt(halves(x_pair), g_pair)
        parts = []
        for k in (0, 1):
            h = 2 * p + k
            gap = sums_t[h : h + 1, :] - sums[:, h : h + 1]
            decay = jnp.exp(jnp.where(ahead, gap * (rate[h] * (-1.0 / CODE_UNIT)), LOW))
            mixing = mixing + decay * both[k * rows : (k + 1) * rows]
            parts.append((decay * kernel).astype(BF))
        gx[:, at] = nn(jnp.concatenate(parts, axis=1), halves(g_pair)).astype(BF)
        x_t[at, :] = x_pair.astype(F32).T.astype(BF)
    mixed = (mixing * INJECT).astype(BF)
    gb[...] = nn(mixed, c_rows)
    gc[...] = tn(mixed, b_rows)


def carry_body(
    at, order, m1, m2, m3, rate, gain, w, gs, bc, scaled_x, scaled_g, leave, gx, gb, gc, x_t,
    keep, give, mine, yours,
):
    z, y, core = at[0], at[1], at[3]
    n = keep.shape[0]
    slope = rate[...] * (-1.0 / CODE_UNIT)

    def fade(ref):
        v = ref[LANES : LANES + 16, :].astype(F32)
        return ((v[0:1] * 256.0 + v[1:2]) * 256.0 + v[2:3]) * slope

    l1, l2, l3 = fade(m1), fade(m2), fade(m3)
    s1, s2, s3 = (m[:LANES, :].astype(F32) for m in (m1, m2, m3))

    def use(cond, log):
        return jnp.where(cond, jnp.exp(log), 0.0)

    zero = jnp.zeros_like(l1)
    state = use(y >= 1, zero) * s1 + use(y >= 2, l1) * s2 + use(y >= 3, l1 + l2) * s3
    back = use(y < 3, zero) * s3 + use(y < 2, l3) * s2 + use(y < 1, l3 + l2) * s1
    state, back = state.astype(BF), back.astype(BF)
    b_cot = gb[...] + nt(scaled_x[...], back) * INJECT
    c_cot = gc[...] + nt(scaled_g[...], state)
    cot = jnp.concatenate([b_cot, c_cot], axis=1).astype(BF)
    out = gx[...].astype(F32) + leave[...].astype(F32) * (nn(bc[:, :LANES], back) * INJECT)
    out = out + gs[...].astype(F32) * gain[...] + nt(cot, w[...])

    @pl.when(z == 0)
    def _():
        keep[...] = out[:n].astype(BF)
        give[...] = out[n:].astype(BF)

    @pl.when(z == 1)
    def _():
        keep[...] = out[n:].astype(BF)
        give[...] = out[:n].astype(BF)

    grad = nn(x_t[...], cot) * order
    grad = grad.reshape(4, 8, 4, 2, 8, 2 * LANES)
    for side in (0, 1):

        @pl.when(core == side)
        def _():
            for x in range(4):
                for ref, c in ((mine, side), (yours, 1 - side)):
                    ref[:, x] = grad[:, :, x, c].reshape(4, 64, 2 * LANES).astype(BF)


def unpack_body(at, keep, far, out):
    z = at[0]
    n = keep.shape[0]
    row, col = iota((2 * n, n), 0), iota((2 * n, n), 1)
    ours, theirs = one(row == 2 * col + z), one(row == 2 * col + 1 - z)
    out[...] = (nn(ours, keep[...]) + nn(theirs, far[...])).astype(BF)


def softened(k_pair, v_pair, q_pair, g_pair, seen):
    rows = q_pair.shape[0]
    score = nt(halves(k_pair, SCALE), q_pair)
    inner = nt(halves(v_pair), g_pair)
    result = []
    for k in (0, 1):
        s = jnp.where(seen, score[k * rows : (k + 1) * rows], LOW)
        result.append((s, inner[k * rows : (k + 1) * rows]))
    return result


def row_sums(s, d):
    top = jnp.max(s, axis=0, keepdims=True)
    e = jnp.exp(s - top)
    norm = jnp.sum(e, axis=0, keepdims=True)
    return e, top, norm, jnp.sum(e * d, axis=0, keepdims=True) / norm


def merged(log_a, delta_a, log_b, delta_b):
    top = jnp.maximum(log_a, log_b)
    a, b = jnp.exp(log_a - top), jnp.exp(log_b - top)
    norm = a + b
    return top + jnp.log(norm), (a * delta_a + b * delta_b) / norm


def seen_mask(rows, cross):
    key, query = iota((rows, rows), 0), iota((rows, rows), 1)
    order = key >= query if cross else key <= query
    return jnp.logical_and(order, (key & 1) == (query & 1))


def stats_body(q, k, v, g, stats):
    rows, width = q.shape
    seen = seen_mask(rows, False)
    logs, deltas = [], []
    for p in range(width // LANES):
        at = slice(p * LANES, (p + 1) * LANES)
        for s, d in softened(k[:, at], v[:, at], q[:, at], g[:, at], seen):
            e, top, norm, delta = row_sums(s, d)
            logs.append(top + jnp.log(norm))
            deltas.append(delta)
    stats[0] = jnp.concatenate(logs + deltas, axis=0)


def products(ps, ds, q_pair, k_pair, g_pair):
    p_side = jnp.concatenate(ps, axis=1)
    d_side = jnp.concatenate(ds, axis=1)
    grad_v = nn(p_side, halves(g_pair))
    grad_k = nn(d_side, halves(q_pair, SCALE))
    grad_q = tn(jnp.concatenate(ds, axis=0), halves(k_pair, SCALE))
    return grad_q, grad_k, grad_v


def cross_body(qg, k, v, gq, gk, gv):
    rows, width = k.shape
    heads = width // HEAD
    theirs = from_pieces(qg, 2 * rows)
    seen = seen_mask(rows, True)
    logs, deltas = [], []
    for p in range(width // LANES):
        at = slice(p * LANES, (p + 1) * LANES)
        q_pair, k_pair, g_pair = qg[:rows, at], k[:, at], qg[rows : 2 * rows, at]
        ps, ds = [], []
        for j, (s, d) in enumerate(softened(k_pair, v[:, at], q_pair, g_pair, seen)):
            h = 2 * p + j
            e, top, norm, delta = row_sums(s, d)
            log_here = top + jnp.log(norm)
            logs.append(log_here)
            deltas.append(delta)
            log_norm, delta = merged(
                log_here, delta, theirs[h : h + 1, :], theirs[heads + h : heads + h + 1, :]
            )
            prob = e * jnp.exp(top - log_norm)
            ps.append(prob.astype(BF))
            ds.append((prob * (d - delta)).astype(BF))
        a, b, c = products(ps, ds, q_pair, k_pair, g_pair)
        gq[:rows, at] = a.astype(BF)
        gk[:, at] = b.astype(BF)
        gv[:, at] = c.astype(BF)
    add_pieces(jnp.concatenate(logs + deltas, axis=0), gq, rows)


def apart(value):
    return value.reshape(value.shape[0] // 2, 2, value.shape[1]).astype(BF)


def own_body(at_ref, q, k, v, g, ours, gq_far, gk_far, gv_far, gq, gk, gv):
    rows, width = q.shape
    heads = width // HEAD
    seen = seen_mask(rows, False)
    begins = at_ref[2] == 0
    near = ours[0]
    away = from_pieces(gq_far, rows)
    for p in range(width // LANES):
        at = slice(p * LANES, (p + 1) * LANES)
        q_pair, k_pair, g_pair = q[:, at], k[:, at], g[:, at]
        ps, ds = [], []
        for j, (s, d) in enumerate(softened(k_pair, v[:, at], q_pair, g_pair, seen)):
            h = 2 * p + j
            far = jnp.where(begins, LOW, away[h : h + 1])
            log_norm, delta = merged(
                near[h : h + 1],
                near[heads + h : heads + h + 1],
                far,
                away[heads + h : heads + h + 1],
            )
            prob = jnp.exp(s - log_norm)
            ps.append(prob.astype(BF))
            ds.append((prob * (d - delta)).astype(BF))
        a, b, c = products(ps, ds, q_pair, k_pair, g_pair)
        gq[:, :, at] = apart(a + gq_far[:rows, at].astype(F32))
        gk[:, :, at] = apart(b + gk_far[:, at].astype(F32))
        gv[:, :, at] = apart(c + gv_far[:, at].astype(F32))


def local(
    frames_x, bc_weight, decay_codes, decay_rates, skip_gain, queries, keys, values, cotangent
):
    length, blocks, width = frames_x.shape
    rows = length * blocks
    heads = decay_rates.shape[0]
    tm = lax.axis_size(TM)
    ny, nx, nz = lax.axis_size("y"), lax.axis_size("x"), lax.axis_size(("zh", "zl"))
    y, z, core = lax.axis_index("y"), lax.axis_index("zh"), lax.axis_index("c")
    at = jnp.stack([z, y, 2 * y + z, core]).astype(jnp.int32)
    flip = [(0, 1), (1, 0)]
    to_prev = [(i, i - 1) for i in range(1, tm)]
    to_next = [(i - 1, i) for i in range(1, tm)]

    def flat(a):
        return a.reshape(rows, width)

    x2, g2, q2, k2, v2 = (flat(a) for a in (frames_x, cotangent, queries, keys, values))
    codes = jnp.transpose(decay_codes, (1, 2, 0))
    rate_wide = jnp.repeat(decay_rates, HEAD)[None]
    gain_wide = jnp.repeat(skip_gain, HEAD)[None]

    msg = (rows // 2, 2 * width + LANES)
    own, out = call(pack_body, [(msg, BF)] * 2, [at], [x2, g2, codes])
    got = lax.ppermute(out, "zh", flip)

    steps = width // GROUP
    stats = ((steps, 2 * GROUP // HEAD, rows), F32)
    stats_own = call(stats_body, [stats], [], [q2, k2, v2, g2], steps=steps)[0]
    qg = call(join_body, [((2 * rows + 16, width), BF)], [], [q2, g2, stats_own], steps=steps)[0]
    qg_next = lax.ppermute(qg, TM, to_prev)

    wide = (rows, width)
    state = (LANES + 16, width)
    square = (rows, LANES)
    xs, gs, bc, sums, sums_t, scaled_x, scaled_g, leave, m1, m2, m3 = call(
        summary_body,
        [(wide, BF), (wide, BF), ((rows, 2 * LANES), BF), (square, F32), (square, F32)]
        + [(wide, BF)] * 3
        + [(state, BF)] * 3,
        [at],
        [own, got, bc_weight, rate_wide],
        [qg],
    )
    m1, m2, m3 = (
        lax.ppermute(m, "y", [(i, (i + s) % ny) for i in range(ny)])
        for s, m in ((1, m1), (2, m2), (3, m3))
    )
    gx, gb, gc, x_t = call(
        inner_body,
        [(wide, BF), (square, F32), (square, F32), ((width, rows), BF)],
        [decay_rates],
        [xs, gs, bc, sums, sums_t],
    )
    gq_out, gk_far, gv_far = call(
        cross_body,
        [((rows + 16, width), BF), (wide, BF), (wide, BF)],
        [],
        [qg_next, k2, v2],
        steps=steps,
    )
    order = 1.0 / (rows * tm * lax.axis_size(("zl", "x", "c")))
    keep, give, mine, yours = call(
        lambda at_ref, *refs: carry_body(at_ref, order, *refs),
        [((rows // 2, width), BF)] * 2 + [((ny, nx, nz * 8, 2 * LANES), BF)] * 2,
        [at],
        [m1, m2, m3, rate_wide, gain_wide, bc_weight, gs, bc, scaled_x, scaled_g, leave, gx, gb, gc, x_t],
        [gq_out],
    )
    gx_far = lax.ppermute(give, "zh", flip)

    chip = (mine.astype(F32) + lax.ppermute(yours, "c", flip).astype(F32)).astype(BF)
    chip = chip.reshape(ny * nx, nz * 8, 2 * LANES)
    spread = lax.all_to_all(chip, ("y", "x"), 0, 0, tiled=True)
    plane = jnp.sum(spread.astype(F32), axis=0).astype(BF).reshape(nz, 8, 2 * LANES)
    spread = lax.all_to_all(plane, ("zh", "zl"), 0, 0, tiled=True)
    grad_bc = jnp.sum(spread.astype(F32), axis=0)

    gq_far = lax.ppermute(gq_out, TM, to_next)
    gq, gk, gv = call(
        own_body,
        [((length, blocks, width), BF)] * 3,
        [at],
        [q2, k2, v2, g2, stats_own, gq_far, gk_far, gv_far],
        [chip],
        steps=steps,
    )
    shape = (length, blocks, width)
    grad_x = call(unpack_body, [(wide, BF)], [at], [keep, gx_far], [gk])[0]
    return grad_x.reshape(shape), gq.reshape(shape), gk.reshape(shape), gv.reshape(shape), grad_bc


def solution(mesh):
    tm, blk = mesh.devices.shape
    fine = Mesh(
        mesh.devices.reshape(tm // 2, 2, blk // 8, 4, 2), TM + ("zl", "x", "c")
    )
    tokens = P(TM, ("zl", "x", "c"), None)
    return jax.shard_map(
        local,
        mesh=fine,
        in_specs=(tokens, P(), tokens, P(), P(), tokens, tokens, tokens, tokens),
        out_specs=(tokens,) * 4 + (P(TM + ("zl", "x", "c"), None),),
        check_vma=False,
    )
```
